256 devices in a mesh: grp: 4 (over x), tp: 8 (over z), mem: 8 (over y, core).
Axes of the slice: x: 4, y: 4, z: 8, core: 2. Of those that a mesh axis runs over, the one named last changes fastest.
Arguments:
- tokens: bfloat16 [64, 12288], P('grp', 'mem'), may hold values from -110 to 110, as said below
- norm_gain: float32 [12288], P('mem'), may hold values from 0.5 to 1.5
- w_query: bfloat16 [12288, 12288], P('mem', 'tp'), may hold values from -0.0546875 to 0.0546875
- w_keyval: bfloat16 [2, 12288, 1024], P(None, 'mem', 'tp'), may hold values from -0.0546875 to 0.0546875
- w_out: bfloat16 [12288, 12288], P('tp', 'mem'), may hold values from -0.25 to 0.25
- key_cache: bfloat16 [8, 1024, 128, 128], P('tp', ('grp', 'mem')), may hold values from -1000 to 1000, as said below
- value_cache: bfloat16 [8, 1024, 128, 128], P('tp', ('grp', 'mem')), may hold values from -6 to 6
- req_len: int32 [64], replicated, may hold values from 1 to 2047, as said below
- span_request: int32 [1024], P(('grp', 'mem')), may hold values from -1 to 63, as said below
- span_first: int32 [1024], P(('grp', 'mem')), may hold values from 0 to 1920, as said below
- new_slot: int32 [64], replicated, may hold values from 0 to 1023, as said below
Outputs:
- attn_out: bfloat16 [64, 12288], P('grp', 'mem')
The draws below stay inside these ranges and needn't reach their ends.
Inputs may be any that keep to these rules, and one draw needn't show every extreme that they name: Every request holds ceil((req_len + 1) / 128) spans with firsts 0, 128, 256, ...; at most 16 spans a request; one request has exactly 16 spans. `span_request`: each request's spans sit in distinct slots; on every owner the used slots come first, then empty ones (-1); owners are filled unevenly. `span_first`: multiple of 128; 0 in empty slots. `new_slot`: the slot of the request's span that contains position req_len. `tokens`: real values. `key_cache`: real values.
All inputs are finite; a program needn't handle non-finite values.
Results may differ from the reference program's by a relative error of at most 0.015.
Values may be sent and summed in bfloat16 or wider, within the bound.
A program may use at most 64 MiB of HBM per device.

```python
import jax
import jax.numpy as jnp
from jax import lax

D = 12288
HQ = 96
KVH = 8
HD = 128
SPAN = 128
MOST_CH = 16
CH_DEV = 32
REQUESTS = 64
SPANS = 1024


def layout_tables(key):
    keys = jax.random.split(key, 6)
    request_ids = jnp.arange(REQUESTS, dtype=jnp.int32)
    counts = jax.random.randint(keys[0], (REQUESTS,), MOST_CH // 2, MOST_CH + 1)
    longest = jax.random.randint(keys[1], (), 0, REQUESTS)
    shortest = (longest + jax.random.randint(keys[2], (), 1, REQUESTS)) % REQUESTS
    counts = jnp.where(request_ids == longest, MOST_CH, jnp.where(request_ids == shortest, 1, counts))
    remainder = jax.random.randint(keys[3], (REQUESTS,), 1, SPAN)
    remainder = jnp.where(request_ids == longest, SPAN - 1, jnp.where(request_ids == shortest, 1, remainder))
    lengths = (counts - 1) * SPAN + remainder
    fill_order = jax.random.permutation(keys[4], REQUESTS).astype(jnp.int32)
    ordered = counts[fill_order]
    fill_end = jnp.cumsum(ordered).astype(jnp.int32)
    fill_begin = fill_end - ordered
    summed = fill_end[-1]
    slot_ids = jnp.arange(SPANS, dtype=jnp.int32)
    position_in = jnp.sum((fill_end[None, :] <= slot_ids[:, None]).astype(jnp.int32), axis=1)
    clipped = jnp.minimum(position_in, REQUESTS - 1)
    living = slot_ids < summed
    fill_req = jnp.where(living, fill_order[clipped], -1).astype(jnp.int32)
    fill_first = jnp.where(living, (slot_ids - fill_begin[clipped]) * SPAN, 0).astype(jnp.int32)
    scatter_perm = jax.random.permutation(keys[5], SPANS).astype(jnp.int32)
    placed_req = jnp.zeros((SPANS,), jnp.int32).at[scatter_perm].set(fill_req)
    placed_first = jnp.zeros((SPANS,), jnp.int32).at[scatter_perm].set(fill_first)
    sort_key = slot_ids // CH_DEV * (2 * SPANS) + (placed_req < 0).astype(jnp.int32) * SPANS + slot_ids
    order = jnp.argsort(sort_key, stable=True).astype(jnp.int32)
    span_request = placed_req[order]
    span_first = placed_first[order]
    position_of = jnp.zeros((SPANS,), jnp.int32).at[order].set(slot_ids)
    rank_of = jnp.zeros((REQUESTS,), jnp.int32).at[fill_order].set(request_ids)
    last_fill = fill_end[rank_of] - 1
    new_slot = position_of[scatter_perm[last_fill]]
    return (lengths.astype(jnp.int32), span_request, span_first, new_slot.astype(jnp.int32))


def draw_req_len(key, part):
    return layout_tables(key)[0]


def draw_span_request(key, part):
    return layout_tables(key)[1]


def draw_span_first(key, part):
    return layout_tables(key)[2]


def draw_new_slot(key, part):
    return layout_tables(key)[3]


def draw_tokens(key, part):
    key = jax.random.fold_in(key, 11)
    first_key, second_key = jax.random.split(key)
    ramp = jnp.arange(D, dtype=jnp.float32) / D
    normal_part = jnp.clip(jax.random.normal(first_key, (REQUESTS, D), jnp.float32), -6.0, 6.0)
    column_scale = 0.6 + 1.2 * ramp
    row_scale = jnp.exp(jax.random.uniform(second_key, (REQUESTS, 1), jnp.float32, 0.0, 2.3))
    return (normal_part * column_scale[None, :] * row_scale).astype(jnp.bfloat16)


def draw_key_cache(key, part):
    key = jax.random.fold_in(key, 23)
    first_key = jax.random.fold_in(key, 0)
    normal_part = jnp.clip(jax.random.normal(first_key, (KVH, SPANS, SPAN, HD), jnp.float32), -6.0, 6.0)
    return jnp.clip(normal_part, -1000.0, 1000.0).astype(jnp.bfloat16)


def shard_levels(stream_key, dims, cuts, smallest, top_value):
    gain = 1.0
    for dim, shards_of in cuts:
        draws = jax.random.uniform(jax.random.fold_in(jax.random.fold_in(stream_key, 6), dim), (shards_of,), jnp.float32, smallest / len(cuts), top_value / len(cuts))
        gain = gain * jnp.repeat(jnp.exp(draws), dims[dim] // shards_of).reshape((-1,) + (1,) * (len(dims) - 1 - dim))
    return gain


def normal_values(stream_key, shape, deviation, bound, cuts=(), held_as=jnp.bfloat16):
    values = deviation * jax.random.normal(stream_key, shape, jnp.float32)
    if cuts:
        values = values * shard_levels(stream_key, shape, cuts, -0.22, 0.18)
    return jnp.clip(values, -bound, bound).astype(held_as)


def setup_inputs(seed: int = 0) -> dict:
    key_of = jax.random.split(jax.random.key(seed), 12)
    return {
        "tokens": draw_tokens(jax.random.fold_in(key_of[11], 71), 0),
        "norm_gain": jnp.clip(1.0 + 0.1 * jax.random.normal(key_of[1], (D,), jnp.float32), 0.5, 1.5),
        "w_query": normal_values(key_of[2], (D, HQ * HD), D ** -0.5, 0.0546875, ((0, 8), (1, 8))),
        "w_keyval": normal_values(key_of[3], (2, D, KVH * HD), D ** -0.5, 0.0546875, ((1, 8), (2, 8))),
        "w_out": normal_values(key_of[4], (HQ * HD, D), (4 * HD) ** -0.5, 0.25, ((0, 8), (1, 8))),
        "key_cache": draw_key_cache(jax.random.fold_in(key_of[11], 71), 0),
        "value_cache": normal_values(key_of[6], (KVH, SPANS, SPAN, HD), 1.0, 6.0, ((0, 8), (1, 32))),
        "req_len": draw_req_len(jax.random.fold_in(key_of[11], 71), 0),
        "span_request": draw_span_request(jax.random.fold_in(key_of[11], 71), 0),
        "span_first": draw_span_first(jax.random.fold_in(key_of[11], 71), 0),
        "new_slot": draw_new_slot(jax.random.fold_in(key_of[11], 71), 0),
    }


epsilon = 1e-05
rope_base = 1000000.0
very_low = -1e+30

def rotary(vectors, positions):
    halfway = vectors.shape[-1] // 2
    frequency = rope_base ** (-(jnp.arange(halfway).astype(jnp.float32) * 2.0) / vectors.shape[-1])
    angles = positions.astype(jnp.float32)[:, None] * frequency[None, :]
    c = jnp.cos(angles)[:, None, :]
    s = jnp.sin(angles)[:, None, :]
    a = vectors[..., :halfway]
    b = vectors[..., halfway:]
    return jnp.concatenate([a * c - b * s, a * s + b * c], axis=-1)

def reference(tokens, norm_gain, w_query, w_keyval, w_out, key_cache, value_cache, req_len, span_request, span_first, new_slot):
    tokens_wide = tokens.astype(jnp.float32)
    root_mean = jnp.sqrt(lax.optimization_barrier(jnp.sum(tokens_wide * tokens_wide, axis=1)) / D + epsilon)
    scaled = (tokens_wide * norm_gain[None, :]).astype(jnp.bfloat16)
    query_part = jnp.dot(scaled, w_query, preferred_element_type=jnp.float32) / root_mean[:, None]
    key_part = jnp.dot(scaled, w_keyval[0], preferred_element_type=jnp.float32) / root_mean[:, None]
    value_part = jnp.dot(scaled, w_keyval[1], preferred_element_type=jnp.float32) / root_mean[:, None]
    queries = rotary(query_part.reshape(REQUESTS, HQ, HD), req_len).astype(jnp.bfloat16)
    new_keys = rotary(key_part.reshape(REQUESTS, KVH, HD), req_len).astype(jnp.bfloat16)
    new_values = value_part.reshape(REQUESTS, KVH, HD).astype(jnp.bfloat16)
    group_size = HQ // KVH
    living = span_request >= 0
    owner_req = jnp.maximum(span_request, 0).astype(jnp.int32)
    lengths = req_len[owner_req]
    positions = span_first[:, None] + jnp.arange(SPAN, dtype=jnp.int32)[None, :]
    visible = living[:, None] & (positions <= lengths[:, None])
    is_new = jnp.arange(SPANS, dtype=jnp.int32) == new_slot[owner_req]
    brand_new = visible & (positions == lengths[:, None]) & is_new[:, None]
    query_rows = queries[owner_req].reshape(SPANS, KVH, group_size, HD).transpose(1, 0, 2, 3)
    key_rows = new_keys[owner_req].transpose(1, 0, 2)
    value_rows = new_values[owner_req].transpose(1, 0, 2)

    def one_head(pieces):
        query_head, key_head, value_head, key_new, value_new = pieces
        key_head = jnp.where(brand_new[:, :, None], key_new[:, None, :], key_head)
        value_head = jnp.where(brand_new[:, :, None], value_new[:, None, :], value_head)
        scores = jnp.einsum('cgd,cjd->cgj', query_head.astype(jnp.float32), key_head.astype(jnp.float32)) * HD ** (-0.5)
        scores = jnp.where(visible[:, None, :], scores, very_low)
        span_max = lax.optimization_barrier(jnp.max(scores, axis=-1))
        weights = jnp.where(visible[:, None, :], jnp.exp(scores - span_max[..., None]), 0.0)
        span_total = lax.optimization_barrier(jnp.sum(weights, axis=-1))
        rounded = weights.astype(jnp.bfloat16).astype(jnp.float32)
        span_sum = jnp.einsum('cgj,cjd->cgd', rounded, value_head.astype(jnp.float32))
        return (span_max, span_total, span_sum)
    span_max, span_total, span_sum = lax.map(one_head, (query_rows, key_cache, value_cache, key_rows, value_rows))
    member = span_request[None, :] == jnp.arange(REQUESTS, dtype=jnp.int32)[:, None]
    member_wide = member[:, None, :, None]
    top = lax.optimization_barrier(jnp.max(jnp.where(member_wide, span_max[None], very_low), axis=2))
    factor = jnp.exp(jnp.where(member_wide, span_max[None] - top[:, :, None, :], very_low))
    total = lax.optimization_barrier(jnp.sum(factor * span_total[None], axis=2))
    accum = jnp.einsum('rkcg,kcgd->rkgd', factor, span_sum)
    attended = (accum / total[..., None]).astype(jnp.bfloat16).reshape(REQUESTS, HQ * HD)
    return jnp.dot(attended, w_out, preferred_element_type=jnp.float32).astype(jnp.bfloat16)
```

```python
import functools

import jax
import jax.numpy as jnp
from jax import lax
from jax.experimental import pallas as pl
from jax.experimental.pallas import tpu as pltpu
from jax.sharding import PartitionSpec as P

MESH = pl.DeviceIdType.MESH
HBM = pltpu.MemorySpace.HBM
D = 12288
epsilon = 1e-05
rope_base = 1000000.0
very_low = -1e30
SLOTS = 16
f32 = jnp.float32
bf16 = jnp.bfloat16


def chunks(count, width, body):
    def step(b, carry):
        stores = [body(b * width + u) for u in range(width)]
        for store in stores:
            store()
        return carry

    lax.fori_loop(0, count // width, step, 0)


def iota(shape, dim):
    return lax.broadcasted_iota(jnp.int32, shape, dim)


def kernel(
    n_grp, n_tp, n_mem,
    tokens, gain, w_query, w_keyval, w_out, key_cache, value_cache, req_len, span_request, span_first, new_slot,
    out,
    tok_v, gain_v, wq_v, wkv_v, wo_v, key_v, val_v, len_s, req_s, first_s, slot_s, lim_s, new_s, own_s,
    part, part_in, table, pick, col_req, leader, qkv, scores, maxima, tops, stat_top, spans,
    soft_out, soft_in, stat, blend, att, att_wide, sums, sums_in, done, local_sem, send_sem, recv_sem,
):
    g, t, m = lax.axis_index("grp"), lax.axis_index("tp"), lax.axis_index("mem")
    owners = n_grp * n_mem
    owner = g * n_mem + m
    rows, width = tok_v.shape
    requests = len_s.shape[0]
    own_rows = rows // n_mem
    out_rows = rows // n_tp
    spans_here = req_s.shape[0]
    q_cols = wq_v.shape[1]
    head_dim = key_v.shape[3]
    heads = q_cols // head_dim
    tile = own_rows * SLOTS
    k_chunks = 6
    k_step = width // k_chunks

    small = [
        pltpu.make_async_copy(req_len, len_s, local_sem.at[0]),
        pltpu.make_async_copy(span_request, req_s, local_sem.at[1]),
        pltpu.make_async_copy(span_first, first_s, local_sem.at[2]),
        pltpu.make_async_copy(new_slot, slot_s, local_sem.at[3]),
    ]
    tok_copy = pltpu.make_async_copy(tokens, tok_v, local_sem.at[4])
    gain_copy = pltpu.make_async_copy(gain, gain_v, local_sem.at[5])
    wkv_copy = pltpu.make_async_copy(w_keyval, wkv_v, local_sem.at[6])
    key_copy = pltpu.make_async_copy(key_cache, key_v, local_sem.at[7])
    val_copy = pltpu.make_async_copy(value_cache, val_v, local_sem.at[8])
    out_copy = pltpu.make_async_copy(w_out, wo_v, local_sem.at[9])
    wq_copies = [
        pltpu.make_async_copy(
            w_query.at[pl.ds(c * k_step, k_step), :], wq_v.at[pl.ds(c * k_step, k_step), :], local_sem.at[10 + c]
        )
        for c in range(k_chunks)
    ]
    tok_copy.start()
    gain_copy.start()
    for copy in wq_copies + [wkv_copy] + small + [key_copy, val_copy, out_copy]:
        copy.start()

    barrier = pltpu.get_barrier_semaphore()

    def owner_at(i):
        place = lax.rem(owner + i, owners)
        return place, {"grp": place // n_mem, "mem": lax.rem(place, n_mem)}

    def greet_owner(i, carry):
        pl.semaphore_signal(barrier, inc=1, device_id=owner_at(i)[1], device_id_type=MESH)
        return carry

    def greet_head(i, carry):
        pl.semaphore_signal(barrier, inc=1, device_id={"tp": lax.rem(t + i, n_tp)}, device_id_type=MESH)
        return carry

    lax.fori_loop(1, owners, greet_owner, 0)
    lax.fori_loop(1, n_tp, greet_head, 0)

    tok_copy.wait()
    gain_copy.wait()
    wide = tok_v[...].astype(f32)
    square = jnp.sum(wide * wide, axis=1, keepdims=True)
    scaled = (wide * gain_v[...].reshape(1, width)).astype(bf16)
    projected = jnp.zeros((rows, q_cols), f32)
    for c in range(k_chunks):
        wq_copies[c].wait()
        projected += jnp.dot(
            scaled[:, c * k_step : (c + 1) * k_step],
            wq_v[c * k_step : (c + 1) * k_step, :],
            preferred_element_type=f32,
        )
    wkv_copy.wait()
    new_part = [jnp.dot(scaled, wkv_v[i], preferred_element_type=f32) for i in range(2)]
    pieces = [projected[:, h * head_dim : (h + 1) * head_dim] for h in range(heads)] + new_part
    pieces += [jnp.broadcast_to(square, (rows, head_dim))]
    pieces += [jnp.zeros((rows, head_dim), f32)] * (SLOTS - len(pieces))
    for h, piece in enumerate(pieces):
        part[pl.ds(h, rows, stride=SLOTS), :] = piece

    pl.semaphore_wait(barrier, owners - 1 + n_tp - 1)

    def send_part(i, carry):
        to = lax.rem(m + i, n_mem)
        pltpu.make_async_remote_copy(
            src_ref=part.at[pl.ds(pl.multiple_of(to * tile, tile), tile), :],
            dst_ref=part_in.at[m],
            send_sem=send_sem.at[0],
            recv_sem=recv_sem.at[0],
            device_id={"mem": to},
            device_id_type=MESH,
        ).start()
        return carry

    lax.fori_loop(1, n_mem, send_part, 0)
    part_in[m] = part[pl.ds(pl.multiple_of(m * tile, tile), tile), :]

    for copy in small:
        copy.wait()
    lane = iota((1, head_dim), 1)
    own_len = [len_s[g * rows + m * own_rows + i] for i in range(own_rows)]
    position = jnp.where(iota((tile, 1), 0) < SLOTS, own_len[0], own_len[1]).astype(f32)
    half = head_dim // 2
    power = (lax.rem(lane, half).astype(f32) * 2.0) / head_dim
    frequency = jnp.exp(power * -jnp.log(jnp.full((1, head_dim), rope_base, f32)))
    angles = position * frequency
    slot_row = lax.rem(iota((tile, head_dim), 0), SLOTS)
    turned = slot_row < heads + 1
    cosine = jnp.where(turned, jnp.cos(angles), 1.0)
    sine = jnp.where(turned, jnp.sin(angles), 0.0)
    table[0] = cosine
    table[1] = jnp.where(lane < half, -sine, sine)

    def span_scalars(c, carry):
        r = jnp.maximum(req_s[c], 0)
        limit = jnp.where(req_s[c] >= 0, len_s[r] - first_s[c], -1)
        lim_s[c] = limit
        new_s[c] = jnp.where(slot_s[r] == owner * spans_here + c, limit, -1)
        own_s[c] = r
        return carry

    lax.fori_loop(0, spans_here, span_scalars, 0)

    flat = spans_here * SLOTS
    column = iota((1, flat), 1)
    target = jnp.zeros((1, flat), jnp.int32)
    in_rows = iota((spans_here, head_dim), 0)
    by_row = jnp.zeros((spans_here, head_dim), jnp.int32)
    for c in range(spans_here):
        target = jnp.where(column // SLOTS == c, req_s[c] * SLOTS, target)
        by_row = jnp.where(in_rows == c, req_s[c], by_row)
    target = target + lax.rem(column, SLOTS)
    col_req[...] = by_row
    first_of = jnp.ones((spans_here, head_dim), f32)
    for c in range(spans_here):
        first_of = jnp.where((by_row == req_s[c]) & (in_rows > c), 0.0, first_of)
    leader[...] = first_of

    pick_rows = 128

    def fill_pick(b, carry):
        at = pl.multiple_of(b * pick_rows, pick_rows)
        row = iota((pick_rows, flat), 0) + at
        pick[pl.ds(at, pick_rows), :] = jnp.where(row == target, 1.0, 0.0).astype(bf16)
        return carry

    lax.fori_loop(0, requests * SLOTS // pick_rows, fill_pick, 0)

    def wait_for(buffer, amount, kind):
        ref = buffer.at[pl.ds(0, amount)]
        pltpu.make_async_copy(ref, ref, kind).wait()

    wait_for(part_in, n_mem - 1, recv_sem.at[0])
    total = part_in[0]
    for i in range(1, n_mem):
        total = total + part_in[i]
    normed = []
    for i in range(own_rows):
        block = total[i * SLOTS : (i + 1) * SLOTS]
        root_mean = jnp.sqrt(block[heads + 2 : heads + 3] / D + epsilon)
        normed.append(block / root_mean)
    normed = jnp.concatenate(normed, axis=0)
    finished = normed * table[0] + pltpu.roll(normed, half, axis=1) * table[1]
    qkv[pl.ds(owner * own_rows, own_rows)] = finished.astype(bf16).reshape(own_rows, SLOTS, head_dim)

    def send_rows(i, carry):
        here = pl.ds(owner * own_rows, own_rows)
        pltpu.make_async_remote_copy(
            src_ref=qkv.at[here],
            dst_ref=qkv.at[here],
            send_sem=send_sem.at[1],
            recv_sem=recv_sem.at[1],
            device_id=owner_at(i)[1],
            device_id_type=MESH,
        ).start()
        return carry

    lax.fori_loop(1, owners, send_rows, 0)
    key_copy.wait()
    val_copy.wait()
    wait_for(qkv, (owners - 1) * own_rows, recv_sem.at[1])

    scale = head_dim**-0.5
    head = iota((SLOTS, head_dim), 0)
    lanes = iota((SLOTS, head_dim), 1)
    diagonal = lanes == head
    repeated = lax.rem(lanes, SLOTS) == head

    def score(c):
        tile_c = qkv[own_s[c]]
        raw = lax.dot_general(tile_c, key_v[0, c], (((1,), (1,)), ((), ())), preferred_element_type=f32)
        tile_wide = tile_c.astype(f32)
        fresh = jnp.sum(tile_wide * tile_wide[heads : heads + 1], axis=1, keepdims=True)
        shown = jnp.where(lanes <= lim_s[c], jnp.where(lanes == new_s[c], fresh, raw) * scale, very_low)
        top = jnp.max(shown, axis=1, keepdims=True)
        top_row = jnp.sum(jnp.where(repeated, top, 0.0), axis=0, keepdims=True)

        def store():
            scores[c] = shown
            maxima[pl.ds(c, 1), :] = top_row

        return store

    chunks(spans_here, 8, score)
    every = maxima[...]
    request_top = every
    for c in range(spans_here):
        request_top = jnp.maximum(request_top, jnp.where(col_req[...] == req_s[c], every[c : c + 1], very_low))
    tops[...] = request_top
    group = lane // SLOTS
    high = request_top.astype(bf16).astype(f32)
    middle = (request_top - high).astype(bf16).astype(f32)
    low = request_top - high - middle
    told = jnp.where(group == 2, high, jnp.where(group == 3, middle, jnp.where(group == 4, low, 0.0)))
    stat_top[...] = told * leader[...]

    def weigh(c):
        tile_c = qkv[own_s[c]]
        top = jnp.sum(jnp.where(diagonal, tops[pl.ds(c, 1), :], 0.0), axis=1, keepdims=True)
        weights = jnp.exp(scores[c] - top)
        total = jnp.sum(weights, axis=1, keepdims=True)
        is_new = lanes == new_s[c]
        fresh = jnp.sum(jnp.where(is_new, weights, 0.0), axis=1, keepdims=True)
        rounded = jnp.where(is_new, 0.0, weights).astype(bf16)
        value = jnp.dot(rounded, val_v[0, c], preferred_element_type=f32)
        value += fresh.astype(bf16).astype(f32) * tile_c[heads + 1 : heads + 2].astype(f32)
        total_row = jnp.sum(jnp.where(repeated, total, 0.0), axis=0, keepdims=True)
        total_high = total_row.astype(bf16).astype(f32)
        row = jnp.where(group == 0, total_high, jnp.where(group == 1, total_row - total_high, stat_top[pl.ds(c, 1), :]))
        result = jnp.where(head == heads, row, value).astype(bf16)

        def store():
            spans[pl.ds(pl.multiple_of(c * SLOTS, SLOTS), SLOTS), :] = result

        return store

    chunks(spans_here, 8, weigh)

    parts = 4
    at_once = owners // parts

    def gather(b, carry):
        at = pl.multiple_of(b * at_once * tile, at_once * tile)
        summed = jnp.dot(pick[pl.ds(at, at_once * tile), :], spans[...], preferred_element_type=f32)
        soft_out[pl.ds(b * at_once, at_once)] = summed.astype(bf16).reshape(at_once, tile, head_dim)
        return carry

    lax.fori_loop(0, parts, gather, 0)

    def send_soft(i, carry):
        place, device = owner_at(i)
        pltpu.make_async_remote_copy(
            src_ref=soft_out.at[place],
            dst_ref=soft_in.at[owner],
            send_sem=send_sem.at[2],
            recv_sem=recv_sem.at[2],
            device_id=device,
            device_id_type=MESH,
        ).start()
        return carry

    lax.fori_loop(1, owners, send_soft, 0)
    soft_in[owner] = soft_out[owner]
    wait_for(soft_in, owners - 1, recv_sem.at[2])

    def read_stat(s):
        lower = [soft_in[s, i * SLOTS : (i + 1) * SLOTS, :].astype(f32)[heads : heads + 1] for i in range(own_rows)]

        def store():
            for i in range(own_rows):
                stat[i, pl.ds(s, 1), :] = lower[i]

        return store

    chunks(owners, 8, read_stat)
    for i in range(own_rows):
        said = stat[i]

        def lanes_from(k):
            return pltpu.roll(said, head_dim - k * SLOTS, axis=1)

        total = said + lanes_from(1)
        top = jnp.where(total > 0.0, lanes_from(2) + lanes_from(3) + lanes_from(4), very_low)
        factor = jnp.exp(top - jnp.max(top, axis=0, keepdims=True))
        blend[i] = factor / jnp.sum(factor * total, axis=0, keepdims=True)

    def join(b, carry):
        sums_now = list(carry)
        for u in range(8):
            s = b * 8 + u
            for i in range(own_rows):
                factor = jnp.sum(jnp.where(diagonal, blend[i, pl.ds(s, 1), :], 0.0), axis=1, keepdims=True)
                sums_now[i] = sums_now[i] + factor * soft_in[s, i * SLOTS : (i + 1) * SLOTS, :].astype(f32)
        return tuple(sums_now)

    joined = lax.fori_loop(0, owners // 8, join, tuple(jnp.zeros((SLOTS, head_dim), f32) for _ in range(own_rows)))
    for i in range(own_rows):
        att[m * own_rows + i] = joined[i].astype(bf16)

    def send_att(i, carry):
        here = pl.ds(m * own_rows, own_rows)
        pltpu.make_async_remote_copy(
            src_ref=att.at[here],
            dst_ref=att.at[here],
            send_sem=send_sem.at[3],
            recv_sem=recv_sem.at[3],
            device_id={"mem": lax.rem(m + i, n_mem)},
            device_id_type=MESH,
        ).start()
        return carry

    lax.fori_loop(1, n_mem, send_att, 0)
    out_copy.wait()
    wait_for(att, (n_mem - 1) * own_rows, recv_sem.at[3])

    att_wide[...] = att[...].astype(f32).reshape(rows * SLOTS, head_dim)
    left = jnp.concatenate([att_wide[pl.ds(h, rows, stride=SLOTS), :] for h in range(heads)], axis=1).astype(bf16)
    product = jnp.dot(left, wo_v[...], preferred_element_type=f32)
    out_cols = product.shape[1] // head_dim
    for n in range(out_cols):
        sums[pl.ds(n, rows, stride=out_cols), :] = product[:, n * head_dim : (n + 1) * head_dim]

    slab = out_rows * out_cols

    def send_sums(i, carry):
        to = lax.rem(t + i, n_tp)
        pltpu.make_async_remote_copy(
            src_ref=sums.at[pl.ds(pl.multiple_of(to * slab, 8), slab), :],
            dst_ref=sums_in.at[t],
            send_sem=send_sem.at[4],
            recv_sem=recv_sem.at[4],
            device_id={"tp": to},
            device_id_type=MESH,
        ).start()
        return carry

    lax.fori_loop(1, n_tp, send_sums, 0)
    sums_in[t] = sums[pl.ds(pl.multiple_of(t * slab, 8), slab), :]
    wait_for(sums_in, n_tp - 1, recv_sem.at[4])
    total = sums_in[0]
    for i in range(1, n_tp):
        total = total + sums_in[i]
    here = pl.ds(pl.multiple_of(t * slab, 8), slab)
    done[here, :] = total

    def send_done(i, carry):
        pltpu.make_async_remote_copy(
            src_ref=done.at[here, :],
            dst_ref=done.at[here, :],
            send_sem=send_sem.at[5],
            recv_sem=recv_sem.at[5],
            device_id={"tp": lax.rem(t + i, n_tp)},
            device_id_type=MESH,
        ).start()
        return carry

    lax.fori_loop(1, n_tp, send_done, 0)
    wait_for(done, (n_tp - 1) * slab, recv_sem.at[5])
    for n in range(out_cols):
        out[:, n * head_dim : (n + 1) * head_dim] = done[pl.ds(n, rows, stride=out_cols), :].astype(bf16)

    wait_for(part, (n_mem - 1) * tile, send_sem.at[0])
    wait_for(qkv, (owners - 1) * own_rows, send_sem.at[1])
    wait_for(soft_out, owners - 1, send_sem.at[2])
    wait_for(att, (n_mem - 1) * own_rows, send_sem.at[3])
    wait_for(sums, (n_tp - 1) * slab, send_sem.at[4])
    wait_for(done, (n_tp - 1) * slab, send_sem.at[5])


def per_device(n_grp, n_tp, n_mem, *args):
    tokens, norm_gain, w_query, w_keyval, w_out, key_cache, value_cache, req_len, span_request, _, _ = args
    rows, width = tokens.shape
    q_cols = w_query.shape[1]
    head_dim = key_cache.shape[3]
    spans_here = span_request.shape[0]
    requests = req_len.shape[0]
    owners = n_grp * n_mem
    own_rows = rows // n_mem
    tile = own_rows * SLOTS
    out_width = w_out.shape[1]
    slab = rows // n_tp * out_width // head_dim
    scratch = [
        pltpu.VMEM(tokens.shape, bf16),
        pltpu.VMEM(norm_gain.shape, f32),
        pltpu.VMEM(w_query.shape, bf16),
        pltpu.VMEM(w_keyval.shape, bf16),
        pltpu.VMEM(w_out.shape, bf16),
        pltpu.VMEM(key_cache.shape, bf16),
        pltpu.VMEM(value_cache.shape, bf16),
        pltpu.SMEM((requests,), jnp.int32),
        pltpu.SMEM((spans_here,), jnp.int32),
        pltpu.SMEM((spans_here,), jnp.int32),
        pltpu.SMEM((requests,), jnp.int32),
        pltpu.SMEM((spans_here,), jnp.int32),
        pltpu.SMEM((spans_here,), jnp.int32),
        pltpu.SMEM((spans_here,), jnp.int32),
        pltpu.VMEM((rows * SLOTS, head_dim), f32),
        pltpu.VMEM((n_mem, tile, head_dim), f32),
        pltpu.VMEM((2, tile, head_dim), f32),
        pltpu.VMEM((requests * SLOTS, spans_here * SLOTS), bf16),
        pltpu.VMEM((spans_here, head_dim), jnp.int32),
        pltpu.VMEM((spans_here, head_dim), f32),
        pltpu.VMEM((requests, SLOTS, head_dim), bf16),
        pltpu.VMEM((spans_here, SLOTS, head_dim), f32),
        pltpu.VMEM((spans_here, head_dim), f32),
        pltpu.VMEM((spans_here, head_dim), f32),
        pltpu.VMEM((spans_here, head_dim), f32),
        pltpu.VMEM((spans_here * SLOTS, head_dim), bf16),
        pltpu.VMEM((owners, tile, head_dim), bf16),
        pltpu.VMEM((owners, tile, head_dim), bf16),
        pltpu.VMEM((own_rows, owners, head_dim), f32),
        pltpu.VMEM((own_rows, owners, head_dim), f32),
        pltpu.VMEM((rows, SLOTS, head_dim), bf16),
        pltpu.VMEM((rows * SLOTS, head_dim), f32),
        pltpu.VMEM((rows * out_width // head_dim, head_dim), f32),
        pltpu.VMEM((n_tp, slab, head_dim), f32),
        pltpu.VMEM((rows * out_width // head_dim, head_dim), f32),
        pltpu.SemaphoreType.DMA((16,)),
        pltpu.SemaphoreType.DMA((6,)),
        pltpu.SemaphoreType.DMA((6,)),
    ]
    return pl.pallas_call(
        functools.partial(kernel, n_grp, n_tp, n_mem),
        out_shape=jax.ShapeDtypeStruct((rows, out_width), bf16),
        in_specs=[pl.BlockSpec(memory_space=HBM)] * len(args),
        out_specs=pl.BlockSpec(memory_space=pltpu.VMEM),
        scratch_shapes=scratch,
        compiler_params=pltpu.CompilerParams(
            collective_id=0, has_side_effects=True, vmem_limit_bytes=40 * 1024 * 1024
        ),
        cost_estimate=pl.CostEstimate(flops=200_000_000, bytes_accessed=12_600_000, transcendentals=100_000),
    )(*args)


def solution(mesh):
    placed = (
        P("grp", "mem"),
        P("mem"),
        P("mem", "tp"),
        P(None, "mem", "tp"),
        P("tp", "mem"),
        P("tp", ("grp", "mem"), None, None),
        P("tp", ("grp", "mem"), None, None),
        P(),
        P(("grp", "mem")),
        P(("grp", "mem")),
        P(),
    )
    body = functools.partial(per_device, mesh.shape["grp"], mesh.shape["tp"], mesh.shape["mem"])
    return jax.shard_map(body, mesh=mesh, in_specs=placed, out_specs=P("grp", "mem"), check_vma=False)
```

```python
import functools

import jax
import jax.numpy as jnp
from jax import lax
from jax.experimental import pallas as pl
from jax.experimental.pallas import tpu as pltpu
from jax.sharding import PartitionSpec as P

MESH = pl.DeviceIdType.MESH
HBM = pltpu.MemorySpace.HBM
D = 12288
epsilon = 1e-05
rope_base = 1000000.0
very_low = -1e30
SLOTS = 16
f32 = jnp.float32
bf16 = jnp.bfloat16


def chunks(count, width, body):
    def step(b, carry):
        stores = [body(b * width + u) for u in range(width)]
        for store in stores:
            store()
        return carry

    lax.fori_loop(0, count // width, step, 0)


def hops(d, size):
    return min(d, size - d)


def far_first(size, each):
    chips = sorted(range(size), key=lambda d: -hops(d, size))
    return [d * each + c for d in chips for c in range(each)]


def iota(shape, dim):
    return lax.broadcasted_iota(jnp.int32, shape, dim)


def kernel(
    n_grp, n_tp, n_mem,
    tokens, gain, w_query, w_keyval, w_out, key_cache, value_cache, req_len, span_request, span_first, new_slot,
    out,
    tok_v, gain_v, wq_v, wkv_v, wo_v, key_v, val_v, len_s, req_s, first_s, slot_s, lim_s, new_s, own_s,
    part, part_in, table, pick, col_req, leader, qkv, scores, maxima, tops, stat_top, spans,
    soft_out, soft_in, stat, blend, att, att_wide, wide_rows, sums, sums_in, done, local_sem, send_sem, recv_sem,
):
    g, t, m = lax.axis_index("grp"), lax.axis_index("tp"), lax.axis_index("mem")
    owners = n_grp * n_mem
    owner = g * n_mem + m
    rows, width = tok_v.shape
    requests = len_s.shape[0]
    own_rows = rows // n_mem
    out_rows = rows // n_tp
    spans_here = req_s.shape[0]
    q_cols = wq_v.shape[1]
    head_dim = key_v.shape[3]
    heads = q_cols // head_dim
    tile = own_rows * SLOTS
    k_chunks = 6
    k_step = width // k_chunks

    small = [
        pltpu.make_async_copy(req_len, len_s, local_sem.at[0]),
        pltpu.make_async_copy(span_request, req_s, local_sem.at[1]),
        pltpu.make_async_copy(span_first, first_s, local_sem.at[2]),
        pltpu.make_async_copy(new_slot, slot_s, local_sem.at[3]),
    ]
    tok_copy = pltpu.make_async_copy(tokens, tok_v, local_sem.at[4])
    gain_copy = pltpu.make_async_copy(gain, gain_v, local_sem.at[5])
    wkv_copy = pltpu.make_async_copy(w_keyval, wkv_v, local_sem.at[6])
    key_copy = pltpu.make_async_copy(key_cache, key_v, local_sem.at[7])
    val_copy = pltpu.make_async_copy(value_cache, val_v, local_sem.at[8])
    out_copy = pltpu.make_async_copy(w_out, wo_v, local_sem.at[9])
    wq_copies = [
        pltpu.make_async_copy(
            w_query.at[pl.ds(c * k_step, k_step), :], wq_v.at[pl.ds(c * k_step, k_step), :], local_sem.at[10 + c]
        )
        for c in range(k_chunks)
    ]
    tok_copy.start()
    gain_copy.start()
    for copy in wq_copies + [wkv_copy] + small:
        copy.start()

    barrier = pltpu.get_barrier_semaphore()

    def owner_at(dg, dm):
        to_g = lax.rem(g + dg, n_grp)
        to_m = lax.rem(m // 2 + dm // 2, n_mem // 2) * 2 + lax.rem(m + dm, 2)
        return to_g * n_mem + to_m, {"grp": to_g, "mem": to_m}

    mem_order = far_first(n_mem // 2, 2)
    for dg in far_first(n_grp, 1):
        for dm in mem_order:
            if dg or dm:
                pl.semaphore_signal(barrier, inc=1, device_id=owner_at(dg, dm)[1], device_id_type=MESH)
    tp_order = [d for d in far_first(n_tp, 1) if d]
    for d in tp_order:
        pl.semaphore_signal(barrier, inc=1, device_id={"tp": lax.rem(t + d, n_tp)}, device_id_type=MESH)
    mem_order = [d for d in mem_order if d]
    owner_order = sorted(
        [(dg, dm) for dg in range(n_grp) for dm in range(n_mem) if dg or dm],
        key=lambda d: -hops(d[0], n_grp) - hops(d[1] // 2, n_mem // 2),
    )

    tok_copy.wait()
    gain_copy.wait()
    wide = tok_v[...].astype(f32)
    square = jnp.sum(wide * wide, axis=1, keepdims=True)
    scaled = (wide * gain_v[...].reshape(1, width)).astype(bf16)
    projected = jnp.zeros((rows, q_cols), f32)
    for c in range(k_chunks):
        wq_copies[c].wait()
        projected += jnp.dot(
            scaled[:, c * k_step : (c + 1) * k_step],
            wq_v[c * k_step : (c + 1) * k_step, :],
            preferred_element_type=f32,
        )
    wkv_copy.wait()
    for copy in (key_copy, val_copy, out_copy):
        copy.start()
    new_part = [jnp.dot(scaled, wkv_v[i], preferred_element_type=f32) for i in range(2)]
    pieces = [projected[:, h * head_dim : (h + 1) * head_dim] for h in range(heads)] + new_part
    pieces += [jnp.broadcast_to(square, (rows, head_dim))]
    pieces += [jnp.zeros((rows, head_dim), f32)] * (SLOTS - len(pieces))
    for h, piece in enumerate(pieces):
        part[pl.ds(h, rows, stride=SLOTS), :] = piece

    pl.semaphore_wait(barrier, owners - 1 + n_tp - 1)

    for d in mem_order:
        to = owner_at(0, d)[1]["mem"]
        pltpu.make_async_remote_copy(
            src_ref=part.at[pl.ds(pl.multiple_of(to * tile, tile), tile), :],
            dst_ref=part_in.at[m],
            send_sem=send_sem.at[0],
            recv_sem=recv_sem.at[0],
            device_id={"mem": to},
            device_id_type=MESH,
        ).start()
    part_in[m] = part[pl.ds(pl.multiple_of(m * tile, tile), tile), :]

    for copy in small:
        copy.wait()
    lane = iota((1, head_dim), 1)
    own_len = [len_s[g * rows + m * own_rows + i] for i in range(own_rows)]
    position = jnp.where(iota((tile, 1), 0) < SLOTS, own_len[0], own_len[1]).astype(f32)
    half = head_dim // 2
    power = (lax.rem(lane, half).astype(f32) * 2.0) / head_dim
    frequency = jnp.exp(power * -jnp.log(jnp.full((1, head_dim), rope_base, f32)))
    angles = position * frequency
    slot_row = lax.rem(iota((tile, head_dim), 0), SLOTS)
    turned = slot_row < heads + 1
    cosine = jnp.where(turned, jnp.cos(angles), 1.0)
    sine = jnp.where(turned, jnp.sin(angles), 0.0)
    table[0] = cosine
    table[1] = jnp.where(lane < half, -sine, sine)

    def span_scalars(c, carry):
        r = jnp.maximum(req_s[c], 0)
        limit = jnp.where(req_s[c] >= 0, len_s[r] - first_s[c], -1)
        lim_s[c] = limit
        new_s[c] = jnp.where(slot_s[r] == owner * spans_here + c, limit, -1)
        own_s[c] = r
        return carry

    lax.fori_loop(0, spans_here, span_scalars, 0)

    flat = spans_here * SLOTS
    column = iota((1, flat), 1)
    target = jnp.zeros((1, flat), jnp.int32)
    in_rows = iota((spans_here, head_dim), 0)
    by_row = jnp.zeros((spans_here, head_dim), jnp.int32)
    for c in range(spans_here):
        target = jnp.where(column // SLOTS == c, req_s[c] * SLOTS, target)
        by_row = jnp.where(in_rows == c, req_s[c], by_row)
    target = target + lax.rem(column, SLOTS)
    col_req[...] = by_row
    first_of = jnp.ones((spans_here, head_dim), f32)
    for c in range(spans_here):
        first_of = jnp.where((by_row == req_s[c]) & (in_rows > c), 0.0, first_of)
    leader[...] = first_of

    pick_rows = 128

    def fill_pick(b, carry):
        at = pl.multiple_of(b * pick_rows, pick_rows)
        row = iota((pick_rows, flat), 0) + at
        pick[pl.ds(at, pick_rows), :] = jnp.where(row == target, 1.0, 0.0).astype(bf16)
        return carry

    lax.fori_loop(0, requests * SLOTS // pick_rows, fill_pick, 0)

    def wait_for(buffer, amount, kind):
        ref = buffer.at[pl.ds(0, amount)]
        pltpu.make_async_copy(ref, ref, kind).wait()

    wait_for(part_in, n_mem - 1, recv_sem.at[0])
    total = part_in[0]
    for i in range(1, n_mem):
        total = total + part_in[i]
    normed = []
    for i in range(own_rows):
        block = total[i * SLOTS : (i + 1) * SLOTS]
        root_mean = jnp.sqrt(block[heads + 2 : heads + 3] / D + epsilon)
        normed.append(block / root_mean)
    normed = jnp.concatenate(normed, axis=0)
    finished = normed * table[0] + pltpu.roll(normed, half, axis=1) * table[1]
    qkv[pl.ds(owner * own_rows, own_rows)] = finished.astype(bf16).reshape(own_rows, SLOTS, head_dim)

    here = pl.ds(owner * own_rows, own_rows)
    for d in owner_order:
        pltpu.make_async_remote_copy(
            src_ref=qkv.at[here],
            dst_ref=qkv.at[here],
            send_sem=send_sem.at[1],
            recv_sem=recv_sem.at[1],
            device_id=owner_at(*d)[1],
            device_id_type=MESH,
        ).start()
    key_copy.wait()
    val_copy.wait()
    wait_for(qkv, (owners - 1) * own_rows, recv_sem.at[1])

    scale = head_dim**-0.5
    head = iota((SLOTS, head_dim), 0)
    lanes = iota((SLOTS, head_dim), 1)
    diagonal = lanes == head
    repeated = lax.rem(lanes, SLOTS) == head

    def score(c):
        tile_c = qkv[own_s[c]]
        raw = lax.dot_general(tile_c, key_v[0, c], (((1,), (1,)), ((), ())), preferred_element_type=f32)
        tile_wide = tile_c.astype(f32)
        fresh = jnp.sum(tile_wide * tile_wide[heads : heads + 1], axis=1, keepdims=True)
        shown = jnp.where(lanes <= lim_s[c], jnp.where(lanes == new_s[c], fresh, raw) * scale, very_low)
        top = jnp.max(shown, axis=1, keepdims=True)
        top_row = jnp.sum(jnp.where(repeated, top, 0.0), axis=0, keepdims=True)

        def store():
            scores[c] = shown
            maxima[pl.ds(c, 1), :] = top_row

        return store

    chunks(spans_here, 8, score)
    every = maxima[...]
    request_top = every
    for c in range(spans_here):
        request_top = jnp.maximum(request_top, jnp.where(col_req[...] == req_s[c], every[c : c + 1], very_low))
    tops[...] = request_top
    group = lane // SLOTS
    high = request_top.astype(bf16).astype(f32)
    middle = (request_top - high).astype(bf16).astype(f32)
    low = request_top - high - middle
    told = jnp.where(group == 2, high, jnp.where(group == 3, middle, jnp.where(group == 4, low, 0.0)))
    stat_top[...] = told * leader[...]

    def weigh(c):
        tile_c = qkv[own_s[c]]
        top = jnp.sum(jnp.where(diagonal, tops[pl.ds(c, 1), :], 0.0), axis=1, keepdims=True)
        weights = jnp.exp(scores[c] - top)
        total = jnp.sum(weights, axis=1, keepdims=True)
        is_new = lanes == new_s[c]
        fresh = jnp.sum(jnp.where(is_new, weights, 0.0), axis=1, keepdims=True)
        rounded = jnp.where(is_new, 0.0, weights).astype(bf16)
        value = jnp.dot(rounded, val_v[0, c], preferred_element_type=f32)
        value += fresh.astype(bf16).astype(f32) * tile_c[heads + 1 : heads + 2].astype(f32)
        total_row = jnp.sum(jnp.where(repeated, total, 0.0), axis=0, keepdims=True)
        total_high = total_row.astype(bf16).astype(f32)
        row = jnp.where(group == 0, total_high, jnp.where(group == 1, total_row - total_high, stat_top[pl.ds(c, 1), :]))
        result = jnp.where(head == heads, row, value).astype(bf16)

        def store():
            spans[pl.ds(pl.multiple_of(c * SLOTS, SLOTS), SLOTS), :] = result

        return store

    chunks(spans_here, 8, weigh)

    for dg in far_first(n_grp, 1):
        group_of = lax.rem(g + dg, n_grp)
        at = pl.multiple_of(group_of * n_mem * tile, n_mem * tile)
        summed = jnp.dot(pick[pl.ds(at, n_mem * tile), :], spans[...], preferred_element_type=f32)
        soft_out[pl.ds(group_of * n_mem, n_mem)] = summed.astype(bf16).reshape(n_mem, tile, head_dim)
        for d in mem_order if dg == 0 else mem_order + [0]:
            place, device = owner_at(dg, d)
            pltpu.make_async_remote_copy(
                src_ref=soft_out.at[place],
                dst_ref=soft_in.at[owner],
                send_sem=send_sem.at[2],
                recv_sem=recv_sem.at[2],
                device_id=device,
                device_id_type=MESH,
            ).start()
    soft_in[owner] = soft_out[owner]
    wait_for(soft_in, owners - 1, recv_sem.at[2])

    def read_stat(s):
        lower = [soft_in[s, i * SLOTS : (i + 1) * SLOTS, :].astype(f32)[heads : heads + 1] for i in range(own_rows)]

        def store():
            for i in range(own_rows):
                stat[i, pl.ds(s, 1), :] = lower[i]

        return store

    chunks(owners, 8, read_stat)
    for i in range(own_rows):
        said = stat[i]

        def lanes_from(k):
            return pltpu.roll(said, head_dim - k * SLOTS, axis=1)

        total = said + lanes_from(1)
        top = jnp.where(total > 0.0, lanes_from(2) + lanes_from(3) + lanes_from(4), very_low)
        factor = jnp.exp(top - jnp.max(top, axis=0, keepdims=True))
        blend[i] = factor / jnp.sum(factor * total, axis=0, keepdims=True)

    def join(b, carry):
        sums_now = list(carry)
        for u in range(8):
            s = b * 8 + u
            for i in range(own_rows):
                factor = jnp.sum(jnp.where(diagonal, blend[i, pl.ds(s, 1), :], 0.0), axis=1, keepdims=True)
                sums_now[i] = sums_now[i] + factor * soft_in[s, i * SLOTS : (i + 1) * SLOTS, :].astype(f32)
        return tuple(sums_now)

    joined = lax.fori_loop(0, owners // 8, join, tuple(jnp.zeros((SLOTS, head_dim), f32) for _ in range(own_rows)))
    for i in range(own_rows):
        att[m * own_rows + i] = joined[i].astype(bf16)

    here = pl.ds(m * own_rows, own_rows)
    for d in mem_order:
        pltpu.make_async_remote_copy(
            src_ref=att.at[here],
            dst_ref=att.at[here],
            send_sem=send_sem.at[3],
            recv_sem=recv_sem.at[3],
            device_id={"mem": owner_at(0, d)[1]["mem"]},
            device_id_type=MESH,
        ).start()
    out_copy.wait()
    wait_for(att, (n_mem - 1) * own_rows, recv_sem.at[3])

    out_cols = wo_v.shape[1] // head_dim
    slab = out_rows * SLOTS
    for n in range(out_cols, SLOTS):
        wide_rows[pl.ds(n, rows, stride=SLOTS), :] = jnp.zeros((rows, head_dim), f32)
    att_wide[...] = att[...].astype(f32).reshape(rows * SLOTS, head_dim)
    left = jnp.concatenate([att_wide[pl.ds(h, rows, stride=SLOTS), :] for h in range(heads)], axis=1).astype(bf16)
    product = jnp.dot(left, wo_v[...], preferred_element_type=f32)
    for n in range(out_cols):
        wide_rows[pl.ds(n, rows, stride=SLOTS), :] = product[:, n * head_dim : (n + 1) * head_dim]
    sums[...] = wide_rows[...].astype(bf16).reshape(n_tp, slab, head_dim)

    for d in tp_order:
        to = lax.rem(t + d, n_tp)
        pltpu.make_async_remote_copy(
            src_ref=sums.at[to],
            dst_ref=sums_in.at[t],
            send_sem=send_sem.at[4],
            recv_sem=recv_sem.at[4],
            device_id={"tp": to},
            device_id_type=MESH,
        ).start()
    sums_in[t] = sums[t]
    wait_for(sums_in, n_tp - 1, recv_sem.at[4])
    total = sums_in[0].astype(f32)
    for i in range(1, n_tp):
        total = total + sums_in[i].astype(f32)
    done[t] = total.astype(bf16)
    for d in tp_order:
        pltpu.make_async_remote_copy(
            src_ref=done.at[t],
            dst_ref=done.at[t],
            send_sem=send_sem.at[5],
            recv_sem=recv_sem.at[5],
            device_id={"tp": lax.rem(t + d, n_tp)},
            device_id_type=MESH,
        ).start()
    wait_for(done, n_tp - 1, recv_sem.at[5])
    wide_rows[...] = done[...].astype(f32).reshape(rows * SLOTS, head_dim)
    for n in range(out_cols):
        out[:, n * head_dim : (n + 1) * head_dim] = wide_rows[pl.ds(n, rows, stride=SLOTS), :].astype(bf16)

    wait_for(part, (n_mem - 1) * tile, send_sem.at[0])
    wait_for(qkv, (owners - 1) * own_rows, send_sem.at[1])
    wait_for(soft_out, owners - 1, send_sem.at[2])
    wait_for(att, (n_mem - 1) * own_rows, send_sem.at[3])
    wait_for(sums, n_tp - 1, send_sem.at[4])
    wait_for(done, n_tp - 1, send_sem.at[5])


def per_device(n_grp, n_tp, n_mem, *args):
    tokens, norm_gain, w_query, w_keyval, w_out, key_cache, value_cache, req_len, span_request, _, _ = args
    rows, width = tokens.shape
    q_cols = w_query.shape[1]
    head_dim = key_cache.shape[3]
    spans_here = span_request.shape[0]
    requests = req_len.shape[0]
    owners = n_grp * n_mem
    own_rows = rows // n_mem
    tile = own_rows * SLOTS
    out_width = w_out.shape[1]
    slab = rows // n_tp * SLOTS
    scratch = [
        pltpu.VMEM(tokens.shape, bf16),
        pltpu.VMEM(norm_gain.shape, f32),
        pltpu.VMEM(w_query.shape, bf16),
        pltpu.VMEM(w_keyval.shape, bf16),
        pltpu.VMEM(w_out.shape, bf16),
        pltpu.VMEM(key_cache.shape, bf16),
        pltpu.VMEM(value_cache.shape, bf16),
        pltpu.SMEM((requests,), jnp.int32),
        pltpu.SMEM((spans_here,), jnp.int32),
        pltpu.SMEM((spans_here,), jnp.int32),
        pltpu.SMEM((requests,), jnp.int32),
        pltpu.SMEM((spans_here,), jnp.int32),
        pltpu.SMEM((spans_here,), jnp.int32),
        pltpu.SMEM((spans_here,), jnp.int32),
        pltpu.VMEM((rows * SLOTS, head_dim), f32),
        pltpu.VMEM((n_mem, tile, head_dim), f32),
        pltpu.VMEM((2, tile, head_dim), f32),
        pltpu.VMEM((requests * SLOTS, spans_here * SLOTS), bf16),
        pltpu.VMEM((spans_here, head_dim), jnp.int32),
        pltpu.VMEM((spans_here, head_dim), f32),
        pltpu.VMEM((requests, SLOTS, head_dim), bf16),
        pltpu.VMEM((spans_here, SLOTS, head_dim), f32),
        pltpu.VMEM((spans_here, head_dim), f32),
        pltpu.VMEM((spans_here, head_dim), f32),
        pltpu.VMEM((spans_here, head_dim), f32),
        pltpu.VMEM((spans_here * SLOTS, head_dim), bf16),
        pltpu.VMEM((owners, tile, head_dim), bf16),
        pltpu.VMEM((owners, tile, head_dim), bf16),
        pltpu.VMEM((own_rows, owners, head_dim), f32),
        pltpu.VMEM((own_rows, owners, head_dim), f32),
        pltpu.VMEM((rows, SLOTS, head_dim), bf16),
        pltpu.VMEM((rows * SLOTS, head_dim), f32),
        pltpu.VMEM((rows * SLOTS, head_dim), f32),
        pltpu.VMEM((n_tp, slab, head_dim), bf16),
        pltpu.VMEM((n_tp, slab, head_dim), bf16),
        pltpu.VMEM((n_tp, slab, head_dim), bf16),
        pltpu.SemaphoreType.DMA((16,)),
        pltpu.SemaphoreType.DMA((6,)),
        pltpu.SemaphoreType.DMA((6,)),
    ]
    return pl.pallas_call(
        functools.partial(kernel, n_grp, n_tp, n_mem),
        out_shape=jax.ShapeDtypeStruct((rows, out_width), bf16),
        in_specs=[pl.BlockSpec(memory_space=HBM)] * len(args),
        out_specs=pl.BlockSpec(memory_space=pltpu.VMEM),
        scratch_shapes=scratch,
        compiler_params=pltpu.CompilerParams(
            collective_id=0, has_side_effects=True, vmem_limit_bytes=64 * 1024 * 1024
        ),
        cost_estimate=pl.CostEstimate(flops=200_000_000, bytes_accessed=12_600_000, transcendentals=100_000),
    )(*args)


def solution(mesh):
    placed = (
        P("grp", "mem"),
        P("mem"),
        P("mem", "tp"),
        P(None, "mem", "tp"),
        P("tp", "mem"),
        P("tp", ("grp", "mem"), None, None),
        P("tp", ("grp", "mem"), None, None),
        P(),
        P(("grp", "mem")),
        P(("grp", "mem")),
        P(),
    )
    body = functools.partial(per_device, mesh.shape["grp"], mesh.shape["tp"], mesh.shape["mem"])
    return jax.shard_map(body, mesh=mesh, in_specs=placed, out_specs=P("grp", "mem"), check_vma=False)
```

```python
import functools

import jax
import jax.numpy as jnp
from jax import lax
from jax.experimental import pallas as pl
from jax.experimental.pallas import tpu as pltpu
from jax.sharding import PartitionSpec as P

MESH = pl.DeviceIdType.MESH
HBM = pltpu.MemorySpace.HBM
D = 12288
epsilon = 1e-05
rope_base = 1000000.0
very_low = -1e30
SLOTS = 16
f32 = jnp.float32
bf16 = jnp.bfloat16


def chunks(count, width, body):
    def step(b, carry):
        stores = [body(b * width + u) for u in range(width)]
        for store in stores:
            store()
        return carry

    lax.fori_loop(0, count // width, step, 0)


def hops(d, size):
    return min(d, size - d)


def far_first(size, each):
    chips = sorted(range(size), key=lambda d: -hops(d, size))
    return [d * each + c for d in chips for c in range(each)]


def iota(shape, dim):
    return lax.broadcasted_iota(jnp.int32, shape, dim)


def kernel(
    n_grp, n_tp, n_mem,
    tokens, gain, w_query, w_keyval, w_out, key_cache, value_cache, req_len, span_request, span_first, new_slot,
    out,
    tok_v, gain_v, wq_v, wkv_v, wo_v, key_v, val_v, len_s, req_s, first_s, slot_s, lim_s, new_s, own_s,
    part, part_in, table, pick, col_req, leader, qkv, scores, maxima, tops, stat_top, spans,
    soft_out, soft_in, stat, blend, att, att_wide, wide_rows, sums, sums_in, done, local_sem, send_sem, recv_sem,
):
    g, t, m = lax.axis_index("grp"), lax.axis_index("tp"), lax.axis_index("mem")
    owners = n_grp * n_mem
    owner = g * n_mem + m
    rows, width = tok_v.shape
    requests = len_s.shape[0]
    own_rows = rows // n_mem
    out_rows = rows // n_tp
    spans_here = req_s.shape[0]
    q_cols = wq_v.shape[1]
    head_dim = key_v.shape[3]
    heads = q_cols // head_dim
    tile = own_rows * SLOTS
    k_chunks = 6
    k_step = width // k_chunks

    small = [
        pltpu.make_async_copy(req_len, len_s, local_sem.at[0]),
        pltpu.make_async_copy(span_request, req_s, local_sem.at[1]),
        pltpu.make_async_copy(span_first, first_s, local_sem.at[2]),
        pltpu.make_async_copy(new_slot, slot_s, local_sem.at[3]),
    ]
    tok_copy = pltpu.make_async_copy(tokens, tok_v, local_sem.at[4])
    gain_copy = pltpu.make_async_copy(gain, gain_v, local_sem.at[5])
    wkv_copy = pltpu.make_async_copy(w_keyval, wkv_v, local_sem.at[6])
    key_copy = pltpu.make_async_copy(key_cache, key_v, local_sem.at[7])
    val_copy = pltpu.make_async_copy(value_cache, val_v, local_sem.at[8])
    out_copy = pltpu.make_async_copy(w_out, wo_v, local_sem.at[9])
    wq_copies = [
        pltpu.make_async_copy(
            w_query.at[pl.ds(c * k_step, k_step), :], wq_v.at[pl.ds(c * k_step, k_step), :], local_sem.at[10 + c]
        )
        for c in range(k_chunks)
    ]
    tok_copy.start()
    gain_copy.start()
    for copy in wq_copies + [wkv_copy] + small:
        copy.start()

    barrier = pltpu.get_barrier_semaphore()

    def owner_at(dg, dm):
        to_g = lax.rem(g + dg, n_grp)
        to_m = lax.rem(m // 2 + dm // 2, n_mem // 2) * 2 + lax.rem(m + dm, 2)
        return to_g * n_mem + to_m, {"grp": to_g, "mem": to_m}

    mem_order = far_first(n_mem // 2, 2)
    for dg in far_first(n_grp, 1):
        for dm in mem_order:
            if dg or dm:
                pl.semaphore_signal(barrier, inc=1, device_id=owner_at(dg, dm)[1], device_id_type=MESH)
    tp_order = [d for d in far_first(n_tp, 1) if d]
    for d in tp_order:
        pl.semaphore_signal(barrier, inc=1, device_id={"tp": lax.rem(t + d, n_tp)}, device_id_type=MESH)
    mem_order = [d for d in mem_order if d]
    owner_order = sorted(
        [(dg, dm) for dg in range(n_grp) for dm in range(n_mem) if dg or dm],
        key=lambda d: -hops(d[0], n_grp) - hops(d[1] // 2, n_mem // 2),
    )

    tok_copy.wait()
    gain_copy.wait()
    wide = tok_v[...].astype(f32)
    square = jnp.sum(wide * wide, axis=1, keepdims=True)
    scaled = (wide * gain_v[...].reshape(1, width)).astype(bf16)
    projected = jnp.zeros((rows, q_cols), f32)
    for c in range(k_chunks):
        wq_copies[c].wait()
        projected += jnp.dot(
            scaled[:, c * k_step : (c + 1) * k_step],
            wq_v[c * k_step : (c + 1) * k_step, :],
            preferred_element_type=f32,
        )
    wkv_copy.wait()
    for copy in (key_copy, val_copy, out_copy):
        copy.start()
    new_part = [jnp.dot(scaled, wkv_v[i], preferred_element_type=f32) for i in range(2)]
    pieces = [projected[:, h * head_dim : (h + 1) * head_dim] for h in range(heads)] + new_part
    pieces += [jnp.broadcast_to(square, (rows, head_dim))]
    pieces += [jnp.zeros((rows, head_dim), f32)] * (SLOTS - len(pieces))
    for h, piece in enumerate(pieces):
        part[pl.ds(h, rows, stride=SLOTS), :] = piece

    pl.semaphore_wait(barrier, owners - 1 + n_tp - 1)

    for d in mem_order:
        to = owner_at(0, d)[1]["mem"]
        pltpu.make_async_remote_copy(
            src_ref=part.at[pl.ds(pl.multiple_of(to * tile, tile), tile), :],
            dst_ref=part_in.at[m],
            send_sem=send_sem.at[0],
            recv_sem=recv_sem.at[0],
            device_id={"mem": to},
            device_id_type=MESH,
        ).start()
    part_in[m] = part[pl.ds(pl.multiple_of(m * tile, tile), tile), :]

    for copy in small:
        copy.wait()
    lane = iota((1, head_dim), 1)
    own_len = [len_s[g * rows + m * own_rows + i] for i in range(own_rows)]
    position = jnp.where(iota((tile, 1), 0) < SLOTS, own_len[0], own_len[1]).astype(f32)
    half = head_dim // 2
    power = (lax.rem(lane, half).astype(f32) * 2.0) / head_dim
    frequency = jnp.exp(power * -jnp.log(jnp.full((1, head_dim), rope_base, f32)))
    angles = position * frequency
    slot_row = lax.rem(iota((tile, head_dim), 0), SLOTS)
    turned = slot_row < heads + 1
    cosine = jnp.where(turned, jnp.cos(angles), 1.0)
    sine = jnp.where(turned, jnp.sin(angles), 0.0)
    table[0] = cosine
    table[1] = jnp.where(lane < half, -sine, sine)

    def span_scalars(c, carry):
        r = jnp.maximum(req_s[c], 0)
        limit = jnp.where(req_s[c] >= 0, len_s[r] - first_s[c], -1)
        lim_s[c] = limit
        new_s[c] = jnp.where(slot_s[r] == owner * spans_here + c, limit, -1)
        own_s[c] = r
        return carry

    lax.fori_loop(0, spans_here, span_scalars, 0)

    flat = spans_here * SLOTS
    column = iota((1, flat), 1)
    target = jnp.zeros((1, flat), jnp.int32)
    in_rows = iota((spans_here, head_dim), 0)
    by_row = jnp.zeros((spans_here, head_dim), jnp.int32)
    for c in range(spans_here):
        target = jnp.where(column // SLOTS == c, req_s[c] * SLOTS, target)
        by_row = jnp.where(in_rows == c, req_s[c], by_row)
    target = target + lax.rem(column, SLOTS)
    col_req[...] = by_row
    first_of = jnp.ones((spans_here, head_dim), f32)
    for c in range(spans_here):
        first_of = jnp.where((by_row == req_s[c]) & (in_rows > c), 0.0, first_of)
    leader[...] = first_of

    pick_rows = 128

    def fill_pick(b, carry):
        at = pl.multiple_of(b * pick_rows, pick_rows)
        row = iota((pick_rows, flat), 0) + at
        pick[pl.ds(at, pick_rows), :] = jnp.where(row == target, 1.0, 0.0).astype(bf16)
        return carry

    lax.fori_loop(0, requests * SLOTS // pick_rows, fill_pick, 0)

    def wait_for(buffer, amount, kind):
        ref = buffer.at[pl.ds(0, amount)]
        pltpu.make_async_copy(ref, ref, kind).wait()

    wait_for(part_in, n_mem - 1, recv_sem.at[0])
    total = part_in[0]
    for i in range(1, n_mem):
        total = total + part_in[i]
    normed = []
    for i in range(own_rows):
        block = total[i * SLOTS : (i + 1) * SLOTS]
        root_mean = jnp.sqrt(block[heads + 2 : heads + 3] / D + epsilon)
        normed.append(block / root_mean)
    normed = jnp.concatenate(normed, axis=0)
    finished = normed * table[0] + pltpu.roll(normed, half, axis=1) * table[1]
    qkv[pl.ds(owner * own_rows, own_rows)] = finished.astype(bf16).reshape(own_rows, SLOTS, head_dim)

    here = pl.ds(owner * own_rows, own_rows)
    for d in owner_order:
        pltpu.make_async_remote_copy(
            src_ref=qkv.at[here],
            dst_ref=qkv.at[here],
            send_sem=send_sem.at[1],
            recv_sem=recv_sem.at[1],
            device_id=owner_at(*d)[1],
            device_id_type=MESH,
        ).start()
    key_copy.wait()
    val_copy.wait()
    wait_for(qkv, (owners - 1) * own_rows, recv_sem.at[1])

    scale = head_dim**-0.5
    head = iota((SLOTS, head_dim), 0)
    lanes = iota((SLOTS, head_dim), 1)
    diagonal = lanes == head
    repeated = lax.rem(lanes, SLOTS) == head

    def score(c):
        tile_c = qkv[own_s[c]]
        raw = lax.dot_general(tile_c, key_v[0, c], (((1,), (1,)), ((), ())), preferred_element_type=f32)
        tile_wide = tile_c.astype(f32)
        fresh = jnp.sum(tile_wide * tile_wide[heads : heads + 1], axis=1, keepdims=True)
        shown = jnp.where(lanes <= lim_s[c], jnp.where(lanes == new_s[c], fresh, raw) * scale, very_low)
        top = jnp.max(shown, axis=1, keepdims=True)
        top_row = jnp.sum(jnp.where(repeated, top, 0.0), axis=0, keepdims=True)

        def store():
            scores[c] = shown
            maxima[pl.ds(c, 1), :] = top_row

        return store

    chunks(spans_here, 32, score)
    every = maxima[...]
    request_top = every
    for c in range(spans_here):
        request_top = jnp.maximum(request_top, jnp.where(col_req[...] == req_s[c], every[c : c + 1], very_low))
    tops[...] = request_top
    group = lane // SLOTS
    high = request_top.astype(bf16).astype(f32)
    middle = (request_top - high).astype(bf16).astype(f32)
    low = request_top - high - middle
    told = jnp.where(group == 2, high, jnp.where(group == 3, middle, jnp.where(group == 4, low, 0.0)))
    stat_top[...] = told * leader[...]

    def weigh(c):
        tile_c = qkv[own_s[c]]
        top = jnp.sum(jnp.where(diagonal, tops[pl.ds(c, 1), :], 0.0), axis=1, keepdims=True)
        weights = jnp.exp(scores[c] - top)
        total = jnp.sum(weights, axis=1, keepdims=True)
        is_new = lanes == new_s[c]
        fresh = jnp.sum(jnp.where(is_new, weights, 0.0), axis=1, keepdims=True)
        rounded = jnp.where(is_new, 0.0, weights).astype(bf16)
        value = jnp.dot(rounded, val_v[0, c], preferred_element_type=f32)
        value += fresh.astype(bf16).astype(f32) * tile_c[heads + 1 : heads + 2].astype(f32)
        total_row = jnp.sum(jnp.where(repeated, total, 0.0), axis=0, keepdims=True)
        total_high = total_row.astype(bf16).astype(f32)
        row = jnp.where(group == 0, total_high, jnp.where(group == 1, total_row - total_high, stat_top[pl.ds(c, 1), :]))
        result = jnp.where(head == heads, row, value).astype(bf16)

        def store():
            spans[pl.ds(pl.multiple_of(c * SLOTS, SLOTS), SLOTS), :] = result

        return store

    chunks(spans_here, 32, weigh)

    for dg in far_first(n_grp, 1):
        group_of = lax.rem(g + dg, n_grp)
        at = pl.multiple_of(group_of * n_mem * tile, n_mem * tile)
        summed = jnp.dot(pick[pl.ds(at, n_mem * tile), :], spans[...], preferred_element_type=f32)
        soft_out[pl.ds(group_of * n_mem, n_mem)] = summed.astype(bf16).reshape(n_mem, tile, head_dim)
        for d in mem_order if dg == 0 else mem_order + [0]:
            place, device = owner_at(dg, d)
            pltpu.make_async_remote_copy(
                src_ref=soft_out.at[place],
                dst_ref=soft_in.at[owner],
                send_sem=send_sem.at[2],
                recv_sem=recv_sem.at[2],
                device_id=device,
                device_id_type=MESH,
            ).start()
    soft_in[owner] = soft_out[owner]
    wait_for(soft_in, owners - 1, recv_sem.at[2])

    def read_stat(s):
        lower = [soft_in[s, i * SLOTS : (i + 1) * SLOTS, :].astype(f32)[heads : heads + 1] for i in range(own_rows)]

        def store():
            for i in range(own_rows):
                stat[i, pl.ds(s, 1), :] = lower[i]

        return store

    chunks(owners, 8, read_stat)
    for i in range(own_rows):
        said = stat[i]

        def lanes_from(k):
            return pltpu.roll(said, head_dim - k * SLOTS, axis=1)

        total = said + lanes_from(1)
        top = jnp.where(total > 0.0, lanes_from(2) + lanes_from(3) + lanes_from(4), very_low)
        factor = jnp.exp(top - jnp.max(top, axis=0, keepdims=True))
        blend[i] = factor / jnp.sum(factor * total, axis=0, keepdims=True)

    def join(b, carry):
        sums_now = list(carry)
        for u in range(8):
            s = b * 8 + u
            for i in range(own_rows):
                factor = jnp.sum(jnp.where(diagonal, blend[i, pl.ds(s, 1), :], 0.0), axis=1, keepdims=True)
                sums_now[i] = sums_now[i] + factor * soft_in[s, i * SLOTS : (i + 1) * SLOTS, :].astype(f32)
        return tuple(sums_now)

    joined = lax.fori_loop(0, owners // 8, join, tuple(jnp.zeros((SLOTS, head_dim), f32) for _ in range(own_rows)))
    for i in range(own_rows):
        att[m * own_rows + i] = joined[i].astype(bf16)

    here = pl.ds(m * own_rows, own_rows)
    for d in mem_order:
        pltpu.make_async_remote_copy(
            src_ref=att.at[here],
            dst_ref=att.at[here],
            send_sem=send_sem.at[3],
            recv_sem=recv_sem.at[3],
            device_id={"mem": owner_at(0, d)[1]["mem"]},
            device_id_type=MESH,
        ).start()
    out_copy.wait()
    wait_for(att, (n_mem - 1) * own_rows, recv_sem.at[3])

    out_cols = wo_v.shape[1] // head_dim
    slab = out_rows * SLOTS
    for n in range(out_cols, SLOTS):
        wide_rows[pl.ds(n, rows, stride=SLOTS), :] = jnp.zeros((rows, head_dim), f32)
    att_wide[...] = att[...].astype(f32).reshape(rows * SLOTS, head_dim)
    left = jnp.concatenate([att_wide[pl.ds(h, rows, stride=SLOTS), :] for h in range(heads)], axis=1).astype(bf16)
    product = jnp.dot(left, wo_v[...], preferred_element_type=f32)
    for n in range(out_cols):
        wide_rows[pl.ds(n, rows, stride=SLOTS), :] = product[:, n * head_dim : (n + 1) * head_dim]
    sums[...] = wide_rows[...].astype(bf16).reshape(n_tp, slab, head_dim)

    for d in tp_order:
        to = lax.rem(t + d, n_tp)
        pltpu.make_async_remote_copy(
            src_ref=sums.at[to],
            dst_ref=sums_in.at[t],
            send_sem=send_sem.at[4],
            recv_sem=recv_sem.at[4],
            device_id={"tp": to},
            device_id_type=MESH,
        ).start()
    sums_in[t] = sums[t]
    wait_for(sums_in, n_tp - 1, recv_sem.at[4])
    total = sums_in[0].astype(f32)
    for i in range(1, n_tp):
        total = total + sums_in[i].astype(f32)
    done[t] = total.astype(bf16)
    for d in tp_order:
        pltpu.make_async_remote_copy(
            src_ref=done.at[t],
            dst_ref=done.at[t],
            send_sem=send_sem.at[5],
            recv_sem=recv_sem.at[5],
            device_id={"tp": lax.rem(t + d, n_tp)},
            device_id_type=MESH,
        ).start()
    wait_for(done, n_tp - 1, recv_sem.at[5])
    wide_rows[...] = done[...].astype(f32).reshape(rows * SLOTS, head_dim)
    for n in range(out_cols):
        out[:, n * head_dim : (n + 1) * head_dim] = wide_rows[pl.ds(n, rows, stride=SLOTS), :].astype(bf16)

    wait_for(part, (n_mem - 1) * tile, send_sem.at[0])
    wait_for(qkv, (owners - 1) * own_rows, send_sem.at[1])
    wait_for(soft_out, owners - 1, send_sem.at[2])
    wait_for(att, (n_mem - 1) * own_rows, send_sem.at[3])
    wait_for(sums, n_tp - 1, send_sem.at[4])
    wait_for(done, n_tp - 1, send_sem.at[5])


def per_device(n_grp, n_tp, n_mem, *args):
    tokens, norm_gain, w_query, w_keyval, w_out, key_cache, value_cache, req_len, span_request, _, _ = args
    rows, width = tokens.shape
    q_cols = w_query.shape[1]
    head_dim = key_cache.shape[3]
    spans_here = span_request.shape[0]
    requests = req_len.shape[0]
    owners = n_grp * n_mem
    own_rows = rows // n_mem
    tile = own_rows * SLOTS
    out_width = w_out.shape[1]
    slab = rows // n_tp * SLOTS
    scratch = [
        pltpu.VMEM(tokens.shape, bf16),
        pltpu.VMEM(norm_gain.shape, f32),
        pltpu.VMEM(w_query.shape, bf16),
        pltpu.VMEM(w_keyval.shape, bf16),
        pltpu.VMEM(w_out.shape, bf16),
        pltpu.VMEM(key_cache.shape, bf16),
        pltpu.VMEM(value_cache.shape, bf16),
        pltpu.SMEM((requests,), jnp.int32),
        pltpu.SMEM((spans_here,), jnp.int32),
        pltpu.SMEM((spans_here,), jnp.int32),
        pltpu.SMEM((requests,), jnp.int32),
        pltpu.SMEM((spans_here,), jnp.int32),
        pltpu.SMEM((spans_here,), jnp.int32),
        pltpu.SMEM((spans_here,), jnp.int32),
        pltpu.VMEM((rows * SLOTS, head_dim), f32),
        pltpu.VMEM((n_mem, tile, head_dim), f32),
        pltpu.VMEM((2, tile, head_dim), f32),
        pltpu.VMEM((requests * SLOTS, spans_here * SLOTS), bf16),
        pltpu.VMEM((spans_here, head_dim), jnp.int32),
        pltpu.VMEM((spans_here, head_dim), f32),
        pltpu.VMEM((requests, SLOTS, head_dim), bf16),
        pltpu.VMEM((spans_here, SLOTS, head_dim), f32),
        pltpu.VMEM((spans_here, head_dim), f32),
        pltpu.VMEM((spans_here, head_dim), f32),
        pltpu.VMEM((spans_here, head_dim), f32),
        pltpu.VMEM((spans_here * SLOTS, head_dim), bf16),
        pltpu.VMEM((owners, tile, head_dim), bf16),
        pltpu.VMEM((owners, tile, head_dim), bf16),
        pltpu.VMEM((own_rows, owners, head_dim), f32),
        pltpu.VMEM((own_rows, owners, head_dim), f32),
        pltpu.VMEM((rows, SLOTS, head_dim), bf16),
        pltpu.VMEM((rows * SLOTS, head_dim), f32),
        pltpu.VMEM((rows * SLOTS, head_dim), f32),
        pltpu.VMEM((n_tp, slab, head_dim), bf16),
        pltpu.VMEM((n_tp, slab, head_dim), bf16),
        pltpu.VMEM((n_tp, slab, head_dim), bf16),
        pltpu.SemaphoreType.DMA((16,)),
        pltpu.SemaphoreType.DMA((6,)),
        pltpu.SemaphoreType.DMA((6,)),
    ]
    return pl.pallas_call(
        functools.partial(kernel, n_grp, n_tp, n_mem),
        out_shape=pltpu.VMEM((rows, out_width), bf16),
        in_specs=[pl.BlockSpec(memory_space=HBM)] * len(args),
        out_specs=pl.BlockSpec(memory_space=pltpu.VMEM),
        scratch_shapes=scratch,
        compiler_params=pltpu.CompilerParams(
            collective_id=0, has_side_effects=True, vmem_limit_bytes=48 * 1024 * 1024
        ),
        cost_estimate=pl.CostEstimate(flops=200_000_000, bytes_accessed=12_600_000, transcendentals=100_000),
    )(*[pltpu.with_memory_space_constraint(a, HBM) for a in args])


def solution(mesh):
    placed = (
        P("grp", "mem"),
        P("mem"),
        P("mem", "tp"),
        P(None, "mem", "tp"),
        P("tp", "mem"),
        P("tp", ("grp", "mem"), None, None),
        P("tp", ("grp", "mem"), None, None),
        P(),
        P(("grp", "mem")),
        P(("grp", "mem")),
        P(),
    )
    body = functools.partial(per_device, mesh.shape["grp"], mesh.shape["tp"], mesh.shape["mem"])
    return jax.shard_map(body, mesh=mesh, in_specs=placed, out_specs=P("grp", "mem"), check_vma=False)
```

```python
import functools

import jax
import jax.numpy as jnp
from jax import lax
from jax.experimental import pallas as pl
from jax.experimental.pallas import tpu as pltpu
from jax.sharding import PartitionSpec as P

MESH = pl.DeviceIdType.MESH
HBM = pltpu.MemorySpace.HBM
D = 12288
epsilon = 1e-05
rope_base = 1000000.0
very_low = -1e30
SLOTS = 16
PAIR = 24
f32 = jnp.float32
bf16 = jnp.bfloat16


def chunks(count, width, body):
    def step(b, carry):
        stores = [body(b * width + u) for u in range(width)]
        for store in stores:
            store()
        return carry

    lax.fori_loop(0, count // width, step, 0)


def hops(d, size):
    return min(d, size - d)


def far_first(size, each):
    chips = sorted(range(size), key=lambda d: -hops(d, size))
    return [d * each + c for d in chips for c in range(each)]


def iota(shape, dim):
    return lax.broadcasted_iota(jnp.int32, shape, dim)


def kernel(
    n_grp, n_tp, n_mem,
    tokens, gain, w_query, w_keyval, w_out, key_cache, value_cache, req_len, span_request, span_first, new_slot,
    out,
    tok_v, gain_v, wq_v, wkv_v, wo_v, key_v, val_v, len_s, req_s, first_s, lim_s, pair_s, odd_s,
    part, part_in, table, pick, pick_stat, col_req, leader, qrows, newest, new_score, values, maxima, totals, factors, spans,
    soft_out, soft_in, stat_out, stat_in, blend, att, att_wide, wide_rows, sums, sums_in, done, local_sem, send_sem, recv_sem,
):
    g, t, m = lax.axis_index("grp"), lax.axis_index("tp"), lax.axis_index("mem")
    owners = n_grp * n_mem
    owner = g * n_mem + m
    rows, width = tok_v.shape
    requests = len_s.shape[0]
    own_rows = rows // n_mem
    out_rows = rows // n_tp
    spans_here = req_s.shape[0]
    q_cols = wq_v.shape[1]
    head_dim = key_v.shape[3]
    heads = q_cols // head_dim
    tile = own_rows * SLOTS
    k_chunks = 6
    k_step = width // k_chunks

    small = [
        pltpu.make_async_copy(req_len, len_s, local_sem.at[0]),
        pltpu.make_async_copy(span_request, req_s, local_sem.at[1]),
        pltpu.make_async_copy(span_first, first_s, local_sem.at[2]),
    ]
    tok_copy = pltpu.make_async_copy(tokens, tok_v, local_sem.at[4])
    gain_copy = pltpu.make_async_copy(gain, gain_v, local_sem.at[5])
    wkv_copy = pltpu.make_async_copy(w_keyval, wkv_v, local_sem.at[6])
    key_copy = pltpu.make_async_copy(key_cache, key_v, local_sem.at[7])
    val_copy = pltpu.make_async_copy(value_cache, val_v, local_sem.at[8])
    out_copy = pltpu.make_async_copy(w_out, wo_v, local_sem.at[9])
    wq_copies = [
        pltpu.make_async_copy(
            w_query.at[pl.ds(c * k_step, k_step), :], wq_v.at[pl.ds(c * k_step, k_step), :], local_sem.at[10 + c]
        )
        for c in range(k_chunks)
    ]
    tok_copy.start()
    gain_copy.start()
    for copy in wq_copies + [wkv_copy] + small:
        copy.start()

    barrier = pltpu.get_barrier_semaphore()

    def owner_at(dg, dm):
        to_g = lax.rem(g + dg, n_grp)
        to_m = lax.rem(m // 2 + dm // 2, n_mem // 2) * 2 + lax.rem(m + dm, 2)
        return to_g * n_mem + to_m, {"grp": to_g, "mem": to_m}

    mem_order = far_first(n_mem // 2, 2)
    for dg in far_first(n_grp, 1):
        for dm in mem_order:
            if dg or dm:
                pl.semaphore_signal(barrier, inc=1, device_id=owner_at(dg, dm)[1], device_id_type=MESH)
    tp_order = [d for d in far_first(n_tp, 1) if d]
    for d in tp_order:
        pl.semaphore_signal(barrier, inc=1, device_id={"tp": lax.rem(t + d, n_tp)}, device_id_type=MESH)
    mem_order = [d for d in mem_order if d]
    owner_order = sorted(
        [(dg, dm) for dg in range(n_grp) for dm in range(n_mem) if dg or dm],
        key=lambda d: -hops(d[0], n_grp) - hops(d[1] // 2, n_mem // 2),
    )

    tok_copy.wait()
    gain_copy.wait()
    wide = tok_v[...].astype(f32)
    square = jnp.sum(wide * wide, axis=1, keepdims=True)
    scaled = (wide * gain_v[...].reshape(1, width)).astype(bf16)
    projected = jnp.zeros((rows, q_cols), f32)
    for c in range(k_chunks):
        wq_copies[c].wait()
        projected += jnp.dot(
            scaled[:, c * k_step : (c + 1) * k_step],
            wq_v[c * k_step : (c + 1) * k_step, :],
            preferred_element_type=f32,
        )
    wkv_copy.wait()
    for copy in (key_copy, val_copy, out_copy):
        copy.start()
    new_part = [jnp.dot(scaled, wkv_v[i], preferred_element_type=f32) for i in range(2)]
    pieces = [projected[:, h * head_dim : (h + 1) * head_dim] for h in range(heads)] + new_part
    pieces += [jnp.broadcast_to(square, (rows, head_dim))]
    pieces += [jnp.zeros((rows, head_dim), f32)] * (SLOTS - len(pieces))
    for h, piece in enumerate(pieces):
        part[pl.ds(h, rows, stride=SLOTS), :] = piece

    pl.semaphore_wait(barrier, owners - 1 + n_tp - 1)

    for d in mem_order:
        to = owner_at(0, d)[1]["mem"]
        pltpu.make_async_remote_copy(
            src_ref=part.at[pl.ds(pl.multiple_of(to * tile, tile), tile), :],
            dst_ref=part_in.at[m],
            send_sem=send_sem.at[0],
            recv_sem=recv_sem.at[0],
            device_id={"mem": to},
            device_id_type=MESH,
        ).start()
    part_in[m] = part[pl.ds(pl.multiple_of(m * tile, tile), tile), :]

    for copy in small:
        copy.wait()
    lane = iota((1, head_dim), 1)
    own_len = [len_s[g * rows + m * own_rows + i] for i in range(own_rows)]
    position = jnp.where(iota((tile, 1), 0) < SLOTS, own_len[0], own_len[1]).astype(f32)
    half = head_dim // 2
    power = (lax.rem(lane, half).astype(f32) * 2.0) / head_dim
    frequency = jnp.exp(power * -jnp.log(jnp.full((1, head_dim), rope_base, f32)))
    angles = position * frequency
    slot_row = lax.rem(iota((tile, head_dim), 0), SLOTS)
    turned = slot_row < heads + 1
    cosine = jnp.where(turned, jnp.cos(angles), 1.0)
    sine = jnp.where(turned, jnp.sin(angles), 0.0)
    table[0] = cosine
    table[1] = jnp.where(lane < half, -sine, sine)

    def span_scalars(c, carry):
        r = jnp.maximum(req_s[c], 0)
        lim_s[c] = jnp.where(req_s[c] >= 0, len_s[r] - first_s[c], 0)
        pair_s[c] = r // 2
        odd_s[c] = lax.rem(r, 2)
        return carry

    lax.fori_loop(0, spans_here, span_scalars, 0)

    flat = spans_here * SLOTS
    column = iota((1, flat), 1)
    in_rows = iota((spans_here, head_dim), 0)
    by_column = jnp.zeros((1, flat), jnp.int32)
    by_row = jnp.zeros((spans_here, head_dim), jnp.int32)
    stat_column = iota((1, 6 * spans_here), 1)
    by_stat = jnp.zeros((1, 6 * spans_here), jnp.int32)
    for c in range(spans_here):
        by_column = jnp.where(column // SLOTS == c, req_s[c], by_column)
        by_row = jnp.where(in_rows == c, req_s[c], by_row)
        by_stat = jnp.where(lax.rem(stat_column, spans_here) == c, req_s[c], by_stat)
    col_req[...] = by_row
    first_of = jnp.ones((spans_here, head_dim), f32)
    for c in range(spans_here):
        first_of = jnp.where((by_row == req_s[c]) & (in_rows > c), 0.0, first_of)
    leader[...] = first_of
    row_in = lax.rem(column, SLOTS)
    nowhere = -requests * SLOTS
    of_first = jnp.where(row_in < 12, row_in, nowhere)
    of_second = jnp.where(row_in < 8, row_in + 16, jnp.where(row_in < 12, nowhere, row_in))
    target = (by_column + 2) // 2 * PAIR - PAIR + jnp.where(lax.rem(by_column + 2, 2) == 1, of_second, of_first)
    target = jnp.where(by_column < 0, nowhere, target)
    pick_rows = 96

    def fill_pick(b, carry):
        at = pl.multiple_of(b * pick_rows, pick_rows)
        row = iota((pick_rows, flat), 0) + at
        pick[pl.ds(at, pick_rows), :] = jnp.where(row == target, 1.0, 0.0).astype(bf16)
        return carry

    lax.fori_loop(0, owners * PAIR // pick_rows, fill_pick, 0)
    wanted = iota((owners, 6 * spans_here), 0) * 2 + stat_column // (3 * spans_here)
    pick_stat[...] = jnp.where(wanted == by_stat, 1.0, 0.0).astype(bf16)

    def wait_for(buffer, amount, kind):
        ref = buffer.at[pl.ds(0, amount)]
        pltpu.make_async_copy(ref, ref, kind).wait()

    wait_for(part_in, n_mem - 1, recv_sem.at[0])
    total = part_in[0]
    for i in range(1, n_mem):
        total = total + part_in[i]
    normed = []
    for i in range(own_rows):
        block = total[i * SLOTS : (i + 1) * SLOTS]
        root_mean = jnp.sqrt(block[heads + 2 : heads + 3] / D + epsilon)
        normed.append(block / root_mean)
    normed = jnp.concatenate(normed, axis=0)
    finished = normed * table[0] + pltpu.roll(normed, half, axis=1) * table[1]

    def in_pair(block):
        sub_row = iota((8, head_dim), 0)
        middle = jnp.where(sub_row < 4, block[8:16], pltpu.roll(block[24:32], 4, axis=0))
        return jnp.concatenate([block[0:8], middle, block[16:24]], axis=0)

    qrows[owner] = in_pair(finished).astype(bf16)

    for d in owner_order:
        pltpu.make_async_remote_copy(
            src_ref=qrows.at[owner],
            dst_ref=qrows.at[owner],
            send_sem=send_sem.at[1],
            recv_sem=recv_sem.at[1],
            device_id=owner_at(*d)[1],
            device_id_type=MESH,
        ).start()
    scale = head_dim**-0.5
    rounded = finished.astype(bf16).astype(f32)
    pair_row = iota((PAIR, head_dim), 0)
    pair_lane = iota((PAIR, head_dim), 1)
    of_first = pair_row < 12
    pair_diagonal = pair_lane == jnp.where(of_first, pair_row, jnp.where(pair_row < 16, pair_row + 32, pair_row + 16))
    new_key = jnp.where(of_first, rounded[heads : heads + 1], rounded[SLOTS + heads : SLOTS + heads + 1])
    newest[...] = jnp.where(of_first, rounded[heads + 1 : heads + 2], rounded[SLOTS + heads + 1 : SLOTS + heads + 2])
    fresh = jnp.sum(in_pair(rounded) * new_key, axis=1, keepdims=True) * scale
    new_score[...] = jnp.sum(jnp.where(pair_diagonal, fresh, 0.0), axis=0, keepdims=True)
    key_copy.wait()
    val_copy.wait()
    wait_for(qrows, owners - 1, recv_sem.at[1])

    head = iota((SLOTS, head_dim), 0)
    lanes = iota((SLOTS, head_dim), 1)
    diagonal = lanes == head
    repeated = lax.rem(lanes, SLOTS) == head

    def query_of(c):
        pair = qrows[pair_s[c]].astype(f32)
        rows_of = [jnp.where(odd_s[c] == 1, pair[16:24], pair[0:8]), pair[8:16]]
        return jnp.concatenate(rows_of, axis=0).astype(bf16)

    def soften(c, raw):
        shown = jnp.where(lanes < lim_s[c], raw * scale, very_low)
        top = jnp.max(shown, axis=1, keepdims=True)
        weights = jnp.exp(shown - top)
        total = jnp.sum(weights, axis=1, keepdims=True)
        top_row = jnp.sum(jnp.where(repeated, top, 0.0), axis=0, keepdims=True)
        total_row = jnp.sum(jnp.where(repeated, total, 0.0), axis=0, keepdims=True)
        return weights.astype(bf16), top_row, total_row

    all_spans = range(spans_here)
    raws = [
        lax.dot_general(query_of(c), key_v[0, c], (((1,), (1,)), ((), ())), preferred_element_type=f32)
        for c in all_spans
    ]
    softened = [soften(c, raws[c]) for c in all_spans]
    for c in all_spans:
        values[c] = jnp.dot(softened[c][0], val_v[0, c], preferred_element_type=f32)
    for c in all_spans:
        maxima[c : c + 1, :] = softened[c][1]
        totals[c : c + 1, :] = softened[c][2]
    every = maxima[...]
    request_top = every
    for c in range(spans_here):
        request_top = jnp.maximum(request_top, jnp.where(col_req[...] == req_s[c], every[c : c + 1], very_low))
    factor = jnp.exp(every - request_top)
    factors[...] = factor
    group = lane // SLOTS
    said = jnp.where(lax.rem(group, 2) == 0, request_top * leader[...], factor * totals[...])
    high = said.astype(bf16)
    rest = said - high.astype(f32)
    middle = rest.astype(bf16)
    low = (rest - middle.astype(f32)).astype(bf16)
    thirds = jnp.concatenate([high, middle, low], axis=0).astype(f32)
    first_lanes = jnp.where(group < 2, thirds, 0.0).astype(bf16)
    second_lanes = jnp.where((group == 2) | (group == 3), thirds, 0.0).astype(bf16)
    stats = jnp.dot(
        pick_stat[...], jnp.concatenate([first_lanes, second_lanes], axis=0), preferred_element_type=f32
    )
    stat_out[...] = stats.reshape(owners, 1, head_dim)
    for d in owner_order:
        place, device = owner_at(*d)
        pltpu.make_async_remote_copy(
            src_ref=stat_out.at[place],
            dst_ref=stat_in.at[owner],
            send_sem=send_sem.at[6],
            recv_sem=recv_sem.at[6],
            device_id=device,
            device_id_type=MESH,
        ).start()
    stat_in[owner] = stat_out[owner]

    def weigh(c):
        factor = jnp.sum(jnp.where(diagonal, factors[pl.ds(c, 1), :], 0.0), axis=1, keepdims=True)
        result = (values[c] * factor).astype(bf16)

        def store():
            spans[pl.ds(pl.multiple_of(c * SLOTS, SLOTS), SLOTS), :] = result

        return store

    chunks(spans_here, 32, weigh)

    for dg in far_first(n_grp, 1):
        group_of = lax.rem(g + dg, n_grp)
        at = pl.multiple_of(group_of * n_mem * PAIR, n_mem * PAIR)
        summed = jnp.dot(pick[pl.ds(at, n_mem * PAIR), :], spans[...], preferred_element_type=f32)
        soft_out[pl.ds(group_of * n_mem, n_mem)] = summed.astype(bf16).reshape(n_mem, PAIR, head_dim)
        for d in mem_order if dg == 0 else mem_order + [0]:
            place, device = owner_at(dg, d)
            pltpu.make_async_remote_copy(
                src_ref=soft_out.at[place],
                dst_ref=soft_in.at[owner],
                send_sem=send_sem.at[2],
                recv_sem=recv_sem.at[2],
                device_id=device,
                device_id_type=MESH,
            ).start()
    soft_in[owner] = soft_out[owner]
    wait_for(stat_in, owners - 1, recv_sem.at[6])
    stats = stat_in[...].reshape(owners, head_dim)
    total = pltpu.roll(stats, head_dim - SLOTS, axis=1)
    top = jnp.where(total > 0.0, stats, very_low)
    new_top = new_score[...]
    most = jnp.maximum(jnp.max(top, axis=0, keepdims=True), new_top)
    factor = jnp.exp(top - most)
    new_factor = jnp.exp(new_top - most)
    whole = jnp.sum(factor * total, axis=0, keepdims=True) + new_factor
    blend[...] = factor / whole
    new_share = jnp.sum(jnp.where(pair_diagonal, new_factor / whole, 0.0), axis=1, keepdims=True)
    wait_for(soft_in, owners - 1, recv_sem.at[2])

    def join(b, carry):
        for u in range(16):
            s = b * 16 + u
            share = jnp.sum(jnp.where(pair_diagonal, blend[pl.ds(s, 1), :], 0.0), axis=1, keepdims=True)
            carry = carry + share * soft_in[s].astype(f32)
        return carry

    att[m] = lax.fori_loop(0, owners // 16, join, new_share * newest[...]).astype(bf16)

    for d in mem_order:
        pltpu.make_async_remote_copy(
            src_ref=att.at[m],
            dst_ref=att.at[m],
            send_sem=send_sem.at[3],
            recv_sem=recv_sem.at[3],
            device_id={"mem": owner_at(0, d)[1]["mem"]},
            device_id_type=MESH,
        ).start()
    out_copy.wait()
    wait_for(att, n_mem - 1, recv_sem.at[3])

    out_cols = wo_v.shape[1] // head_dim
    att_wide[...] = att[...].astype(f32).reshape(n_mem * PAIR, head_dim)

    def head_rows(h):
        second = h + 16 if h < 8 else h + 4
        return jnp.concatenate([att_wide[pl.ds(row, n_mem, stride=PAIR), :] for row in (h, second)], axis=0)

    left = jnp.concatenate([head_rows(h) for h in range(heads)], axis=1).astype(bf16)
    product = jnp.dot(left, wo_v[...], preferred_element_type=f32)
    for n in range(out_cols):
        for i in range(own_rows):
            piece = product[i * n_mem : (i + 1) * n_mem, n * head_dim : (n + 1) * head_dim]
            wide_rows[pl.ds(i * out_cols + n, n_mem, stride=own_rows * out_cols), :] = piece
    sums[...] = wide_rows[...].astype(bf16).reshape(n_tp, out_rows * out_cols, head_dim)

    for d in tp_order:
        to = lax.rem(t + d, n_tp)
        pltpu.make_async_remote_copy(
            src_ref=sums.at[to],
            dst_ref=sums_in.at[t],
            send_sem=send_sem.at[4],
            recv_sem=recv_sem.at[4],
            device_id={"tp": to},
            device_id_type=MESH,
        ).start()
    sums_in[t] = sums[t]
    wait_for(sums_in, n_tp - 1, recv_sem.at[4])
    total = sums_in[0].astype(f32)
    for i in range(1, n_tp):
        total = total + sums_in[i].astype(f32)
    done[t] = total.astype(bf16)
    for d in tp_order:
        pltpu.make_async_remote_copy(
            src_ref=done.at[t],
            dst_ref=done.at[t],
            send_sem=send_sem.at[5],
            recv_sem=recv_sem.at[5],
            device_id={"tp": lax.rem(t + d, n_tp)},
            device_id_type=MESH,
        ).start()
    wait_for(done, n_tp - 1, recv_sem.at[5])
    wide_rows[...] = done[...].astype(f32).reshape(rows * out_cols, head_dim)
    for n in range(out_cols):
        out[:, n * head_dim : (n + 1) * head_dim] = wide_rows[pl.ds(n, rows, stride=out_cols), :].astype(bf16)

    wait_for(part, (n_mem - 1) * tile, send_sem.at[0])
    wait_for(qrows, owners - 1, send_sem.at[1])
    wait_for(soft_out, owners - 1, send_sem.at[2])
    wait_for(stat_out, owners - 1, send_sem.at[6])
    wait_for(att, n_mem - 1, send_sem.at[3])
    wait_for(sums, n_tp - 1, send_sem.at[4])
    wait_for(done, n_tp - 1, send_sem.at[5])


def per_device(n_grp, n_tp, n_mem, *args):
    tokens, norm_gain, w_query, w_keyval, w_out, key_cache, value_cache, req_len, span_request, _, _ = args
    rows, width = tokens.shape
    q_cols = w_query.shape[1]
    head_dim = key_cache.shape[3]
    spans_here = span_request.shape[0]
    requests = req_len.shape[0]
    owners = n_grp * n_mem
    own_rows = rows // n_mem
    tile = own_rows * SLOTS
    out_width = w_out.shape[1]
    slab = rows // n_tp * out_width // head_dim
    scratch = [
        pltpu.VMEM(tokens.shape, bf16),
        pltpu.VMEM(norm_gain.shape, f32),
        pltpu.VMEM(w_query.shape, bf16),
        pltpu.VMEM(w_keyval.shape, bf16),
        pltpu.VMEM(w_out.shape, bf16),
        pltpu.VMEM(key_cache.shape, bf16),
        pltpu.VMEM(value_cache.shape, bf16),
        pltpu.SMEM((requests,), jnp.int32),
        pltpu.SMEM((spans_here,), jnp.int32),
        pltpu.SMEM((spans_here,), jnp.int32),
        pltpu.SMEM((spans_here,), jnp.int32),
        pltpu.SMEM((spans_here,), jnp.int32),
        pltpu.SMEM((spans_here,), jnp.int32),
        pltpu.VMEM((rows * SLOTS, head_dim), f32),
        pltpu.VMEM((n_mem, tile, head_dim), f32),
        pltpu.VMEM((2, tile, head_dim), f32),
        pltpu.VMEM((owners * PAIR, spans_here * SLOTS), bf16),
        pltpu.VMEM((owners, 6 * spans_here), bf16),
        pltpu.VMEM((spans_here, head_dim), jnp.int32),
        pltpu.VMEM((spans_here, head_dim), f32),
        pltpu.VMEM((owners, PAIR, head_dim), bf16),
        pltpu.VMEM((PAIR, head_dim), f32),
        pltpu.VMEM((1, head_dim), f32),
        pltpu.VMEM((spans_here, SLOTS, head_dim), f32),
        pltpu.VMEM((spans_here, head_dim), f32),
        pltpu.VMEM((spans_here, head_dim), f32),
        pltpu.VMEM((spans_here, head_dim), f32),
        pltpu.VMEM((spans_here * SLOTS, head_dim), bf16),
        pltpu.VMEM((owners, PAIR, head_dim), bf16),
        pltpu.VMEM((owners, PAIR, head_dim), bf16),
        pltpu.VMEM((owners, 1, head_dim), f32),
        pltpu.VMEM((owners, 1, head_dim), f32),
        pltpu.VMEM((owners, head_dim), f32),
        pltpu.VMEM((n_mem, PAIR, head_dim), bf16),
        pltpu.VMEM((n_mem * PAIR, head_dim), f32),
        pltpu.VMEM((n_tp * slab, head_dim), f32),
        pltpu.VMEM((n_tp, slab, head_dim), bf16),
        pltpu.VMEM((n_tp, slab, head_dim), bf16),
        pltpu.VMEM((n_tp, slab, head_dim), bf16),
        pltpu.SemaphoreType.DMA((16,)),
        pltpu.SemaphoreType.DMA((7,)),
        pltpu.SemaphoreType.DMA((7,)),
    ]
    return pl.pallas_call(
        functools.partial(kernel, n_grp, n_tp, n_mem),
        out_shape=pltpu.VMEM((rows, out_width), bf16),
        in_specs=[pl.BlockSpec(memory_space=HBM)] * len(args),
        out_specs=pl.BlockSpec(memory_space=pltpu.VMEM),
        scratch_shapes=scratch,
        compiler_params=pltpu.CompilerParams(
            collective_id=0, has_side_effects=True, vmem_limit_bytes=48 * 1024 * 1024
        ),
        cost_estimate=pl.CostEstimate(flops=200_000_000, bytes_accessed=12_600_000, transcendentals=100_000),
    )(*[pltpu.with_memory_space_constraint(a, HBM) for a in args])


def solution(mesh):
    placed = (
        P("grp", "mem"),
        P("mem"),
        P("mem", "tp"),
        P(None, "mem", "tp"),
        P("tp", "mem"),
        P("tp", ("grp", "mem"), None, None),
        P("tp", ("grp", "mem"), None, None),
        P(),
        P(("grp", "mem")),
        P(("grp", "mem")),
        P(),
    )
    body = functools.partial(per_device, mesh.shape["grp"], mesh.shape["tp"], mesh.shape["mem"])
    return jax.shard_map(body, mesh=mesh, in_specs=placed, out_specs=P("grp", "mem"), check_vma=False)
```

```python
import functools

import jax
import jax.numpy as jnp
from jax import lax
from jax.experimental import pallas as pl
from jax.experimental.pallas import tpu as pltpu
from jax.sharding import PartitionSpec as P

MESH = pl.DeviceIdType.MESH
HBM = pltpu.MemorySpace.HBM
D = 12288
epsilon = 1e-05
rope_base = 1000000.0
very_low = -1e30
SLOTS = 16
PAIR = 24
f32 = jnp.float32
bf16 = jnp.bfloat16


def chunks(count, width, body):
    def step(b, carry):
        stores = [body(b * width + u) for u in range(width)]
        for store in stores:
            store()
        return carry

    lax.fori_loop(0, count // width, step, 0)


def hops(d, size):
    return min(d, size - d)


def far_first(size, each):
    chips = sorted(range(size), key=lambda d: -hops(d, size))
    return [d * each + c for d in chips for c in range(each)]


def iota(shape, dim):
    return lax.broadcasted_iota(jnp.int32, shape, dim)


def kernel(
    n_grp, n_tp, n_mem,
    tokens, gain, w_query, w_keyval, w_out, key_cache, value_cache, req_len, span_request, span_first, new_slot,
    out,
    tok_v, gain_v, wq_v, wkv_v, wo_v, key_v, val_v, len_s, req_s, first_s, lim_s, pair_s, odd_s,
    part, part_in, table, pick, pick_stat, col_req, leader, qrows, newest, new_score, values, maxima, totals, factors, spans,
    soft_out, soft_in, stat_out, stat_in, blend, att, att_wide, wide_rows, sums, sums_in, done, local_sem, send_sem, recv_sem, tp_sem,
):
    g, t, m = lax.axis_index("grp"), lax.axis_index("tp"), lax.axis_index("mem")
    owners = n_grp * n_mem
    owner = g * n_mem + m
    rows, width = tok_v.shape
    requests = len_s.shape[0]
    own_rows = rows // n_mem
    out_rows = rows // n_tp
    spans_here = req_s.shape[0]
    q_cols = wq_v.shape[1]
    head_dim = key_v.shape[3]
    heads = q_cols // head_dim
    tile = own_rows * SLOTS
    k_chunks = 6
    k_step = width // k_chunks

    small = [
        pltpu.make_async_copy(req_len, len_s, local_sem.at[0]),
        pltpu.make_async_copy(span_request, req_s, local_sem.at[1]),
        pltpu.make_async_copy(span_first, first_s, local_sem.at[2]),
    ]
    tok_copy = pltpu.make_async_copy(tokens, tok_v, local_sem.at[4])
    gain_copy = pltpu.make_async_copy(gain, gain_v, local_sem.at[5])
    wkv_copy = pltpu.make_async_copy(w_keyval, wkv_v, local_sem.at[6])
    key_copy = pltpu.make_async_copy(key_cache, key_v, local_sem.at[7])
    val_copy = pltpu.make_async_copy(value_cache, val_v, local_sem.at[8])
    out_copy = pltpu.make_async_copy(w_out, wo_v, local_sem.at[9])
    wq_copies = [
        pltpu.make_async_copy(
            w_query.at[pl.ds(c * k_step, k_step), :], wq_v.at[pl.ds(c * k_step, k_step), :], local_sem.at[10 + c]
        )
        for c in range(k_chunks)
    ]
    tok_copy.start()
    gain_copy.start()
    for copy in wq_copies + [wkv_copy] + small:
        copy.start()

    barrier = pltpu.get_barrier_semaphore()

    def owner_at(dg, dm):
        to_g = lax.rem(g + dg, n_grp)
        to_m = lax.rem(m // 2 + dm // 2, n_mem // 2) * 2 + lax.rem(m + dm, 2)
        return to_g * n_mem + to_m, {"grp": to_g, "mem": to_m}

    mem_order = [d for d in far_first(n_mem // 2, 2) if d]
    grp_order = [d for d in far_first(n_grp, 1) if d]
    tp_order = [d for d in far_first(n_tp, 1) if d]
    beside = (1, n_tp - 1)
    for d in mem_order:
        pl.semaphore_signal(barrier, inc=1, device_id=owner_at(0, d)[1], device_id_type=MESH)
    for d in grp_order:
        pl.semaphore_signal(barrier, inc=1, device_id=owner_at(d, 0)[1], device_id_type=MESH)

    def tell_tp(semaphore, distances):
        for d in distances:
            pl.semaphore_signal(semaphore, inc=1, device_id={"tp": lax.rem(t + d, n_tp)}, device_id_type=MESH)

    tell_tp(barrier, beside)
    owner_order = sorted(
        [(dg, dm) for dg in range(n_grp) for dm in range(n_mem) if dg or dm],
        key=lambda d: -hops(d[0], n_grp) - hops(d[1] // 2, n_mem // 2),
    )

    tok_copy.wait()
    gain_copy.wait()
    wide = tok_v[...].astype(f32)
    square = jnp.sum(wide * wide, axis=1, keepdims=True)
    scaled = (wide * gain_v[...].reshape(1, width)).astype(bf16)
    projected = jnp.zeros((rows, q_cols), f32)
    for c in range(k_chunks):
        wq_copies[c].wait()
        projected += jnp.dot(
            scaled[:, c * k_step : (c + 1) * k_step],
            wq_v[c * k_step : (c + 1) * k_step, :],
            preferred_element_type=f32,
        )
    wkv_copy.wait()
    for copy in (key_copy, val_copy, out_copy):
        copy.start()
    new_part = [jnp.dot(scaled, wkv_v[i], preferred_element_type=f32) for i in range(2)]
    pieces = [projected[:, h * head_dim : (h + 1) * head_dim] for h in range(heads)] + new_part
    pieces += [jnp.broadcast_to(square, (rows, head_dim))]
    pieces += [jnp.zeros((rows, head_dim), f32)] * (SLOTS - len(pieces))
    for h, piece in enumerate(pieces):
        part[pl.ds(h, rows, stride=SLOTS), :] = piece

    pl.semaphore_wait(barrier, len(mem_order) + len(grp_order) + len(beside))
    tell_tp(tp_sem.at[0], beside)

    for d in mem_order:
        to = owner_at(0, d)[1]["mem"]
        pltpu.make_async_remote_copy(
            src_ref=part.at[pl.ds(pl.multiple_of(to * tile, tile), tile), :],
            dst_ref=part_in.at[m],
            send_sem=send_sem.at[0],
            recv_sem=recv_sem.at[0],
            device_id={"mem": to},
            device_id_type=MESH,
        ).start()
    part_in[m] = part[pl.ds(pl.multiple_of(m * tile, tile), tile), :]

    for copy in small:
        copy.wait()
    lane = iota((1, head_dim), 1)
    own_len = [len_s[g * rows + m * own_rows + i] for i in range(own_rows)]
    position = jnp.where(iota((tile, 1), 0) < SLOTS, own_len[0], own_len[1]).astype(f32)
    half = head_dim // 2
    power = (lax.rem(lane, half).astype(f32) * 2.0) / head_dim
    frequency = jnp.exp(power * -jnp.log(jnp.full((1, head_dim), rope_base, f32)))
    angles = position * frequency
    slot_row = lax.rem(iota((tile, head_dim), 0), SLOTS)
    turned = slot_row < heads + 1
    cosine = jnp.where(turned, jnp.cos(angles), 1.0)
    sine = jnp.where(turned, jnp.sin(angles), 0.0)
    table[0] = cosine
    table[1] = jnp.where(lane < half, -sine, sine)

    def span_scalars(c, carry):
        r = jnp.maximum(req_s[c], 0)
        lim_s[c] = jnp.where(req_s[c] >= 0, len_s[r] - first_s[c], 0)
        pair_s[c] = r // 2
        odd_s[c] = lax.rem(r, 2)
        return carry

    lax.fori_loop(0, spans_here, span_scalars, 0)

    flat = spans_here * SLOTS
    column = iota((1, flat), 1)
    in_rows = iota((spans_here, head_dim), 0)
    by_column = jnp.zeros((1, flat), jnp.int32)
    by_row = jnp.zeros((spans_here, head_dim), jnp.int32)
    stat_column = iota((1, 6 * spans_here), 1)
    by_stat = jnp.zeros((1, 6 * spans_here), jnp.int32)
    for c in range(spans_here):
        by_column = jnp.where(column // SLOTS == c, req_s[c], by_column)
        by_row = jnp.where(in_rows == c, req_s[c], by_row)
        by_stat = jnp.where(lax.rem(stat_column, spans_here) == c, req_s[c], by_stat)
    col_req[...] = by_row
    first_of = jnp.ones((spans_here, head_dim), f32)
    for c in range(spans_here):
        first_of = jnp.where((by_row == req_s[c]) & (in_rows > c), 0.0, first_of)
    leader[...] = first_of
    row_in = lax.rem(column, SLOTS)
    nowhere = -requests * SLOTS
    of_first = jnp.where(row_in < 12, row_in, nowhere)
    of_second = jnp.where(row_in < 8, row_in + 16, jnp.where(row_in < 12, nowhere, row_in))
    target = (by_column + 2) // 2 * PAIR - PAIR + jnp.where(lax.rem(by_column + 2, 2) == 1, of_second, of_first)
    target = jnp.where(by_column < 0, nowhere, target)
    pick_rows = 96

    def fill_pick(b, carry):
        at = pl.multiple_of(b * pick_rows, pick_rows)
        row = iota((pick_rows, flat), 0) + at
        pick[pl.ds(at, pick_rows), :] = jnp.where(row == target, 1.0, 0.0).astype(bf16)
        return carry

    lax.fori_loop(0, owners * PAIR // pick_rows, fill_pick, 0)
    wanted = iota((owners, 6 * spans_here), 0) * 2 + stat_column // (3 * spans_here)
    pick_stat[...] = jnp.where(wanted == by_stat, 1.0, 0.0).astype(bf16)

    def wait_for(buffer, amount, kind):
        ref = buffer.at[pl.ds(0, amount)]
        pltpu.make_async_copy(ref, ref, kind).wait()

    wait_for(part_in, n_mem - 1, recv_sem.at[0])
    total = part_in[0]
    for i in range(1, n_mem):
        total = total + part_in[i]
    normed = []
    for i in range(own_rows):
        block = total[i * SLOTS : (i + 1) * SLOTS]
        root_mean = jnp.sqrt(block[heads + 2 : heads + 3] / D + epsilon)
        normed.append(block / root_mean)
    normed = jnp.concatenate(normed, axis=0)
    finished = normed * table[0] + pltpu.roll(normed, half, axis=1) * table[1]

    def in_pair(block):
        sub_row = iota((8, head_dim), 0)
        middle = jnp.where(sub_row < 4, block[8:16], pltpu.roll(block[24:32], 4, axis=0))
        return jnp.concatenate([block[0:8], middle, block[16:24]], axis=0)

    qrows[owner] = in_pair(finished).astype(bf16)

    for d in owner_order:
        pltpu.make_async_remote_copy(
            src_ref=qrows.at[owner],
            dst_ref=qrows.at[owner],
            send_sem=send_sem.at[1],
            recv_sem=recv_sem.at[1],
            device_id=owner_at(*d)[1],
            device_id_type=MESH,
        ).start()
    pl.semaphore_wait(tp_sem.at[0], len(beside))
    tell_tp(tp_sem.at[1], (2, n_tp - 2))
    scale = head_dim**-0.5
    rounded = finished.astype(bf16).astype(f32)
    pair_row = iota((PAIR, head_dim), 0)
    pair_lane = iota((PAIR, head_dim), 1)
    of_first = pair_row < 12
    pair_diagonal = pair_lane == jnp.where(of_first, pair_row, jnp.where(pair_row < 16, pair_row + 32, pair_row + 16))
    new_key = jnp.where(of_first, rounded[heads : heads + 1], rounded[SLOTS + heads : SLOTS + heads + 1])
    newest[...] = jnp.where(of_first, rounded[heads + 1 : heads + 2], rounded[SLOTS + heads + 1 : SLOTS + heads + 2])
    fresh = jnp.sum(in_pair(rounded) * new_key, axis=1, keepdims=True) * scale
    new_score[...] = jnp.sum(jnp.where(pair_diagonal, fresh, 0.0), axis=0, keepdims=True)
    key_copy.wait()
    val_copy.wait()
    wait_for(qrows, owners - 1, recv_sem.at[1])

    head = iota((SLOTS, head_dim), 0)
    lanes = iota((SLOTS, head_dim), 1)
    diagonal = lanes == head
    repeated = lax.rem(lanes, SLOTS) == head

    def query_of(c):
        pair = qrows[pair_s[c]].astype(f32)
        rows_of = [jnp.where(odd_s[c] == 1, pair[16:24], pair[0:8]), pair[8:16]]
        return jnp.concatenate(rows_of, axis=0).astype(bf16)

    def soften(c, raw):
        shown = jnp.where(lanes < lim_s[c], raw * scale, very_low)
        top = jnp.max(shown, axis=1, keepdims=True)
        weights = jnp.exp(shown - top)
        total = jnp.sum(weights, axis=1, keepdims=True)
        top_row = jnp.sum(jnp.where(repeated, top, 0.0), axis=0, keepdims=True)
        total_row = jnp.sum(jnp.where(repeated, total, 0.0), axis=0, keepdims=True)
        return weights.astype(bf16), top_row, total_row

    all_spans = range(spans_here)
    raws = [
        lax.dot_general(query_of(c), key_v[0, c], (((1,), (1,)), ((), ())), preferred_element_type=f32)
        for c in all_spans
    ]
    softened = [soften(c, raws[c]) for c in all_spans]
    for c in all_spans:
        values[c] = jnp.dot(softened[c][0], val_v[0, c], preferred_element_type=f32)
    for c in all_spans:
        maxima[c : c + 1, :] = softened[c][1]
        totals[c : c + 1, :] = softened[c][2]
    every = maxima[...]
    request_top = every
    for c in range(spans_here):
        request_top = jnp.maximum(request_top, jnp.where(col_req[...] == req_s[c], every[c : c + 1], very_low))
    factor = jnp.exp(every - request_top)
    factors[...] = factor
    group = lane // SLOTS
    said = jnp.where(lax.rem(group, 2) == 0, request_top * leader[...], factor * totals[...])
    high = said.astype(bf16)
    rest = said - high.astype(f32)
    middle = rest.astype(bf16)
    low = (rest - middle.astype(f32)).astype(bf16)
    thirds = jnp.concatenate([high, middle, low], axis=0).astype(f32)
    first_lanes = jnp.where(group < 2, thirds, 0.0).astype(bf16)
    second_lanes = jnp.where((group == 2) | (group == 3), thirds, 0.0).astype(bf16)
    stats = jnp.dot(
        pick_stat[...], jnp.concatenate([first_lanes, second_lanes], axis=0), preferred_element_type=f32
    )
    stat_out[...] = stats.reshape(owners, 1, head_dim)
    for d in owner_order:
        place, device = owner_at(*d)
        pltpu.make_async_remote_copy(
            src_ref=stat_out.at[place],
            dst_ref=stat_in.at[owner],
            send_sem=send_sem.at[6],
            recv_sem=recv_sem.at[6],
            device_id=device,
            device_id_type=MESH,
        ).start()
    stat_in[owner] = stat_out[owner]

    def weigh(c):
        factor = jnp.sum(jnp.where(diagonal, factors[pl.ds(c, 1), :], 0.0), axis=1, keepdims=True)
        result = (values[c] * factor).astype(bf16)

        def store():
            spans[pl.ds(pl.multiple_of(c * SLOTS, SLOTS), SLOTS), :] = result

        return store

    chunks(spans_here, 32, weigh)

    for dg in far_first(n_grp, 1):
        group_of = lax.rem(g + dg, n_grp)
        at = pl.multiple_of(group_of * n_mem * PAIR, n_mem * PAIR)
        summed = jnp.dot(pick[pl.ds(at, n_mem * PAIR), :], spans[...], preferred_element_type=f32)
        soft_out[pl.ds(group_of * n_mem, n_mem)] = summed.astype(bf16).reshape(n_mem, PAIR, head_dim)
        for d in mem_order if dg == 0 else mem_order + [0]:
            place, device = owner_at(dg, d)
            pltpu.make_async_remote_copy(
                src_ref=soft_out.at[place],
                dst_ref=soft_in.at[owner],
                send_sem=send_sem.at[2],
                recv_sem=recv_sem.at[2],
                device_id=device,
                device_id_type=MESH,
            ).start()
    soft_in[owner] = soft_out[owner]
    wait_for(stat_in, owners - 1, recv_sem.at[6])
    stats = stat_in[...].reshape(owners, head_dim)
    total = pltpu.roll(stats, head_dim - SLOTS, axis=1)
    top = jnp.where(total > 0.0, stats, very_low)
    new_top = new_score[...]
    most = jnp.maximum(jnp.max(top, axis=0, keepdims=True), new_top)
    factor = jnp.exp(top - most)
    new_factor = jnp.exp(new_top - most)
    whole = jnp.sum(factor * total, axis=0, keepdims=True) + new_factor
    blend[...] = factor / whole
    new_share = jnp.sum(jnp.where(pair_diagonal, new_factor / whole, 0.0), axis=1, keepdims=True)
    wait_for(soft_in, owners - 1, recv_sem.at[2])

    def join(b, carry):
        for u in range(16):
            s = b * 16 + u
            share = jnp.sum(jnp.where(pair_diagonal, blend[pl.ds(s, 1), :], 0.0), axis=1, keepdims=True)
            carry = carry + share * soft_in[s].astype(f32)
        return carry

    att[m] = lax.fori_loop(0, owners // 16, join, new_share * newest[...]).astype(bf16)

    for d in mem_order:
        pltpu.make_async_remote_copy(
            src_ref=att.at[m],
            dst_ref=att.at[m],
            send_sem=send_sem.at[3],
            recv_sem=recv_sem.at[3],
            device_id={"mem": owner_at(0, d)[1]["mem"]},
            device_id_type=MESH,
        ).start()
    out_copy.wait()
    wait_for(att, n_mem - 1, recv_sem.at[3])

    out_cols = wo_v.shape[1] // head_dim
    att_wide[...] = att[...].astype(f32).reshape(n_mem * PAIR, head_dim)

    def head_rows(h):
        second = h + 16 if h < 8 else h + 4
        return jnp.concatenate([att_wide[pl.ds(row, n_mem, stride=PAIR), :] for row in (h, second)], axis=0)

    left = jnp.concatenate([head_rows(h) for h in range(heads)], axis=1).astype(bf16)
    product = jnp.dot(left, wo_v[...], preferred_element_type=f32)
    for n in range(out_cols):
        for i in range(own_rows):
            piece = product[i * n_mem : (i + 1) * n_mem, n * head_dim : (n + 1) * head_dim]
            wide_rows[pl.ds(i * out_cols + n, n_mem, stride=own_rows * out_cols), :] = piece
    sums[...] = wide_rows[...].astype(bf16).reshape(n_tp, out_rows * out_cols, head_dim)

    pl.semaphore_wait(tp_sem.at[1], len(beside))
    for d in tp_order:
        to = lax.rem(t + d, n_tp)
        pltpu.make_async_remote_copy(
            src_ref=sums.at[to],
            dst_ref=sums_in.at[t],
            send_sem=send_sem.at[4],
            recv_sem=recv_sem.at[4],
            device_id={"tp": to},
            device_id_type=MESH,
        ).start()
    sums_in[t] = sums[t]
    wait_for(sums_in, n_tp - 1, recv_sem.at[4])
    total = sums_in[0].astype(f32)
    for i in range(1, n_tp):
        total = total + sums_in[i].astype(f32)
    done[t] = total.astype(bf16)
    for d in tp_order:
        pltpu.make_async_remote_copy(
            src_ref=done.at[t],
            dst_ref=done.at[t],
            send_sem=send_sem.at[5],
            recv_sem=recv_sem.at[5],
            device_id={"tp": lax.rem(t + d, n_tp)},
            device_id_type=MESH,
        ).start()
    wait_for(done, n_tp - 1, recv_sem.at[5])
    wide_rows[...] = done[...].astype(f32).reshape(rows * out_cols, head_dim)
    for n in range(out_cols):
        out[:, n * head_dim : (n + 1) * head_dim] = wide_rows[pl.ds(n, rows, stride=out_cols), :].astype(bf16)

    wait_for(part, (n_mem - 1) * tile, send_sem.at[0])
    wait_for(qrows, owners - 1, send_sem.at[1])
    wait_for(soft_out, owners - 1, send_sem.at[2])
    wait_for(stat_out, owners - 1, send_sem.at[6])
    wait_for(att, n_mem - 1, send_sem.at[3])
    wait_for(sums, n_tp - 1, send_sem.at[4])
    wait_for(done, n_tp - 1, send_sem.at[5])


def per_device(n_grp, n_tp, n_mem, *args):
    tokens, norm_gain, w_query, w_keyval, w_out, key_cache, value_cache, req_len, span_request, _, _ = args
    rows, width = tokens.shape
    q_cols = w_query.shape[1]
    head_dim = key_cache.shape[3]
    spans_here = span_request.shape[0]
    requests = req_len.shape[0]
    owners = n_grp * n_mem
    own_rows = rows // n_mem
    tile = own_rows * SLOTS
    out_width = w_out.shape[1]
    slab = rows // n_tp * out_width // head_dim
    scratch = [
        pltpu.VMEM(tokens.shape, bf16),
        pltpu.VMEM(norm_gain.shape, f32),
        pltpu.VMEM(w_query.shape, bf16),
        pltpu.VMEM(w_keyval.shape, bf16),
        pltpu.VMEM(w_out.shape, bf16),
        pltpu.VMEM(key_cache.shape, bf16),
        pltpu.VMEM(value_cache.shape, bf16),
        pltpu.SMEM((requests,), jnp.int32),
        pltpu.SMEM((spans_here,), jnp.int32),
        pltpu.SMEM((spans_here,), jnp.int32),
        pltpu.SMEM((spans_here,), jnp.int32),
        pltpu.SMEM((spans_here,), jnp.int32),
        pltpu.SMEM((spans_here,), jnp.int32),
        pltpu.VMEM((rows * SLOTS, head_dim), f32),
        pltpu.VMEM((n_mem, tile, head_dim), f32),
        pltpu.VMEM((2, tile, head_dim), f32),
        pltpu.VMEM((owners * PAIR, spans_here * SLOTS), bf16),
        pltpu.VMEM((owners, 6 * spans_here), bf16),
        pltpu.VMEM((spans_here, head_dim), jnp.int32),
        pltpu.VMEM((spans_here, head_dim), f32),
        pltpu.VMEM((owners, PAIR, head_dim), bf16),
        pltpu.VMEM((PAIR, head_dim), f32),
        pltpu.VMEM((1, head_dim), f32),
        pltpu.VMEM((spans_here, SLOTS, head_dim), f32),
        pltpu.VMEM((spans_here, head_dim), f32),
        pltpu.VMEM((spans_here, head_dim), f32),
        pltpu.VMEM((spans_here, head_dim), f32),
        pltpu.VMEM((spans_here * SLOTS, head_dim), bf16),
        pltpu.VMEM((owners, PAIR, head_dim), bf16),
        pltpu.VMEM((owners, PAIR, head_dim), bf16),
        pltpu.VMEM((owners, 1, head_dim), f32),
        pltpu.VMEM((owners, 1, head_dim), f32),
        pltpu.VMEM((owners, head_dim), f32),
        pltpu.VMEM((n_mem, PAIR, head_dim), bf16),
        pltpu.VMEM((n_mem * PAIR, head_dim), f32),
        pltpu.VMEM((n_tp * slab, head_dim), f32),
        pltpu.VMEM((n_tp, slab, head_dim), bf16),
        pltpu.VMEM((n_tp, slab, head_dim), bf16),
        pltpu.VMEM((n_tp, slab, head_dim), bf16),
        pltpu.SemaphoreType.DMA((16,)),
        pltpu.SemaphoreType.DMA((7,)),
        pltpu.SemaphoreType.DMA((7,)),
        pltpu.SemaphoreType.REGULAR((2,)),
    ]
    return pl.pallas_call(
        functools.partial(kernel, n_grp, n_tp, n_mem),
        out_shape=pltpu.VMEM((rows, out_width), bf16),
        in_specs=[pl.BlockSpec(memory_space=HBM)] * len(args),
        out_specs=pl.BlockSpec(memory_space=pltpu.VMEM),
        scratch_shapes=scratch,
        compiler_params=pltpu.CompilerParams(
            collective_id=0, has_side_effects=True, vmem_limit_bytes=48 * 1024 * 1024
        ),
        cost_estimate=pl.CostEstimate(flops=200_000_000, bytes_accessed=12_600_000, transcendentals=100_000),
    )(*[pltpu.with_memory_space_constraint(a, HBM) for a in args])


def solution(mesh):
    placed = (
        P("grp", "mem"),
        P("mem"),
        P("mem", "tp"),
        P(None, "mem", "tp"),
        P("tp", "mem"),
        P("tp", ("grp", "mem"), None, None),
        P("tp", ("grp", "mem"), None, None),
        P(),
        P(("grp", "mem")),
        P(("grp", "mem")),
        P(),
    )
    body = functools.partial(per_device, mesh.shape["grp"], mesh.shape["tp"], mesh.shape["mem"])
    return jax.shard_map(body, mesh=mesh, in_specs=placed, out_specs=P("grp", "mem"), check_vma=False)
```

```python
import functools

import jax
import jax.numpy as jnp
from jax import lax
from jax.experimental import pallas as pl
from jax.experimental.pallas import tpu as pltpu
from jax.sharding import PartitionSpec as P

MESH = pl.DeviceIdType.MESH
HBM = pltpu.MemorySpace.HBM
D = 12288
epsilon = 1e-05
rope_base = 1000000.0
very_low = -1e30
SLOTS = 16
PAIR = 24
f32 = jnp.float32
bf16 = jnp.bfloat16


def chunks(count, width, body):
    def step(b, carry):
        stores = [body(b * width + u) for u in range(width)]
        for store in stores:
            store()
        return carry

    lax.fori_loop(0, count // width, step, 0)


def hops(d, size):
    return min(d, size - d)


def far_first(size, each):
    chips = sorted(range(size), key=lambda d: -hops(d, size))
    return [d * each + c for d in chips for c in range(each)]


def iota(shape, dim):
    return lax.broadcasted_iota(jnp.int32, shape, dim)


def kernel(
    n_grp, n_tp, n_mem,
    tokens, gain, w_query, w_keyval, w_out, key_cache, value_cache, req_len, span_request, span_first, new_slot,
    out,
    tok_v, gain_v, wq_v, wkv_v, wo_v, key_v, val_v, len_s, req_s, first_s, lim_s, pair_s, odd_s,
    part, part_in, table, pick, pick_stat, col_req, leader, qrows, key_t, newest, new_score, values, maxima, totals, factors, spans,
    soft_out, soft_in, stat_out, stat_in, blend, att, att_wide, wide_rows, sums, sums_in, done, local_sem, send_sem, recv_sem, tp_sem,
):
    g, t, m = lax.axis_index("grp"), lax.axis_index("tp"), lax.axis_index("mem")
    owners = n_grp * n_mem
    owner = g * n_mem + m
    rows, width = tok_v.shape
    requests = len_s.shape[0]
    own_rows = rows // n_mem
    out_rows = rows // n_tp
    spans_here = req_s.shape[0]
    q_cols = wq_v.shape[1]
    head_dim = key_v.shape[3]
    heads = q_cols // head_dim
    tile = own_rows * SLOTS
    k_chunks = 6
    k_step = width // k_chunks

    small = [
        pltpu.make_async_copy(req_len, len_s, local_sem.at[0]),
        pltpu.make_async_copy(span_request, req_s, local_sem.at[1]),
        pltpu.make_async_copy(span_first, first_s, local_sem.at[2]),
    ]
    tok_copy = pltpu.make_async_copy(tokens, tok_v, local_sem.at[4])
    gain_copy = pltpu.make_async_copy(gain, gain_v, local_sem.at[5])
    wkv_copy = pltpu.make_async_copy(w_keyval, wkv_v, local_sem.at[6])
    key_copy = pltpu.make_async_copy(key_cache, key_v, local_sem.at[7])
    val_copy = pltpu.make_async_copy(value_cache, val_v, local_sem.at[8])
    out_copy = pltpu.make_async_copy(w_out, wo_v, local_sem.at[9])
    wq_copies = [
        pltpu.make_async_copy(
            w_query.at[pl.ds(c * k_step, k_step), :], wq_v.at[pl.ds(c * k_step, k_step), :], local_sem.at[10 + c]
        )
        for c in range(k_chunks)
    ]
    tok_copy.start()
    gain_copy.start()
    for copy in wq_copies + [wkv_copy] + small:
        copy.start()

    barrier = pltpu.get_barrier_semaphore()

    def owner_at(dg, dm):
        to_g = lax.rem(g + dg, n_grp)
        to_m = lax.rem(m // 2 + dm // 2, n_mem // 2) * 2 + lax.rem(m + dm, 2)
        return to_g * n_mem + to_m, {"grp": to_g, "mem": to_m}

    mem_order = [d for d in far_first(n_mem // 2, 2) if d]
    grp_order = [d for d in far_first(n_grp, 1) if d]
    tp_order = [d for d in far_first(n_tp, 1) if d]
    beside = (1, n_tp - 1)
    for d in mem_order:
        pl.semaphore_signal(barrier, inc=1, device_id=owner_at(0, d)[1], device_id_type=MESH)
    for d in grp_order:
        pl.semaphore_signal(barrier, inc=1, device_id=owner_at(d, 0)[1], device_id_type=MESH)

    def tell_tp(semaphore, distances):
        for d in distances:
            pl.semaphore_signal(semaphore, inc=1, device_id={"tp": lax.rem(t + d, n_tp)}, device_id_type=MESH)

    tell_tp(barrier, beside)
    owner_order = sorted(
        [(dg, dm) for dg in range(n_grp) for dm in range(n_mem) if dg or dm],
        key=lambda d: -hops(d[0], n_grp) - hops(d[1] // 2, n_mem // 2),
    )

    tok_copy.wait()
    gain_copy.wait()
    wide = tok_v[...].astype(f32)
    square = jnp.sum(wide * wide, axis=1, keepdims=True)
    scaled = (wide * gain_v[...].reshape(1, width)).astype(bf16)
    projected = jnp.zeros((rows, q_cols), f32)
    for c in range(k_chunks):
        wq_copies[c].wait()
        projected += jnp.dot(
            scaled[:, c * k_step : (c + 1) * k_step],
            wq_v[c * k_step : (c + 1) * k_step, :],
            preferred_element_type=f32,
        )
    wkv_copy.wait()
    for copy in (key_copy, val_copy, out_copy):
        copy.start()
    new_part = [jnp.dot(scaled, wkv_v[i], preferred_element_type=f32) for i in range(2)]
    pieces = [projected[:, h * head_dim : (h + 1) * head_dim] for h in range(heads)] + new_part
    pieces += [jnp.broadcast_to(square, (rows, head_dim))]
    pieces += [jnp.zeros((rows, head_dim), f32)] * (SLOTS - len(pieces))
    for h, piece in enumerate(pieces):
        part[pl.ds(h, rows, stride=SLOTS), :] = piece

    pl.semaphore_wait(barrier, len(mem_order) + len(grp_order) + len(beside))
    tell_tp(tp_sem.at[0], beside)

    for d in mem_order:
        to = owner_at(0, d)[1]["mem"]
        pltpu.make_async_remote_copy(
            src_ref=part.at[pl.ds(pl.multiple_of(to * tile, tile), tile), :],
            dst_ref=part_in.at[m],
            send_sem=send_sem.at[0],
            recv_sem=recv_sem.at[0],
            device_id={"mem": to},
            device_id_type=MESH,
        ).start()
    part_in[m] = part[pl.ds(pl.multiple_of(m * tile, tile), tile), :]

    for copy in small:
        copy.wait()
    lane = iota((1, head_dim), 1)
    own_len = [len_s[g * rows + m * own_rows + i] for i in range(own_rows)]
    position = jnp.where(iota((tile, 1), 0) < SLOTS, own_len[0], own_len[1]).astype(f32)
    half = head_dim // 2
    power = (lax.rem(lane, half).astype(f32) * 2.0) / head_dim
    frequency = jnp.exp(power * -jnp.log(jnp.full((1, head_dim), rope_base, f32)))
    angles = position * frequency
    slot_row = lax.rem(iota((tile, head_dim), 0), SLOTS)
    turned = slot_row < heads + 1
    cosine = jnp.where(turned, jnp.cos(angles), 1.0)
    sine = jnp.where(turned, jnp.sin(angles), 0.0)
    table[0] = cosine
    table[1] = jnp.where(lane < half, -sine, sine)

    def span_scalars(c, carry):
        r = jnp.maximum(req_s[c], 0)
        lim_s[c] = jnp.where(req_s[c] >= 0, len_s[r] - first_s[c], 0)
        pair_s[c] = r // 2
        odd_s[c] = lax.rem(r, 2)
        return carry

    lax.fori_loop(0, spans_here, span_scalars, 0)

    flat = spans_here * SLOTS
    column = iota((1, flat), 1)
    in_rows = iota((spans_here, head_dim), 0)
    by_column = jnp.zeros((1, flat), jnp.int32)
    by_row = jnp.zeros((spans_here, head_dim), jnp.int32)
    stat_column = iota((1, 6 * spans_here), 1)
    by_stat = jnp.zeros((1, 6 * spans_here), jnp.int32)
    for c in range(spans_here):
        by_column = jnp.where(column // SLOTS == c, req_s[c], by_column)
        by_row = jnp.where(in_rows == c, req_s[c], by_row)
        by_stat = jnp.where(lax.rem(stat_column, spans_here) == c, req_s[c], by_stat)
    col_req[...] = by_row
    first_of = jnp.ones((spans_here, head_dim), f32)
    for c in range(spans_here):
        first_of = jnp.where((by_row == req_s[c]) & (in_rows > c), 0.0, first_of)
    leader[...] = first_of
    row_in = lax.rem(column, SLOTS)
    nowhere = -requests * SLOTS
    of_first = jnp.where(row_in < 12, row_in, nowhere)
    of_second = jnp.where(row_in < 8, row_in + 16, jnp.where(row_in < 12, nowhere, row_in))
    target = (by_column + 2) // 2 * PAIR - PAIR + jnp.where(lax.rem(by_column + 2, 2) == 1, of_second, of_first)
    target = jnp.where(by_column < 0, nowhere, target)
    pick_rows = 96

    def fill_pick(b, carry):
        at = pl.multiple_of(b * pick_rows, pick_rows)
        row = iota((pick_rows, flat), 0) + at
        pick[pl.ds(at, pick_rows), :] = jnp.where(row == target, 1.0, 0.0).astype(bf16)
        return carry

    lax.fori_loop(0, owners * PAIR // pick_rows, fill_pick, 0)
    wanted = iota((owners, 6 * spans_here), 0) * 2 + stat_column // (3 * spans_here)
    pick_stat[...] = jnp.where(wanted == by_stat, 1.0, 0.0).astype(bf16)

    def wait_for(buffer, amount, kind):
        ref = buffer.at[pl.ds(0, amount)]
        pltpu.make_async_copy(ref, ref, kind).wait()

    wait_for(part_in, n_mem - 1, recv_sem.at[0])
    total = part_in[0]
    for i in range(1, n_mem):
        total = total + part_in[i]
    normed = []
    for i in range(own_rows):
        block = total[i * SLOTS : (i + 1) * SLOTS]
        root_mean = jnp.sqrt(block[heads + 2 : heads + 3] / D + epsilon)
        normed.append(block / root_mean)
    normed = jnp.concatenate(normed, axis=0)
    finished = normed * table[0] + pltpu.roll(normed, half, axis=1) * table[1]

    def in_pair(block):
        sub_row = iota((8, head_dim), 0)
        middle = jnp.where(sub_row < 4, block[8:16], pltpu.roll(block[24:32], 4, axis=0))
        return jnp.concatenate([block[0:8], middle, block[16:24]], axis=0)

    qrows[owner] = in_pair(finished).astype(bf16)

    for d in owner_order:
        pltpu.make_async_remote_copy(
            src_ref=qrows.at[owner],
            dst_ref=qrows.at[owner],
            send_sem=send_sem.at[1],
            recv_sem=recv_sem.at[1],
            device_id=owner_at(*d)[1],
            device_id_type=MESH,
        ).start()
    pl.semaphore_wait(tp_sem.at[0], len(beside))
    tell_tp(tp_sem.at[1], (2, n_tp - 2))
    scale = head_dim**-0.5
    rounded = finished.astype(bf16).astype(f32)
    pair_row = iota((PAIR, head_dim), 0)
    pair_lane = iota((PAIR, head_dim), 1)
    of_first = pair_row < 12
    pair_diagonal = pair_lane == jnp.where(of_first, pair_row, jnp.where(pair_row < 16, pair_row + 32, pair_row + 16))
    new_key = jnp.where(of_first, rounded[heads : heads + 1], rounded[SLOTS + heads : SLOTS + heads + 1])
    newest[...] = jnp.where(of_first, rounded[heads + 1 : heads + 2], rounded[SLOTS + heads + 1 : SLOTS + heads + 2])
    fresh = jnp.sum(in_pair(rounded) * new_key, axis=1, keepdims=True) * scale
    new_score[...] = jnp.sum(jnp.where(pair_diagonal, fresh, 0.0), axis=0, keepdims=True)
    key_copy.wait()

    def turn(c, carry):
        key_t[c] = key_v[0, c].T
        return carry

    lax.fori_loop(0, spans_here, turn, 0)
    val_copy.wait()
    wait_for(qrows, owners - 1, recv_sem.at[1])

    head = iota((SLOTS, head_dim), 0)
    lanes = iota((SLOTS, head_dim), 1)
    diagonal = lanes == head
    repeated = lax.rem(lanes, SLOTS) == head

    def query_of(c):
        pair = qrows[pair_s[c]].astype(f32)
        rows_of = [jnp.where(odd_s[c] == 1, pair[16:24], pair[0:8]), pair[8:16]]
        return jnp.concatenate(rows_of, axis=0).astype(bf16)

    def soften(c, raw):
        shown = jnp.where(lanes < lim_s[c], raw * scale, very_low)
        top = jnp.max(shown, axis=1, keepdims=True)
        weights = jnp.exp(shown - top)
        total = jnp.sum(weights, axis=1, keepdims=True)
        top_row = jnp.sum(jnp.where(repeated, top, 0.0), axis=0, keepdims=True)
        total_row = jnp.sum(jnp.where(repeated, total, 0.0), axis=0, keepdims=True)
        return weights.astype(bf16), top_row, total_row

    all_spans = range(spans_here)
    raws = [
        jnp.dot(query_of(c), key_t[c], preferred_element_type=f32)
        for c in all_spans
    ]
    softened = [soften(c, raws[c]) for c in all_spans]
    for c in all_spans:
        values[c] = jnp.dot(softened[c][0], val_v[0, c], preferred_element_type=f32)
    for c in all_spans:
        maxima[c : c + 1, :] = softened[c][1]
        totals[c : c + 1, :] = softened[c][2]
    every = maxima[...]
    request_top = every
    for c in range(spans_here):
        request_top = jnp.maximum(request_top, jnp.where(col_req[...] == req_s[c], every[c : c + 1], very_low))
    factor = jnp.exp(every - request_top)
    factors[...] = factor
    def weigh(c):
        factor = jnp.sum(jnp.where(diagonal, factors[pl.ds(c, 1), :], 0.0), axis=1, keepdims=True)
        result = (values[c] * factor).astype(bf16)

        def store():
            spans[pl.ds(pl.multiple_of(c * SLOTS, SLOTS), SLOTS), :] = result

        return store

    chunks(spans_here, 32, weigh)

    group = lane // SLOTS
    said = jnp.where(lax.rem(group, 2) == 0, request_top * leader[...], factor * totals[...])
    high = said.astype(bf16)
    rest = said - high.astype(f32)
    middle = rest.astype(bf16)
    low = (rest - middle.astype(f32)).astype(bf16)
    thirds = jnp.concatenate([high, middle, low], axis=0).astype(f32)
    first_lanes = jnp.where(group < 2, thirds, 0.0).astype(bf16)
    second_lanes = jnp.where((group == 2) | (group == 3), thirds, 0.0).astype(bf16)
    stats = jnp.dot(
        pick_stat[...], jnp.concatenate([first_lanes, second_lanes], axis=0), preferred_element_type=f32
    )
    stat_out[...] = stats.reshape(owners, 1, head_dim)
    for d in owner_order:
        place, device = owner_at(*d)
        pltpu.make_async_remote_copy(
            src_ref=stat_out.at[place],
            dst_ref=stat_in.at[owner],
            send_sem=send_sem.at[6],
            recv_sem=recv_sem.at[6],
            device_id=device,
            device_id_type=MESH,
        ).start()
    stat_in[owner] = stat_out[owner]

    for dg in far_first(n_grp, 1):
        group_of = lax.rem(g + dg, n_grp)
        at = pl.multiple_of(group_of * n_mem * PAIR, n_mem * PAIR)
        summed = jnp.dot(pick[pl.ds(at, n_mem * PAIR), :], spans[...], preferred_element_type=f32)
        soft_out[pl.ds(group_of * n_mem, n_mem)] = summed.astype(bf16).reshape(n_mem, PAIR, head_dim)
        for d in mem_order if dg == 0 else mem_order + [0]:
            place, device = owner_at(dg, d)
            pltpu.make_async_remote_copy(
                src_ref=soft_out.at[place],
                dst_ref=soft_in.at[owner],
                send_sem=send_sem.at[2],
                recv_sem=recv_sem.at[2],
                device_id=device,
                device_id_type=MESH,
            ).start()
    soft_in[owner] = soft_out[owner]
    wait_for(stat_in, owners - 1, recv_sem.at[6])
    stats = stat_in[...].reshape(owners, head_dim)
    total = pltpu.roll(stats, head_dim - SLOTS, axis=1)
    top = jnp.where(total > 0.0, stats, very_low)
    new_top = new_score[...]
    most = jnp.maximum(jnp.max(top, axis=0, keepdims=True), new_top)
    factor = jnp.exp(top - most)
    new_factor = jnp.exp(new_top - most)
    whole = jnp.sum(factor * total, axis=0, keepdims=True) + new_factor
    blend[...] = factor / whole
    new_share = jnp.sum(jnp.where(pair_diagonal, new_factor / whole, 0.0), axis=1, keepdims=True)
    wait_for(soft_in, owners - 1, recv_sem.at[2])

    def join(b, carry):
        for u in range(16):
            s = b * 16 + u
            share = jnp.sum(jnp.where(pair_diagonal, blend[pl.ds(s, 1), :], 0.0), axis=1, keepdims=True)
            carry = carry + share * soft_in[s].astype(f32)
        return carry

    att[m] = lax.fori_loop(0, owners // 16, join, new_share * newest[...]).astype(bf16)

    for d in mem_order:
        pltpu.make_async_remote_copy(
            src_ref=att.at[m],
            dst_ref=att.at[m],
            send_sem=send_sem.at[3],
            recv_sem=recv_sem.at[3],
            device_id={"mem": owner_at(0, d)[1]["mem"]},
            device_id_type=MESH,
        ).start()
    out_copy.wait()
    wait_for(att, n_mem - 1, recv_sem.at[3])

    out_cols = wo_v.shape[1] // head_dim
    att_wide[...] = att[...].astype(f32).reshape(n_mem * PAIR, head_dim)

    def head_rows(h):
        second = h + 16 if h < 8 else h + 4
        return jnp.concatenate([att_wide[pl.ds(row, n_mem, stride=PAIR), :] for row in (h, second)], axis=0)

    left = jnp.concatenate([head_rows(h) for h in range(heads)], axis=1).astype(bf16)
    product = jnp.dot(left, wo_v[...], preferred_element_type=f32)
    for n in range(out_cols):
        for i in range(own_rows):
            piece = product[i * n_mem : (i + 1) * n_mem, n * head_dim : (n + 1) * head_dim]
            wide_rows[pl.ds(i * out_cols + n, n_mem, stride=own_rows * out_cols), :] = piece
    sums[...] = wide_rows[...].astype(bf16).reshape(n_tp, out_rows * out_cols, head_dim)

    pl.semaphore_wait(tp_sem.at[1], len(beside))
    for d in tp_order:
        to = lax.rem(t + d, n_tp)
        pltpu.make_async_remote_copy(
            src_ref=sums.at[to],
            dst_ref=sums_in.at[t],
            send_sem=send_sem.at[4],
            recv_sem=recv_sem.at[4],
            device_id={"tp": to},
            device_id_type=MESH,
        ).start()
    sums_in[t] = sums[t]
    wait_for(sums_in, n_tp - 1, recv_sem.at[4])
    total = sums_in[0].astype(f32)
    for i in range(1, n_tp):
        total = total + sums_in[i].astype(f32)
    done[t] = total.astype(bf16)
    for d in tp_order:
        pltpu.make_async_remote_copy(
            src_ref=done.at[t],
            dst_ref=done.at[t],
            send_sem=send_sem.at[5],
            recv_sem=recv_sem.at[5],
            device_id={"tp": lax.rem(t + d, n_tp)},
            device_id_type=MESH,
        ).start()
    wait_for(done, n_tp - 1, recv_sem.at[5])
    wide_rows[...] = done[...].astype(f32).reshape(rows * out_cols, head_dim)
    for n in range(out_cols):
        out[:, n * head_dim : (n + 1) * head_dim] = wide_rows[pl.ds(n, rows, stride=out_cols), :].astype(bf16)

    wait_for(part, (n_mem - 1) * tile, send_sem.at[0])
    wait_for(qrows, owners - 1, send_sem.at[1])
    wait_for(soft_out, owners - 1, send_sem.at[2])
    wait_for(stat_out, owners - 1, send_sem.at[6])
    wait_for(att, n_mem - 1, send_sem.at[3])
    wait_for(sums, n_tp - 1, send_sem.at[4])
    wait_for(done, n_tp - 1, send_sem.at[5])


def per_device(n_grp, n_tp, n_mem, *args):
    tokens, norm_gain, w_query, w_keyval, w_out, key_cache, value_cache, req_len, span_request, _, _ = args
    rows, width = tokens.shape
    q_cols = w_query.shape[1]
    head_dim = key_cache.shape[3]
    spans_here = span_request.shape[0]
    requests = req_len.shape[0]
    owners = n_grp * n_mem
    own_rows = rows // n_mem
    tile = own_rows * SLOTS
    out_width = w_out.shape[1]
    slab = rows // n_tp * out_width // head_dim
    scratch = [
        pltpu.VMEM(tokens.shape, bf16),
        pltpu.VMEM(norm_gain.shape, f32),
        pltpu.VMEM(w_query.shape, bf16),
        pltpu.VMEM(w_keyval.shape, bf16),
        pltpu.VMEM(w_out.shape, bf16),
        pltpu.VMEM(key_cache.shape, bf16),
        pltpu.VMEM(value_cache.shape, bf16),
        pltpu.SMEM((requests,), jnp.int32),
        pltpu.SMEM((spans_here,), jnp.int32),
        pltpu.SMEM((spans_here,), jnp.int32),
        pltpu.SMEM((spans_here,), jnp.int32),
        pltpu.SMEM((spans_here,), jnp.int32),
        pltpu.SMEM((spans_here,), jnp.int32),
        pltpu.VMEM((rows * SLOTS, head_dim), f32),
        pltpu.VMEM((n_mem, tile, head_dim), f32),
        pltpu.VMEM((2, tile, head_dim), f32),
        pltpu.VMEM((owners * PAIR, spans_here * SLOTS), bf16),
        pltpu.VMEM((owners, 6 * spans_here), bf16),
        pltpu.VMEM((spans_here, head_dim), jnp.int32),
        pltpu.VMEM((spans_here, head_dim), f32),
        pltpu.VMEM((owners, PAIR, head_dim), bf16),
        pltpu.VMEM((spans_here, head_dim, key_cache.shape[2]), bf16),
        pltpu.VMEM((PAIR, head_dim), f32),
        pltpu.VMEM((1, head_dim), f32),
        pltpu.VMEM((spans_here, SLOTS, head_dim), f32),
        pltpu.VMEM((spans_here, head_dim), f32),
        pltpu.VMEM((spans_here, head_dim), f32),
        pltpu.VMEM((spans_here, head_dim), f32),
        pltpu.VMEM((spans_here * SLOTS, head_dim), bf16),
        pltpu.VMEM((owners, PAIR, head_dim), bf16),
        pltpu.VMEM((owners, PAIR, head_dim), bf16),
        pltpu.VMEM((owners, 1, head_dim), f32),
        pltpu.VMEM((owners, 1, head_dim), f32),
        pltpu.VMEM((owners, head_dim), f32),
        pltpu.VMEM((n_mem, PAIR, head_dim), bf16),
        pltpu.VMEM((n_mem * PAIR, head_dim), f32),
        pltpu.VMEM((n_tp * slab, head_dim), f32),
        pltpu.VMEM((n_tp, slab, head_dim), bf16),
        pltpu.VMEM((n_tp, slab, head_dim), bf16),
        pltpu.VMEM((n_tp, slab, head_dim), bf16),
        pltpu.SemaphoreType.DMA((16,)),
        pltpu.SemaphoreType.DMA((7,)),
        pltpu.SemaphoreType.DMA((7,)),
        pltpu.SemaphoreType.REGULAR((2,)),
    ]
    return pl.pallas_call(
        functools.partial(kernel, n_grp, n_tp, n_mem),
        out_shape=pltpu.VMEM((rows, out_width), bf16),
        in_specs=[pl.BlockSpec(memory_space=HBM)] * len(args),
        out_specs=pl.BlockSpec(memory_space=pltpu.VMEM),
        scratch_shapes=scratch,
        compiler_params=pltpu.CompilerParams(
            collective_id=0, has_side_effects=True, vmem_limit_bytes=48 * 1024 * 1024
        ),
        cost_estimate=pl.CostEstimate(flops=200_000_000, bytes_accessed=12_600_000, transcendentals=100_000),
    )(*[pltpu.with_memory_space_constraint(a, HBM) for a in args])


def solution(mesh):
    placed = (
        P("grp", "mem"),
        P("mem"),
        P("mem", "tp"),
        P(None, "mem", "tp"),
        P("tp", "mem"),
        P("tp", ("grp", "mem"), None, None),
        P("tp", ("grp", "mem"), None, None),
        P(),
        P(("grp", "mem")),
        P(("grp", "mem")),
        P(),
    )
    body = functools.partial(per_device, mesh.shape["grp"], mesh.shape["tp"], mesh.shape["mem"])
    return jax.shard_map(body, mesh=mesh, in_specs=placed, out_specs=P("grp", "mem"), check_vma=False)
```

```python
import functools

import jax
import jax.numpy as jnp
from jax import lax
from jax.experimental import pallas as pl
from jax.experimental.pallas import tpu as pltpu
from jax.sharding import PartitionSpec as P

MESH = pl.DeviceIdType.MESH
HBM = pltpu.MemorySpace.HBM
D = 12288
epsilon = 1e-05
rope_base = 1000000.0
very_low = -1e30
SLOTS = 16
PAIR = 24
f32 = jnp.float32
bf16 = jnp.bfloat16


def chunks(count, width, body):
    def step(b, carry):
        stores = [body(b * width + u) for u in range(width)]
        for store in stores:
            store()
        return carry

    lax.fori_loop(0, count // width, step, 0)


def hops(d, size):
    return min(d, size - d)


def far_first(size, each):
    chips = sorted(range(size), key=lambda d: -hops(d, size))
    return [d * each + c for d in chips for c in range(each)]


def iota(shape, dim):
    return lax.broadcasted_iota(jnp.int32, shape, dim)


def kernel(
    n_grp, n_tp, n_mem,
    tokens, gain, w_query, w_keyval, w_out, key_cache, value_cache, req_len, span_request, span_first, new_slot,
    out,
    tok_v, gain_v, wq_v, wkv_v, wo_v, key_v, val_v, len_s, req_s, first_s, lim_s, pair_s, odd_s,
    part, part_in, table, pick, pick_stat, col_req, leader, qrows, key_t, newest, new_score, values, maxima, totals, factors, spans,
    soft_out, soft_in, stat_out, stat_in, blend, shares, att, att_wide, wide_rows, sums, sums_in, done, local_sem, send_sem, recv_sem, tp_sem,
):
    g, t, m = lax.axis_index("grp"), lax.axis_index("tp"), lax.axis_index("mem")
    owners = n_grp * n_mem
    owner = g * n_mem + m
    rows, width = tok_v.shape
    requests = len_s.shape[0]
    own_rows = rows // n_mem
    out_rows = rows // n_tp
    spans_here = req_s.shape[0]
    q_cols = wq_v.shape[1]
    head_dim = key_v.shape[3]
    heads = q_cols // head_dim
    tile = own_rows * SLOTS
    k_chunks = 6
    k_step = width // k_chunks

    small = [
        pltpu.make_async_copy(req_len, len_s, local_sem.at[0]),
        pltpu.make_async_copy(span_request, req_s, local_sem.at[1]),
        pltpu.make_async_copy(span_first, first_s, local_sem.at[2]),
    ]
    tok_copy = pltpu.make_async_copy(tokens, tok_v, local_sem.at[4])
    gain_copy = pltpu.make_async_copy(gain, gain_v, local_sem.at[5])
    wkv_copy = pltpu.make_async_copy(w_keyval, wkv_v, local_sem.at[6])
    key_copy = pltpu.make_async_copy(key_cache, key_v, local_sem.at[7])
    val_copy = pltpu.make_async_copy(value_cache, val_v, local_sem.at[8])
    out_copy = pltpu.make_async_copy(w_out, wo_v, local_sem.at[9])
    wq_copies = [
        pltpu.make_async_copy(
            w_query.at[pl.ds(c * k_step, k_step), :], wq_v.at[pl.ds(c * k_step, k_step), :], local_sem.at[10 + c]
        )
        for c in range(k_chunks)
    ]
    barrier = pltpu.get_barrier_semaphore()

    def owner_at(dg, dm):
        to_g = lax.rem(g + dg, n_grp)
        to_m = lax.rem(m // 2 + dm // 2, n_mem // 2) * 2 + lax.rem(m + dm, 2)
        return to_g * n_mem + to_m, {"grp": to_g, "mem": to_m}

    mem_order = [d for d in far_first(n_mem // 2, 2) if d]
    grp_order = [d for d in far_first(n_grp, 1) if d]
    tp_order = [d for d in far_first(n_tp, 1) if d]
    beside = (1, n_tp - 1)
    for d in mem_order:
        pl.semaphore_signal(barrier, inc=1, device_id=owner_at(0, d)[1], device_id_type=MESH)
    for d in grp_order:
        pl.semaphore_signal(barrier, inc=1, device_id=owner_at(d, 0)[1], device_id_type=MESH)

    def tell_tp(semaphore, distances):
        for d in distances:
            pl.semaphore_signal(semaphore, inc=1, device_id={"tp": lax.rem(t + d, n_tp)}, device_id_type=MESH)

    tell_tp(barrier, beside)
    owner_order = sorted(
        [(dg, dm) for dg in range(n_grp) for dm in range(n_mem) if dg or dm],
        key=lambda d: -hops(d[0], n_grp) - hops(d[1] // 2, n_mem // 2),
    )

    tok_copy.start()
    gain_copy.start()
    for copy in [wkv_copy] + wq_copies + small:
        copy.start()

    tok_copy.wait()
    gain_copy.wait()
    wide = tok_v[...].astype(f32)
    square = jnp.sum(wide * wide, axis=1, keepdims=True)
    scaled = (wide * gain_v[...].reshape(1, width)).astype(bf16)
    wkv_copy.wait()
    new_part = [jnp.dot(scaled, wkv_v[i], preferred_element_type=f32) for i in range(2)]
    projected = jnp.zeros((rows, q_cols), f32)
    for c in range(k_chunks):
        wq_copies[c].wait()
        projected += jnp.dot(
            scaled[:, c * k_step : (c + 1) * k_step],
            wq_v[c * k_step : (c + 1) * k_step, :],
            preferred_element_type=f32,
        )
    for copy in (key_copy, val_copy, out_copy):
        copy.start()
    pieces = [projected[:, h * head_dim : (h + 1) * head_dim] for h in range(heads)] + new_part
    pieces += [jnp.broadcast_to(square, (rows, head_dim))]
    pieces += [jnp.zeros((rows, head_dim), f32)] * (SLOTS - len(pieces))
    for h, piece in enumerate(pieces):
        part[pl.ds(h, rows, stride=SLOTS), :] = piece

    pl.semaphore_wait(barrier, len(mem_order) + len(grp_order) + len(beside))
    tell_tp(tp_sem.at[0], beside)

    for d in mem_order:
        to = owner_at(0, d)[1]["mem"]
        pltpu.make_async_remote_copy(
            src_ref=part.at[pl.ds(pl.multiple_of(to * tile, tile), tile), :],
            dst_ref=part_in.at[m],
            send_sem=send_sem.at[0],
            recv_sem=recv_sem.at[0],
            device_id={"mem": to},
            device_id_type=MESH,
        ).start()
    part_in[m] = part[pl.ds(pl.multiple_of(m * tile, tile), tile), :]

    for copy in small:
        copy.wait()
    lane = iota((1, head_dim), 1)
    own_len = [len_s[g * rows + m * own_rows + i] for i in range(own_rows)]
    position = jnp.where(iota((tile, 1), 0) < SLOTS, own_len[0], own_len[1]).astype(f32)
    half = head_dim // 2
    power = (lax.rem(lane, half).astype(f32) * 2.0) / head_dim
    frequency = jnp.exp(power * -jnp.log(jnp.full((1, head_dim), rope_base, f32)))
    angles = position * frequency
    slot_row = lax.rem(iota((tile, head_dim), 0), SLOTS)
    turned = slot_row < heads + 1
    cosine = jnp.where(turned, jnp.cos(angles), 1.0)
    sine = jnp.where(turned, jnp.sin(angles), 0.0)
    table[0] = cosine
    table[1] = jnp.where(lane < half, -sine, sine)


    def wait_for(buffer, amount, kind):
        ref = buffer.at[pl.ds(0, amount)]
        pltpu.make_async_copy(ref, ref, kind).wait()

    wait_for(part_in, n_mem - 1, recv_sem.at[0])
    total = part_in[0]
    for i in range(1, n_mem):
        total = total + part_in[i]
    normed = []
    for i in range(own_rows):
        block = total[i * SLOTS : (i + 1) * SLOTS]
        root_mean = jnp.sqrt(block[heads + 2 : heads + 3] / D + epsilon)
        normed.append(block / root_mean)
    normed = jnp.concatenate(normed, axis=0)
    finished = normed * table[0] + pltpu.roll(normed, half, axis=1) * table[1]

    def in_pair(block):
        sub_row = iota((8, head_dim), 0)
        middle = jnp.where(sub_row < 4, block[8:16], pltpu.roll(block[24:32], 4, axis=0))
        return jnp.concatenate([block[0:8], middle, block[16:24]], axis=0)

    qrows[owner] = in_pair(finished).astype(bf16)

    for d in owner_order:
        pltpu.make_async_remote_copy(
            src_ref=qrows.at[owner],
            dst_ref=qrows.at[owner],
            send_sem=send_sem.at[1],
            recv_sem=recv_sem.at[1],
            device_id=owner_at(*d)[1],
            device_id_type=MESH,
        ).start()
    pl.semaphore_wait(tp_sem.at[0], len(beside))
    tell_tp(tp_sem.at[1], (2, n_tp - 2))
    scale = head_dim**-0.5
    rounded = finished.astype(bf16).astype(f32)
    pair_row = iota((PAIR, head_dim), 0)
    pair_lane = iota((PAIR, head_dim), 1)
    of_first = pair_row < 12
    pair_diagonal = pair_lane == jnp.where(of_first, pair_row, jnp.where(pair_row < 16, pair_row + 32, pair_row + 16))
    new_key = jnp.where(of_first, rounded[heads : heads + 1], rounded[SLOTS + heads : SLOTS + heads + 1])
    newest[...] = jnp.where(of_first, rounded[heads + 1 : heads + 2], rounded[SLOTS + heads + 1 : SLOTS + heads + 2])
    fresh = jnp.sum(in_pair(rounded) * new_key, axis=1, keepdims=True) * scale
    new_score[...] = jnp.sum(jnp.where(pair_diagonal, fresh, 0.0), axis=0, keepdims=True)
    def span_scalars(c, carry):
        r = jnp.maximum(req_s[c], 0)
        lim_s[c] = jnp.where(req_s[c] >= 0, len_s[r] - first_s[c], 0)
        pair_s[c] = r // 2
        odd_s[c] = lax.rem(r, 2)
        return carry

    lax.fori_loop(0, spans_here, span_scalars, 0)

    flat = spans_here * SLOTS
    column = iota((1, flat), 1)
    in_rows = iota((spans_here, head_dim), 0)
    by_column = jnp.zeros((1, flat), jnp.int32)
    by_row = jnp.zeros((spans_here, head_dim), jnp.int32)
    stat_column = iota((1, 6 * spans_here), 1)
    by_stat = jnp.zeros((1, 6 * spans_here), jnp.int32)
    for c in range(spans_here):
        by_column = jnp.where(column // SLOTS == c, req_s[c], by_column)
        by_row = jnp.where(in_rows == c, req_s[c], by_row)
        by_stat = jnp.where(lax.rem(stat_column, spans_here) == c, req_s[c], by_stat)
    col_req[...] = by_row
    first_of = jnp.ones((spans_here, head_dim), f32)
    for c in range(spans_here):
        first_of = jnp.where((by_row == req_s[c]) & (in_rows > c), 0.0, first_of)
    leader[...] = first_of
    row_in = lax.rem(column, SLOTS)
    nowhere = -requests * SLOTS
    of_first = jnp.where(row_in < 12, row_in, nowhere)
    of_second = jnp.where(row_in < 8, row_in + 16, jnp.where(row_in < 12, nowhere, row_in))
    target = (by_column + 2) // 2 * PAIR - PAIR + jnp.where(lax.rem(by_column + 2, 2) == 1, of_second, of_first)
    target = jnp.where(by_column < 0, nowhere, target)
    pick_rows = 96

    def fill_pick(b, carry):
        at = pl.multiple_of(b * pick_rows, pick_rows)
        row = iota((pick_rows, flat), 0) + at
        pick[pl.ds(at, pick_rows), :] = jnp.where(row == target, 1.0, 0.0).astype(bf16)
        return carry

    lax.fori_loop(0, owners * PAIR // pick_rows, fill_pick, 0)
    wanted = iota((owners, 6 * spans_here), 0) * 2 + stat_column // (3 * spans_here)
    pick_stat[...] = jnp.where(wanted == by_stat, 1.0, 0.0).astype(bf16)

    key_copy.wait()

    def turn(c, carry):
        key_t[c] = key_v[0, c].T
        return carry

    lax.fori_loop(0, spans_here, turn, 0)
    val_copy.wait()
    wait_for(qrows, owners - 1, recv_sem.at[1])

    head = iota((SLOTS, head_dim), 0)
    lanes = iota((SLOTS, head_dim), 1)
    diagonal = lanes == head
    repeated = lax.rem(lanes, SLOTS) == head

    def query_of(c):
        pair = qrows[pair_s[c]].astype(f32)
        rows_of = [jnp.where(odd_s[c] == 1, pair[16:24], pair[0:8]), pair[8:16]]
        return jnp.concatenate(rows_of, axis=0).astype(bf16)

    def soften(c, raw):
        shown = jnp.where(lanes < lim_s[c], raw * scale, very_low)
        top = jnp.max(shown, axis=1, keepdims=True)
        weights = jnp.exp(shown - top)
        total = jnp.sum(weights, axis=1, keepdims=True)
        top_row = jnp.sum(jnp.where(repeated, top, 0.0), axis=0, keepdims=True)
        total_row = jnp.sum(jnp.where(repeated, total, 0.0), axis=0, keepdims=True)
        return weights.astype(bf16), top_row, total_row

    all_spans = range(spans_here)
    raws = [
        jnp.dot(query_of(c), key_t[c], preferred_element_type=f32)
        for c in all_spans
    ]
    softened = [soften(c, raws[c]) for c in all_spans]
    for c in all_spans:
        values[c] = jnp.dot(softened[c][0], val_v[0, c], preferred_element_type=f32)
    for c in all_spans:
        maxima[c : c + 1, :] = softened[c][1]
        totals[c : c + 1, :] = softened[c][2]
    every = maxima[...]
    request_top = every
    for c in range(spans_here):
        request_top = jnp.maximum(request_top, jnp.where(col_req[...] == req_s[c], every[c : c + 1], very_low))
    factor = jnp.exp(every - request_top)
    factors[...] = factor
    def weigh(c):
        factor = jnp.sum(jnp.where(diagonal, factors[pl.ds(c, 1), :], 0.0), axis=1, keepdims=True)
        result = (values[c] * factor).astype(bf16)

        def store():
            spans[pl.ds(pl.multiple_of(c * SLOTS, SLOTS), SLOTS), :] = result

        return store

    chunks(spans_here, 32, weigh)

    group = lane // SLOTS
    said = jnp.where(lax.rem(group, 2) == 0, request_top * leader[...], factor * totals[...])
    high = said.astype(bf16)
    rest = said - high.astype(f32)
    middle = rest.astype(bf16)
    low = (rest - middle.astype(f32)).astype(bf16)
    thirds = jnp.concatenate([high, middle, low], axis=0).astype(f32)
    first_lanes = jnp.where(group < 2, thirds, 0.0).astype(bf16)
    second_lanes = jnp.where((group == 2) | (group == 3), thirds, 0.0).astype(bf16)
    stats = jnp.dot(
        pick_stat[...], jnp.concatenate([first_lanes, second_lanes], axis=0), preferred_element_type=f32
    )
    stat_out[...] = stats.reshape(owners, 1, head_dim)
    for d in owner_order:
        place, device = owner_at(*d)
        pltpu.make_async_remote_copy(
            src_ref=stat_out.at[place],
            dst_ref=stat_in.at[owner],
            send_sem=send_sem.at[6],
            recv_sem=recv_sem.at[6],
            device_id=device,
            device_id_type=MESH,
        ).start()
    stat_in[owner] = stat_out[owner]

    for dg in far_first(n_grp, 1):
        group_of = lax.rem(g + dg, n_grp)
        at = pl.multiple_of(group_of * n_mem * PAIR, n_mem * PAIR)
        summed = jnp.dot(pick[pl.ds(at, n_mem * PAIR), :], spans[...], preferred_element_type=f32)
        soft_out[pl.ds(group_of * n_mem, n_mem)] = summed.astype(bf16).reshape(n_mem, PAIR, head_dim)
        for d in mem_order if dg == 0 else mem_order + [0]:
            place, device = owner_at(dg, d)
            pltpu.make_async_remote_copy(
                src_ref=soft_out.at[place],
                dst_ref=soft_in.at[owner],
                send_sem=send_sem.at[2],
                recv_sem=recv_sem.at[2],
                device_id=device,
                device_id_type=MESH,
            ).start()
    soft_in[owner] = soft_out[owner]
    wait_for(stat_in, owners - 1, recv_sem.at[6])
    stats = stat_in[...].reshape(owners, head_dim)
    total = pltpu.roll(stats, head_dim - SLOTS, axis=1)
    top = jnp.where(total > 0.0, stats, very_low)
    new_top = new_score[...]
    most = jnp.maximum(jnp.max(top, axis=0, keepdims=True), new_top)
    factor = jnp.exp(top - most)
    new_factor = jnp.exp(new_top - most)
    whole = jnp.sum(factor * total, axis=0, keepdims=True) + new_factor
    blend[...] = factor / whole
    new_share = jnp.sum(jnp.where(pair_diagonal, new_factor / whole, 0.0), axis=1, keepdims=True)

    def spread(b, carry):
        for u in range(16):
            s = b * 16 + u
            share = jnp.sum(jnp.where(pair_diagonal, blend[pl.ds(s, 1), :], 0.0), axis=1, keepdims=True)
            shares[s] = jnp.broadcast_to(share, (PAIR, head_dim))
        return carry

    lax.fori_loop(0, owners // 16, spread, 0)
    wait_for(soft_in, owners - 1, recv_sem.at[2])

    def join(b, carry):
        for u in range(16):
            s = b * 16 + u
            carry = carry + shares[s] * soft_in[s].astype(f32)
        return carry

    att[m] = lax.fori_loop(0, owners // 16, join, new_share * newest[...]).astype(bf16)

    for d in mem_order:
        pltpu.make_async_remote_copy(
            src_ref=att.at[m],
            dst_ref=att.at[m],
            send_sem=send_sem.at[3],
            recv_sem=recv_sem.at[3],
            device_id={"mem": owner_at(0, d)[1]["mem"]},
            device_id_type=MESH,
        ).start()
    out_copy.wait()
    wait_for(att, n_mem - 1, recv_sem.at[3])

    out_cols = wo_v.shape[1] // head_dim
    att_wide[0 : n_mem * PAIR, :] = att[...].astype(f32).reshape(n_mem * PAIR, head_dim)

    def head_rows(h):
        second = h + 16 if h < 8 else h + 4
        return jnp.concatenate([att_wide[pl.ds(row, n_mem, stride=PAIR), :] for row in (h, second)], axis=0)

    left = jnp.concatenate([head_rows(h) for h in range(heads)], axis=1).astype(bf16)
    product = jnp.dot(left, wo_v[...], preferred_element_type=f32)
    for n in range(out_cols):
        for i in range(own_rows):
            piece = product[i * n_mem : (i + 1) * n_mem, n * head_dim : (n + 1) * head_dim]
            wide_rows[pl.ds(i * out_cols + n, n_mem, stride=own_rows * out_cols), :] = piece
    sums[...] = wide_rows[0 : rows * out_cols, :].astype(bf16).reshape(n_tp, out_rows * out_cols, head_dim)

    pl.semaphore_wait(tp_sem.at[1], len(beside))
    for d in tp_order:
        to = lax.rem(t + d, n_tp)
        pltpu.make_async_remote_copy(
            src_ref=sums.at[to],
            dst_ref=sums_in.at[t],
            send_sem=send_sem.at[4],
            recv_sem=recv_sem.at[4],
            device_id={"tp": to},
            device_id_type=MESH,
        ).start()
    sums_in[t] = sums[t]
    wait_for(sums_in, n_tp - 1, recv_sem.at[4])
    total = sums_in[0].astype(f32)
    for i in range(1, n_tp):
        total = total + sums_in[i].astype(f32)
    done[t] = total.astype(bf16)
    for d in tp_order:
        pltpu.make_async_remote_copy(
            src_ref=done.at[t],
            dst_ref=done.at[t],
            send_sem=send_sem.at[5],
            recv_sem=recv_sem.at[5],
            device_id={"tp": lax.rem(t + d, n_tp)},
            device_id_type=MESH,
        ).start()
    wait_for(done, n_tp - 1, recv_sem.at[5])
    wide_rows[0 : rows * out_cols, :] = done[...].astype(f32).reshape(rows * out_cols, head_dim)
    for n in range(out_cols):
        out[:, n * head_dim : (n + 1) * head_dim] = wide_rows[pl.ds(n, rows, stride=out_cols), :].astype(bf16)

    wait_for(part, (n_mem - 1) * tile, send_sem.at[0])
    wait_for(qrows, owners - 1, send_sem.at[1])
    wait_for(soft_out, owners - 1, send_sem.at[2])
    wait_for(stat_out, owners - 1, send_sem.at[6])
    wait_for(att, n_mem - 1, send_sem.at[3])
    wait_for(sums, n_tp - 1, send_sem.at[4])
    wait_for(done, n_tp - 1, send_sem.at[5])


def per_device(n_grp, n_tp, n_mem, *args):
    tokens, norm_gain, w_query, w_keyval, w_out, key_cache, value_cache, req_len, span_request, _, _ = args
    rows, width = tokens.shape
    q_cols = w_query.shape[1]
    head_dim = key_cache.shape[3]
    spans_here = span_request.shape[0]
    requests = req_len.shape[0]
    owners = n_grp * n_mem
    own_rows = rows // n_mem
    tile = own_rows * SLOTS
    out_width = w_out.shape[1]
    slab = rows // n_tp * out_width // head_dim
    scratch = [
        pltpu.VMEM(tokens.shape, bf16),
        pltpu.VMEM(norm_gain.shape, f32),
        pltpu.VMEM(w_query.shape, bf16),
        pltpu.VMEM(w_keyval.shape, bf16),
        pltpu.VMEM(w_out.shape, bf16),
        pltpu.VMEM(key_cache.shape, bf16),
        pltpu.VMEM(value_cache.shape, bf16),
        pltpu.SMEM((requests,), jnp.int32),
        pltpu.SMEM((spans_here,), jnp.int32),
        pltpu.SMEM((spans_here,), jnp.int32),
        pltpu.SMEM((spans_here,), jnp.int32),
        pltpu.SMEM((spans_here,), jnp.int32),
        pltpu.SMEM((spans_here,), jnp.int32),
        pltpu.VMEM((rows * SLOTS + SLOTS, head_dim), f32),
        pltpu.VMEM((n_mem, tile, head_dim), f32),
        pltpu.VMEM((2, tile, head_dim), f32),
        pltpu.VMEM((owners * PAIR, spans_here * SLOTS), bf16),
        pltpu.VMEM((owners, 6 * spans_here), bf16),
        pltpu.VMEM((spans_here, head_dim), jnp.int32),
        pltpu.VMEM((spans_here, head_dim), f32),
        pltpu.VMEM((owners, PAIR, head_dim), bf16),
        pltpu.VMEM((spans_here, head_dim, key_cache.shape[2]), bf16),
        pltpu.VMEM((PAIR, head_dim), f32),
        pltpu.VMEM((1, head_dim), f32),
        pltpu.VMEM((spans_here, SLOTS, head_dim), f32),
        pltpu.VMEM((spans_here, head_dim), f32),
        pltpu.VMEM((spans_here, head_dim), f32),
        pltpu.VMEM((spans_here, head_dim), f32),
        pltpu.VMEM((spans_here * SLOTS, head_dim), bf16),
        pltpu.VMEM((owners, PAIR, head_dim), bf16),
        pltpu.VMEM((owners, PAIR, head_dim), bf16),
        pltpu.VMEM((owners, 1, head_dim), f32),
        pltpu.VMEM((owners, 1, head_dim), f32),
        pltpu.VMEM((owners, head_dim), f32),
        pltpu.VMEM((owners, PAIR, head_dim), f32),
        pltpu.VMEM((n_mem, PAIR, head_dim), bf16),
        pltpu.VMEM((n_mem * PAIR + PAIR, head_dim), f32),
        pltpu.VMEM((n_tp * slab + slab, head_dim), f32),
        pltpu.VMEM((n_tp, slab, head_dim), bf16),
        pltpu.VMEM((n_tp, slab, head_dim), bf16),
        pltpu.VMEM((n_tp, slab, head_dim), bf16),
        pltpu.SemaphoreType.DMA((16,)),
        pltpu.SemaphoreType.DMA((7,)),
        pltpu.SemaphoreType.DMA((7,)),
        pltpu.SemaphoreType.REGULAR((2,)),
    ]
    return pl.pallas_call(
        functools.partial(kernel, n_grp, n_tp, n_mem),
        out_shape=pltpu.VMEM((rows, out_width), bf16),
        in_specs=[pl.BlockSpec(memory_space=HBM)] * len(args),
        out_specs=pl.BlockSpec(memory_space=pltpu.VMEM),
        scratch_shapes=scratch,
        compiler_params=pltpu.CompilerParams(
            collective_id=0, has_side_effects=True, vmem_limit_bytes=48 * 1024 * 1024
        ),
        cost_estimate=pl.CostEstimate(flops=200_000_000, bytes_accessed=12_600_000, transcendentals=100_000),
    )(*[pltpu.with_memory_space_constraint(a, HBM) for a in args])


def solution(mesh):
    placed = (
        P("grp", "mem"),
        P("mem"),
        P("mem", "tp"),
        P(None, "mem", "tp"),
        P("tp", "mem"),
        P("tp", ("grp", "mem"), None, None),
        P("tp", ("grp", "mem"), None, None),
        P(),
        P(("grp", "mem")),
        P(("grp", "mem")),
        P(),
    )
    body = functools.partial(per_device, mesh.shape["grp"], mesh.shape["tp"], mesh.shape["mem"])
    return jax.shard_map(body, mesh=mesh, in_specs=placed, out_specs=P("grp", "mem"), check_vma=False)
```

```python
import functools

import jax
import jax.numpy as jnp
from jax import lax
from jax.experimental import pallas as pl
from jax.experimental.pallas import tpu as pltpu
from jax.sharding import PartitionSpec as P

MESH = pl.DeviceIdType.MESH
HBM = pltpu.MemorySpace.HBM
D = 12288
epsilon = 1e-05
rope_base = 1000000.0
very_low = -1e30
SLOTS = 16
PAIR = 24
f32 = jnp.float32
bf16 = jnp.bfloat16


def chunks(count, width, body):
    def step(b, carry):
        stores = [body(b * width + u) for u in range(width)]
        for store in stores:
            store()
        return carry

    lax.fori_loop(0, count // width, step, 0)


def hops(d, size):
    return min(d, size - d)


def far_first(size, each):
    chips = sorted(range(size), key=lambda d: -hops(d, size))
    return [d * each + c for d in chips for c in range(each)]


def iota(shape, dim):
    return lax.broadcasted_iota(jnp.int32, shape, dim)


def kernel(
    n_grp, n_tp, n_mem,
    tokens, gain, w_query, w_keyval, w_out, key_cache, value_cache, req_len, span_request, span_first, new_slot,
    out,
    tok_v, gain_v, wq_v, wkv_v, wo_v, key_v, val_v, len_s, req_s, first_s, lim_s, pair_s, odd_s,
    part, part_in, table, pick, pick_stat, same, leader, qrows, key_t, newest, new_score, values, maxima, totals, factors, spans,
    soft_out, soft_in, stat_out, stat_in, blend, shares, att, att_wide, wide_rows, sums, sums_in, done, local_sem, send_sem, recv_sem, tp_sem,
):
    g, t, m = lax.axis_index("grp"), lax.axis_index("tp"), lax.axis_index("mem")
    owners = n_grp * n_mem
    owner = g * n_mem + m
    rows, width = tok_v.shape
    requests = len_s.shape[0]
    own_rows = rows // n_mem
    out_rows = rows // n_tp
    spans_here = req_s.shape[0]
    q_cols = wq_v.shape[1]
    head_dim = key_v.shape[3]
    heads = q_cols // head_dim
    tile = own_rows * SLOTS
    k_chunks = 6
    k_step = width // k_chunks

    small = [
        pltpu.make_async_copy(req_len, len_s, local_sem.at[0]),
        pltpu.make_async_copy(span_request, req_s, local_sem.at[1]),
        pltpu.make_async_copy(span_first, first_s, local_sem.at[2]),
    ]
    tok_copy = pltpu.make_async_copy(tokens, tok_v, local_sem.at[4])
    gain_copy = pltpu.make_async_copy(gain, gain_v, local_sem.at[5])
    wkv_copy = pltpu.make_async_copy(w_keyval, wkv_v, local_sem.at[6])
    key_copy = pltpu.make_async_copy(key_cache, key_v, local_sem.at[7])
    val_copy = pltpu.make_async_copy(value_cache, val_v, local_sem.at[8])
    out_copy = pltpu.make_async_copy(w_out, wo_v, local_sem.at[9])
    wq_copies = [
        pltpu.make_async_copy(
            w_query.at[pl.ds(c * k_step, k_step), :], wq_v.at[pl.ds(c * k_step, k_step), :], local_sem.at[10 + c]
        )
        for c in range(k_chunks)
    ]
    barrier = pltpu.get_barrier_semaphore()

    def owner_at(dg, dm):
        to_g = lax.rem(g + dg, n_grp)
        to_m = lax.rem(m // 2 + dm // 2, n_mem // 2) * 2 + lax.rem(m + dm, 2)
        return to_g * n_mem + to_m, {"grp": to_g, "mem": to_m}

    mem_order = [d for d in far_first(n_mem // 2, 2) if d]
    grp_order = [d for d in far_first(n_grp, 1) if d]
    tp_order = [d for d in far_first(n_tp, 1) if d]
    beside = (1, n_tp - 1)
    for d in mem_order:
        pl.semaphore_signal(barrier, inc=1, device_id=owner_at(0, d)[1], device_id_type=MESH)
    for d in grp_order:
        pl.semaphore_signal(barrier, inc=1, device_id=owner_at(d, 0)[1], device_id_type=MESH)

    def tell_tp(semaphore, distances):
        for d in distances:
            pl.semaphore_signal(semaphore, inc=1, device_id={"tp": lax.rem(t + d, n_tp)}, device_id_type=MESH)

    tell_tp(barrier, beside)
    owner_order = sorted(
        [(dg, dm) for dg in range(n_grp) for dm in range(n_mem) if dg or dm],
        key=lambda d: -hops(d[0], n_grp) - hops(d[1] // 2, n_mem // 2),
    )

    tok_copy.start()
    gain_copy.start()
    for copy in [wkv_copy] + wq_copies + small:
        copy.start()

    tok_copy.wait()
    gain_copy.wait()
    wide = tok_v[...].astype(f32)
    square = jnp.sum(wide * wide, axis=1, keepdims=True)
    scaled = (wide * gain_v[...].reshape(1, width)).astype(bf16)
    wkv_copy.wait()
    new_part = [jnp.dot(scaled, wkv_v[i], preferred_element_type=f32) for i in range(2)]
    projected = jnp.zeros((rows, q_cols), f32)
    for c in range(k_chunks):
        wq_copies[c].wait()
        projected += jnp.dot(
            scaled[:, c * k_step : (c + 1) * k_step],
            wq_v[c * k_step : (c + 1) * k_step, :],
            preferred_element_type=f32,
        )
    for copy in (key_copy, val_copy, out_copy):
        copy.start()
    pieces = [projected[:, h * head_dim : (h + 1) * head_dim] for h in range(heads)] + new_part
    pieces += [jnp.broadcast_to(square, (rows, head_dim))]
    pieces += [jnp.zeros((rows, head_dim), f32)] * (SLOTS - len(pieces))
    for h, piece in enumerate(pieces):
        part[pl.ds(h, rows, stride=SLOTS), :] = piece

    pl.semaphore_wait(barrier, len(mem_order) + len(grp_order) + len(beside))
    tell_tp(tp_sem.at[0], beside)

    for d in mem_order:
        to = owner_at(0, d)[1]["mem"]
        pltpu.make_async_remote_copy(
            src_ref=part.at[pl.ds(pl.multiple_of(to * tile, tile), tile), :],
            dst_ref=part_in.at[m],
            send_sem=send_sem.at[0],
            recv_sem=recv_sem.at[0],
            device_id={"mem": to},
            device_id_type=MESH,
        ).start()
    part_in[m] = part[pl.ds(pl.multiple_of(m * tile, tile), tile), :]

    for copy in small:
        copy.wait()
    lane = iota((1, head_dim), 1)
    own_len = [len_s[g * rows + m * own_rows + i] for i in range(own_rows)]
    position = jnp.where(iota((tile, 1), 0) < SLOTS, own_len[0], own_len[1]).astype(f32)
    half = head_dim // 2
    power = (lax.rem(lane, half).astype(f32) * 2.0) / head_dim
    frequency = jnp.exp(power * -jnp.log(jnp.full((1, head_dim), rope_base, f32)))
    angles = position * frequency
    slot_row = lax.rem(iota((tile, head_dim), 0), SLOTS)
    turned = slot_row < heads + 1
    cosine = jnp.where(turned, jnp.cos(angles), 1.0)
    sine = jnp.where(turned, jnp.sin(angles), 0.0)
    table[0] = cosine
    table[1] = jnp.where(lane < half, -sine, sine)


    def wait_for(buffer, amount, kind):
        ref = buffer.at[pl.ds(0, amount)]
        pltpu.make_async_copy(ref, ref, kind).wait()

    wait_for(part_in, n_mem - 1, recv_sem.at[0])
    total = part_in[0]
    for i in range(1, n_mem):
        total = total + part_in[i]
    normed = []
    for i in range(own_rows):
        block = total[i * SLOTS : (i + 1) * SLOTS]
        root_mean = jnp.sqrt(block[heads + 2 : heads + 3] / D + epsilon)
        normed.append(block / root_mean)
    normed = jnp.concatenate(normed, axis=0)
    finished = normed * table[0] + pltpu.roll(normed, half, axis=1) * table[1]

    def in_pair(block):
        sub_row = iota((8, head_dim), 0)
        middle = jnp.where(sub_row < 4, block[8:16], pltpu.roll(block[24:32], 4, axis=0))
        return jnp.concatenate([block[0:8], middle, block[16:24]], axis=0)

    qrows[owner] = in_pair(finished).astype(bf16)

    for d in owner_order:
        pltpu.make_async_remote_copy(
            src_ref=qrows.at[owner],
            dst_ref=qrows.at[owner],
            send_sem=send_sem.at[1],
            recv_sem=recv_sem.at[1],
            device_id=owner_at(*d)[1],
            device_id_type=MESH,
        ).start()
    pl.semaphore_wait(tp_sem.at[0], len(beside))
    tell_tp(tp_sem.at[1], (2, n_tp - 2))
    scale = head_dim**-0.5
    rounded = finished.astype(bf16).astype(f32)
    pair_row = iota((PAIR, head_dim), 0)
    pair_lane = iota((PAIR, head_dim), 1)
    of_first = pair_row < 12
    pair_diagonal = pair_lane == jnp.where(of_first, pair_row, jnp.where(pair_row < 16, pair_row + 32, pair_row + 16))
    new_key = jnp.where(of_first, rounded[heads : heads + 1], rounded[SLOTS + heads : SLOTS + heads + 1])
    newest[...] = jnp.where(of_first, rounded[heads + 1 : heads + 2], rounded[SLOTS + heads + 1 : SLOTS + heads + 2])
    fresh = jnp.sum(in_pair(rounded) * new_key, axis=1, keepdims=True) * scale
    new_score[...] = jnp.sum(jnp.where(pair_diagonal, fresh, 0.0), axis=0, keepdims=True)
    def span_scalars(c, carry):
        r = jnp.maximum(req_s[c], 0)
        lim_s[c] = jnp.where(req_s[c] >= 0, len_s[r] - first_s[c], 0)
        pair_s[c] = r // 2
        odd_s[c] = lax.rem(r, 2)
        return carry

    lax.fori_loop(0, spans_here, span_scalars, 0)

    flat = spans_here * SLOTS
    column = iota((1, flat), 1)
    in_rows = iota((spans_here, head_dim), 0)
    by_column = jnp.zeros((1, flat), jnp.int32)
    by_row = jnp.zeros((spans_here, head_dim), jnp.int32)
    stat_column = iota((1, 6 * spans_here), 1)
    by_stat = jnp.zeros((1, 6 * spans_here), jnp.int32)
    for c in range(spans_here):
        by_column = jnp.where(column // SLOTS == c, req_s[c], by_column)
        by_row = jnp.where(in_rows == c, req_s[c], by_row)
        by_stat = jnp.where(lax.rem(stat_column, spans_here) == c, req_s[c], by_stat)
    first_of = jnp.ones((spans_here, head_dim), f32)
    for c in range(spans_here):
        first_of = jnp.where((by_row == req_s[c]) & (in_rows > c), 0.0, first_of)
    leader[...] = first_of
    for c in range(spans_here):
        same[c] = jnp.where(by_row == req_s[c], 0.0, very_low * 1e5)
    row_in = lax.rem(column, SLOTS)
    nowhere = -requests * SLOTS
    of_first = jnp.where(row_in < 12, row_in, nowhere)
    of_second = jnp.where(row_in < 8, row_in + 16, jnp.where(row_in < 12, nowhere, row_in))
    target = (by_column + 2) // 2 * PAIR - PAIR + jnp.where(lax.rem(by_column + 2, 2) == 1, of_second, of_first)
    target = jnp.where(by_column < 0, nowhere, target)
    pick_rows = 96

    def fill_pick(b, carry):
        at = pl.multiple_of(b * pick_rows, pick_rows)
        row = iota((pick_rows, flat), 0) + at
        pick[pl.ds(at, pick_rows), :] = jnp.where(row == target, 1.0, 0.0).astype(bf16)
        return carry

    lax.fori_loop(0, owners * PAIR // pick_rows, fill_pick, 0)
    wanted = iota((owners, 6 * spans_here), 0) * 2 + stat_column // (3 * spans_here)
    pick_stat[...] = jnp.where(wanted == by_stat, 1.0, 0.0).astype(bf16)

    key_copy.wait()

    def turn(c, carry):
        key_t[c] = key_v[0, c].T
        return carry

    lax.fori_loop(0, spans_here, turn, 0)
    val_copy.wait()
    wait_for(qrows, owners - 1, recv_sem.at[1])

    head = iota((SLOTS, head_dim), 0)
    lanes = iota((SLOTS, head_dim), 1)
    diagonal = lanes == head
    repeated = lax.rem(lanes, SLOTS) == head

    def query_of(c):
        pair = qrows[pair_s[c]].astype(f32)
        rows_of = [jnp.where(odd_s[c] == 1, pair[16:24], pair[0:8]), pair[8:16]]
        return jnp.concatenate(rows_of, axis=0).astype(bf16)

    def soften(c, raw):
        shown = jnp.where(lanes < lim_s[c], raw * scale, very_low)
        top = jnp.max(shown, axis=1, keepdims=True)
        weights = jnp.exp(shown - top)
        total = jnp.sum(weights, axis=1, keepdims=True)
        top_row = jnp.sum(jnp.where(repeated, top, 0.0), axis=0, keepdims=True)
        total_row = jnp.sum(jnp.where(repeated, total, 0.0), axis=0, keepdims=True)
        return weights.astype(bf16), top_row, total_row

    all_spans = range(spans_here)
    raws = [
        jnp.dot(query_of(c), key_t[c], preferred_element_type=f32)
        for c in all_spans
    ]
    softened = [soften(c, raws[c]) for c in all_spans]
    for c in all_spans:
        values[c] = jnp.dot(softened[c][0], val_v[0, c], preferred_element_type=f32)
    for c in all_spans:
        maxima[c : c + 1, :] = softened[c][1]
        totals[c : c + 1, :] = softened[c][2]
    every = maxima[...]
    request_top = every
    for c in range(spans_here):
        request_top = jnp.maximum(request_top, every[c : c + 1] + same[c])
    factor = jnp.exp(every - request_top)
    factors[...] = factor
    def weigh(c):
        factor = jnp.sum(jnp.where(diagonal, factors[pl.ds(c, 1), :], 0.0), axis=1, keepdims=True)
        result = (values[c] * factor).astype(bf16)

        def store():
            spans[pl.ds(pl.multiple_of(c * SLOTS, SLOTS), SLOTS), :] = result

        return store

    chunks(spans_here, 32, weigh)

    group = lane // SLOTS
    said = jnp.where(lax.rem(group, 2) == 0, request_top * leader[...], factor * totals[...])
    high = said.astype(bf16)
    rest = said - high.astype(f32)
    middle = rest.astype(bf16)
    low = (rest - middle.astype(f32)).astype(bf16)
    thirds = jnp.concatenate([high, middle, low], axis=0).astype(f32)
    first_lanes = jnp.where(group < 2, thirds, 0.0).astype(bf16)
    second_lanes = jnp.where((group == 2) | (group == 3), thirds, 0.0).astype(bf16)
    stats = jnp.dot(
        pick_stat[...], jnp.concatenate([first_lanes, second_lanes], axis=0), preferred_element_type=f32
    )
    stat_out[...] = stats.reshape(owners, 1, head_dim)
    for d in owner_order:
        place, device = owner_at(*d)
        pltpu.make_async_remote_copy(
            src_ref=stat_out.at[place],
            dst_ref=stat_in.at[owner],
            send_sem=send_sem.at[6],
            recv_sem=recv_sem.at[6],
            device_id=device,
            device_id_type=MESH,
        ).start()
    stat_in[owner] = stat_out[owner]

    for dg in far_first(n_grp, 1):
        group_of = lax.rem(g + dg, n_grp)
        at = pl.multiple_of(group_of * n_mem * PAIR, n_mem * PAIR)
        summed = jnp.dot(pick[pl.ds(at, n_mem * PAIR), :], spans[...], preferred_element_type=f32)
        soft_out[pl.ds(group_of * n_mem, n_mem)] = summed.astype(bf16).reshape(n_mem, PAIR, head_dim)
        for d in mem_order if dg == 0 else mem_order + [0]:
            place, device = owner_at(dg, d)
            pltpu.make_async_remote_copy(
                src_ref=soft_out.at[place],
                dst_ref=soft_in.at[owner],
                send_sem=send_sem.at[2],
                recv_sem=recv_sem.at[2],
                device_id=device,
                device_id_type=MESH,
            ).start()
    soft_in[owner] = soft_out[owner]
    wait_for(stat_in, owners - 1, recv_sem.at[6])
    stats = stat_in[...].reshape(owners, head_dim)
    total = pltpu.roll(stats, head_dim - SLOTS, axis=1)
    top = jnp.where(total > 0.0, stats, very_low)
    new_top = new_score[...]
    most = jnp.maximum(jnp.max(top, axis=0, keepdims=True), new_top)
    factor = jnp.exp(top - most)
    new_factor = jnp.exp(new_top - most)
    whole = jnp.sum(factor * total, axis=0, keepdims=True) + new_factor
    blend[...] = factor / whole
    new_share = jnp.sum(jnp.where(pair_diagonal, new_factor / whole, 0.0), axis=1, keepdims=True)

    def spread(b, carry):
        for u in range(16):
            s = b * 16 + u
            share = jnp.sum(jnp.where(pair_diagonal, blend[pl.ds(s, 1), :], 0.0), axis=1, keepdims=True)
            shares[s] = jnp.broadcast_to(share, (PAIR, head_dim))
        return carry

    lax.fori_loop(0, owners // 16, spread, 0)
    wait_for(soft_in, owners - 1, recv_sem.at[2])

    def join(b, carry):
        for u in range(16):
            s = b * 16 + u
            carry = carry + shares[s] * soft_in[s].astype(f32)
        return carry

    att[m] = lax.fori_loop(0, owners // 16, join, new_share * newest[...]).astype(bf16)

    for d in mem_order:
        pltpu.make_async_remote_copy(
            src_ref=att.at[m],
            dst_ref=att.at[m],
            send_sem=send_sem.at[3],
            recv_sem=recv_sem.at[3],
            device_id={"mem": owner_at(0, d)[1]["mem"]},
            device_id_type=MESH,
        ).start()
    out_copy.wait()
    wait_for(att, n_mem - 1, recv_sem.at[3])

    out_cols = wo_v.shape[1] // head_dim
    att_wide[0 : n_mem * PAIR, :] = att[...].astype(f32).reshape(n_mem * PAIR, head_dim)

    def head_rows(h):
        second = h + 16 if h < 8 else h + 4
        return jnp.concatenate([att_wide[pl.ds(row, n_mem, stride=PAIR), :] for row in (h, second)], axis=0)

    left = jnp.concatenate([head_rows(h) for h in range(heads)], axis=1).astype(bf16)
    product = jnp.dot(left, wo_v[...], preferred_element_type=f32)
    for n in range(out_cols):
        for i in range(own_rows):
            piece = product[i * n_mem : (i + 1) * n_mem, n * head_dim : (n + 1) * head_dim]
            wide_rows[pl.ds(i * out_cols + n, n_mem, stride=own_rows * out_cols), :] = piece
    sums[...] = wide_rows[0 : rows * out_cols, :].astype(bf16).reshape(n_tp, out_rows * out_cols, head_dim)

    pl.semaphore_wait(tp_sem.at[1], len(beside))
    for d in tp_order:
        to = lax.rem(t + d, n_tp)
        pltpu.make_async_remote_copy(
            src_ref=sums.at[to],
            dst_ref=sums_in.at[t],
            send_sem=send_sem.at[4],
            recv_sem=recv_sem.at[4],
            device_id={"tp": to},
            device_id_type=MESH,
        ).start()
    sums_in[t] = sums[t]
    wait_for(sums_in, n_tp - 1, recv_sem.at[4])
    total = sums_in[0].astype(f32)
    for i in range(1, n_tp):
        total = total + sums_in[i].astype(f32)
    done[t] = total.astype(bf16)
    for d in tp_order:
        pltpu.make_async_remote_copy(
            src_ref=done.at[t],
            dst_ref=done.at[t],
            send_sem=send_sem.at[5],
            recv_sem=recv_sem.at[5],
            device_id={"tp": lax.rem(t + d, n_tp)},
            device_id_type=MESH,
        ).start()
    wait_for(done, n_tp - 1, recv_sem.at[5])
    wide_rows[0 : rows * out_cols, :] = done[...].astype(f32).reshape(rows * out_cols, head_dim)
    for n in range(out_cols):
        out[:, n * head_dim : (n + 1) * head_dim] = wide_rows[pl.ds(n, rows, stride=out_cols), :].astype(bf16)

    wait_for(part, (n_mem - 1) * tile, send_sem.at[0])
    wait_for(qrows, owners - 1, send_sem.at[1])
    wait_for(soft_out, owners - 1, send_sem.at[2])
    wait_for(stat_out, owners - 1, send_sem.at[6])
    wait_for(att, n_mem - 1, send_sem.at[3])
    wait_for(sums, n_tp - 1, send_sem.at[4])
    wait_for(done, n_tp - 1, send_sem.at[5])


def per_device(n_grp, n_tp, n_mem, *args):
    tokens, norm_gain, w_query, w_keyval, w_out, key_cache, value_cache, req_len, span_request, _, _ = args
    rows, width = tokens.shape
    q_cols = w_query.shape[1]
    head_dim = key_cache.shape[3]
    spans_here = span_request.shape[0]
    requests = req_len.shape[0]
    owners = n_grp * n_mem
    own_rows = rows // n_mem
    tile = own_rows * SLOTS
    out_width = w_out.shape[1]
    slab = rows // n_tp * out_width // head_dim
    scratch = [
        pltpu.VMEM(tokens.shape, bf16),
        pltpu.VMEM(norm_gain.shape, f32),
        pltpu.VMEM(w_query.shape, bf16),
        pltpu.VMEM(w_keyval.shape, bf16),
        pltpu.VMEM(w_out.shape, bf16),
        pltpu.VMEM(key_cache.shape, bf16),
        pltpu.VMEM(value_cache.shape, bf16),
        pltpu.SMEM((requests,), jnp.int32),
        pltpu.SMEM((spans_here,), jnp.int32),
        pltpu.SMEM((spans_here,), jnp.int32),
        pltpu.SMEM((spans_here,), jnp.int32),
        pltpu.SMEM((spans_here,), jnp.int32),
        pltpu.SMEM((spans_here,), jnp.int32),
        pltpu.VMEM((rows * SLOTS + SLOTS, head_dim), f32),
        pltpu.VMEM((n_mem, tile, head_dim), f32),
        pltpu.VMEM((2, tile, head_dim), f32),
        pltpu.VMEM((owners * PAIR, spans_here * SLOTS), bf16),
        pltpu.VMEM((owners, 6 * spans_here), bf16),
        pltpu.VMEM((spans_here, spans_here, head_dim), f32),
        pltpu.VMEM((spans_here, head_dim), f32),
        pltpu.VMEM((owners, PAIR, head_dim), bf16),
        pltpu.VMEM((spans_here, head_dim, key_cache.shape[2]), bf16),
        pltpu.VMEM((PAIR, head_dim), f32),
        pltpu.VMEM((1, head_dim), f32),
        pltpu.VMEM((spans_here, SLOTS, head_dim), f32),
        pltpu.VMEM((spans_here, head_dim), f32),
        pltpu.VMEM((spans_here, head_dim), f32),
        pltpu.VMEM((spans_here, head_dim), f32),
        pltpu.VMEM((spans_here * SLOTS, head_dim), bf16),
        pltpu.VMEM((owners, PAIR, head_dim), bf16),
        pltpu.VMEM((owners, PAIR, head_dim), bf16),
        pltpu.VMEM((owners, 1, head_dim), f32),
        pltpu.VMEM((owners, 1, head_dim), f32),
        pltpu.VMEM((owners, head_dim), f32),
        pltpu.VMEM((owners, PAIR, head_dim), f32),
        pltpu.VMEM((n_mem, PAIR, head_dim), bf16),
        pltpu.VMEM((n_mem * PAIR + PAIR, head_dim), f32),
        pltpu.VMEM((n_tp * slab + slab, head_dim), f32),
        pltpu.VMEM((n_tp, slab, head_dim), bf16),
        pltpu.VMEM((n_tp, slab, head_dim), bf16),
        pltpu.VMEM((n_tp, slab, head_dim), bf16),
        pltpu.SemaphoreType.DMA((16,)),
        pltpu.SemaphoreType.DMA((7,)),
        pltpu.SemaphoreType.DMA((7,)),
        pltpu.SemaphoreType.REGULAR((2,)),
    ]
    return pl.pallas_call(
        functools.partial(kernel, n_grp, n_tp, n_mem),
        out_shape=pltpu.VMEM((rows, out_width), bf16),
        in_specs=[pl.BlockSpec(memory_space=HBM)] * len(args),
        out_specs=pl.BlockSpec(memory_space=pltpu.VMEM),
        scratch_shapes=scratch,
        compiler_params=pltpu.CompilerParams(
            collective_id=0, has_side_effects=True, vmem_limit_bytes=48 * 1024 * 1024
        ),
        cost_estimate=pl.CostEstimate(flops=200_000_000, bytes_accessed=12_600_000, transcendentals=100_000),
    )(*[pltpu.with_memory_space_constraint(a, HBM) for a in args])


def solution(mesh):
    placed = (
        P("grp", "mem"),
        P("mem"),
        P("mem", "tp"),
        P(None, "mem", "tp"),
        P("tp", "mem"),
        P("tp", ("grp", "mem"), None, None),
        P("tp", ("grp", "mem"), None, None),
        P(),
        P(("grp", "mem")),
        P(("grp", "mem")),
        P(),
    )
    body = functools.partial(per_device, mesh.shape["grp"], mesh.shape["tp"], mesh.shape["mem"])
    return jax.shard_map(body, mesh=mesh, in_specs=placed, out_specs=P("grp", "mem"), check_vma=False)
```
